32 devices in a mesh: frame: 16 (over z, y, core), space: 2 (over x).
Axes of the slice: x: 2, y: 2, z: 4, core: 2. Of those that a mesh axis runs over, the one named last changes fastest.
Arguments:
- video_in: bfloat16 [2, 16, 24, 48, 320], P(None, 'frame', 'space')
- time_embed: bfloat16 [2, 16, 1280], P(None, 'frame'), may hold values from -6 to 6
- text_embed: bfloat16 [2, 16, 128, 1024], P(None, 'frame', 'space'), may hold values from -6 to 6
- text_mask: int32 [2, 16, 128], P(None, 'frame'), may hold values from 0 to 1, as said below
- video_mask: int32 [2, 16], replicated, may hold values from 0 to 1, as said below
- video_number: int32 [2, 16], replicated, may hold values from 0 to 1, as said below
- bucket_index: int32 [16, 16], replicated, may hold values from 0 to 31
- norm_gains: float32 [320, 6], replicated, may hold values from 0.5 to 1.5
- bias_table: float32 [32, 5], replicated, may hold values from -4 to 4
- conv_first: bfloat16 [2880, 320], P('frame', 'space'), may hold values from -0.109375 to 0.109375
- conv_second: bfloat16 [2880, 320], P('frame', 'space'), may hold values from -0.109375 to 0.109375
- film_weight: bfloat16 [1280, 640], P('frame', 'space'), may hold values from -0.15625 to 0.15625
- self_project: bfloat16 [320, 960], P('frame', 'space'), may hold values from -0.3125 to 0.3125
- self_output: bfloat16 [320, 320], P('frame', 'space'), may hold values from -1 to 1
- cross_query: bfloat16 [320, 320], P('frame', 'space'), may hold values from -0.3125 to 0.3125
- cross_keyval: bfloat16 [1024, 640], P('frame', 'space'), may hold values from -0.1875 to 0.1875
- cross_output: bfloat16 [320, 320], P('frame', 'space'), may hold values from -0.625 to 0.625
- time_project: bfloat16 [320, 960], P('frame', 'space'), may hold values from -0.3125 to 0.3125
- time_output: bfloat16 [320, 320], P('frame', 'space'), may hold values from -0.5 to 0.5
- feed_up: bfloat16 [320, 1280], P('frame', 'space'), may hold values from -0.3125 to 0.3125
- feed_down: bfloat16 [1280, 320], P('frame', 'space'), may hold values from -0.15625 to 0.15625
- cotangent: bfloat16 [2, 16, 24, 48, 320], P(None, 'frame', 'space'), may hold values from -6 to 6
Outputs:
- block_out: bfloat16 [2, 16, 24, 48, 320], P(None, 'frame', 'space')
- input_grad: bfloat16 [2, 16, 24, 48, 320], P(None, 'frame', 'space')
- gains_grad: float32 [320, 6], replicated
- table_grad: float32 [32, 5], replicated
- conv_first_grad: float32 [2880, 320], P('frame', 'space')
- conv_second_grad: float32 [2880, 320], P('frame', 'space')
- film_grad: float32 [1280, 640], P('frame', 'space')
- self_project_grad: float32 [320, 960], P('frame', 'space')
- self_output_grad: float32 [320, 320], P('frame', 'space')
- cross_query_grad: float32 [320, 320], P('frame', 'space')
- cross_keyval_grad: float32 [1024, 640], P('frame', 'space')
- cross_output_grad: float32 [320, 320], P('frame', 'space')
- time_project_grad: float32 [320, 960], P('frame', 'space')
- time_output_grad: float32 [320, 320], P('frame', 'space')
- feed_up_grad: float32 [320, 1280], P('frame', 'space')
- feed_down_grad: float32 [1280, 320], P('frame', 'space')
The draws below stay inside these ranges and needn't reach their ends.
Inputs may be any that keep to these rules, and one draw needn't show every extreme that they name: `text_mask`: token 0 of every frame's text is real. `video_mask`: the first and the last frame of every aligned group of 16 frames are video frames. `video_number`: the first and the last frame of every aligned group of 16 frames have number 0.
All inputs are finite; a program needn't handle non-finite values.
Results may differ from the reference program's by a relative error of at most 0.025.
Values may be sent and summed in bfloat16 or wider, within the bound.
No kernel may reach another device: no remote copies, remote signals or barrier semaphores. Data moves between devices by JAX's collectives and lax.ppermute only.
A program may use at most 256 MiB of HBM per device.

```python
import jax
import jax.numpy as jnp
from jax import lax

C = 320
HEADS = 5
HEAD = 64
GROUPS = 32
CTX = 1024
TEMB = 1280
FF = 1280
TEXT = 128
IMG_H = 24
IMG_W = 48
FR_DEV = 2
GROUP_LEN = 16
NB = 32
NORMS = 6
N_FRAME = 16


def draw_video_in(key, part):
    key = jax.random.fold_in(key, 11)
    growth = jnp.exp(jnp.linspace(0.0, jnp.log(3.0), IMG_H)).reshape(1, 1, IMG_H, 1, 1)
    extent = (FR_DEV, N_FRAME, IMG_H, IMG_W, C)
    values = jax.random.normal(key, extent, jnp.float32)
    return (values * growth).astype(jnp.bfloat16)


def draw_video_mask(key, part):
    key = jax.random.fold_in(key, 12)
    drawn = jax.random.randint(key, (FR_DEV, N_FRAME), 0, 4)
    position = jnp.arange(N_FRAME) % GROUP_LEN
    border = (position == 0) | (position == GROUP_LEN - 1)
    return jnp.where(border[None, :] | (drawn < 3), 1, 0).astype(jnp.int32)


def draw_video_number(key, part):
    key = jax.random.fold_in(key, 13)
    drawn = jax.random.randint(key, (FR_DEV, N_FRAME), 0, 2)
    position = jnp.arange(N_FRAME) % GROUP_LEN
    border = (position == 0) | (position == GROUP_LEN - 1)
    return jnp.where(border[None, :], 0, drawn).astype(jnp.int32)


def draw_text_mask(key, part):
    key = jax.random.fold_in(key, 14)
    drawn = jax.random.randint(key, (FR_DEV, N_FRAME, TEXT), 0, 4)
    first = (jnp.arange(TEXT) == 0)[None, None, :]
    return jnp.where(first | (drawn < 3), 1, 0).astype(jnp.int32)


def plant(values, own_key, smallest, largest):
    shape = values.shape
    place = [jax.random.randint(jax.random.fold_in(own_key, axis), (), 0, shape[axis]) for axis in range(len(shape))]
    values = values.at[tuple(place)].set(smallest)
    longest = shape.index(max(shape))
    place[longest] = (place[longest] + 1) % shape[longest]
    return values.at[tuple(place)].set(largest)


def shard_levels(own_key, dims, split, low, high):
    def one(dim, shards_of):
        heights = jax.random.uniform(jax.random.fold_in(jax.random.fold_in(own_key, 6), dim), (shards_of,), jnp.float32, low / len(split), high / len(split))
        return jnp.repeat(jnp.exp(heights), dims[dim] // shards_of).reshape((-1,) + (1,) * (len(dims) - dim - 1))

    level = one(*split[0])
    for cut in split[1:]:
        level = level * one(*cut)
    return level


def gaussian(rng, shape, scale, limit, cuts=(), held_as=jnp.bfloat16):
    values = scale * jax.random.normal(rng, shape, jnp.float32)
    if cuts:
        values = values * shard_levels(rng, shape, cuts, -0.22, 0.18)
    return jnp.clip(values, -limit, limit).astype(held_as)


def setup_inputs(seed: int = 0) -> dict:
    arg_keys = jax.random.split(jax.random.key(seed), 23)
    return {
        "video_in": draw_video_in(jax.random.fold_in(arg_keys[22], 71), 0),
        "time_embed": gaussian(arg_keys[1], (FR_DEV, N_FRAME, TEMB), 1.0, 6.0, ((1, 16),)),
        "text_embed": gaussian(arg_keys[2], (FR_DEV, N_FRAME, TEXT, CTX), 1.0, 6.0, ((1, 16), (2, 2))),
        "text_mask": draw_text_mask(jax.random.fold_in(arg_keys[22], 71), 0),
        "video_mask": draw_video_mask(jax.random.fold_in(arg_keys[22], 71), 0),
        "video_number": draw_video_number(jax.random.fold_in(arg_keys[22], 71), 0),
        "bucket_index": plant(jax.random.randint(arg_keys[6], (GROUP_LEN, GROUP_LEN), 0, NB), jax.random.fold_in(arg_keys[6], 1), 0, NB - 1).astype(jnp.int32),
        "norm_gains": jnp.clip(1.0 + 0.1 * jax.random.normal(arg_keys[7], (C, NORMS), jnp.float32), 0.5, 1.5),
        "bias_table": gaussian(arg_keys[8], (NB, HEADS), 1.0, 4.0, (), jnp.float32),
        "conv_first": gaussian(arg_keys[9], (9 * C, C), (9 * C) ** -0.5, 0.109375, ((0, 16), (1, 2))),
        "conv_second": gaussian(arg_keys[10], (9 * C, C), (9 * C) ** -0.5, 0.109375, ((0, 16), (1, 2))),
        "film_weight": gaussian(arg_keys[11], (TEMB, 2 * C), TEMB ** -0.5, 0.15625, ((0, 16), (1, 2))),
        "self_project": gaussian(arg_keys[12], (C, 3 * C), C ** -0.5, 0.3125, ((0, 16), (1, 2))),
        "self_output": gaussian(arg_keys[13], (C, C), (C // 8) ** -0.5, 1.0, ((0, 16), (1, 2))),
        "cross_query": gaussian(arg_keys[14], (C, C), C ** -0.5, 0.3125, ((0, 16), (1, 2))),
        "cross_keyval": gaussian(arg_keys[15], (CTX, 2 * C), CTX ** -0.5, 0.1875, ((0, 16), (1, 2))),
        "cross_output": gaussian(arg_keys[16], (C, C), (C // 4) ** -0.5, 0.625, ((0, 16), (1, 2))),
        "time_project": gaussian(arg_keys[17], (C, 3 * C), C ** -0.5, 0.3125, ((0, 16), (1, 2))),
        "time_output": gaussian(arg_keys[18], (C, C), (C // 2) ** -0.5, 0.5, ((0, 16), (1, 2))),
        "feed_up": gaussian(arg_keys[19], (C, FF), C ** -0.5, 0.3125, ((0, 16), (1, 2))),
        "feed_down": gaussian(arg_keys[20], (FF, C), FF ** -0.5, 0.15625, ((0, 16), (1, 2))),
        "cotangent": gaussian(arg_keys[21], (FR_DEV, N_FRAME, IMG_H, IMG_W, C), 1.0, 6.0, ((1, 16), (2, 2))),
    }


@jax.custom_vjp
def low(v):
    return lax.optimization_barrier(v.astype(jnp.bfloat16)).astype(jnp.float32)

@jax.custom_vjp
def low_back(v):
    return v

def low_keep(v):
    return (low(v), None)

def low_pass(kept, grad):
    return (grad,)

def back_keep(v):
    return (v, None)

def back_low(kept, grad):
    return (low(grad),)
low.defvjp(low_keep, low_pass)
low_back.defvjp(back_keep, back_low)
EPSILON = 1e-05
MASKED = -1e+30
PRECISE = lax.Precision.HIGHEST

def product(left, right):
    return jnp.matmul(left, right, precision=PRECISE, preferred_element_type=jnp.float32)

def layer_norm(layer, gain):
    centered = layer - lax.optimization_barrier(jnp.mean(layer, axis=-1, keepdims=True))
    return centered * lax.rsqrt(lax.optimization_barrier(jnp.mean(centered * centered, axis=-1, keepdims=True)) + EPSILON) * gain

def group_norm(layer, gain):
    grouped = layer.reshape(layer.shape[0], IMG_H * IMG_W, GROUPS, C // GROUPS)
    center = lax.optimization_barrier(jnp.mean(grouped, axis=(1, 3), keepdims=True))
    spread = lax.rsqrt(lax.optimization_barrier(jnp.mean(grouped * grouped, axis=(1, 3), keepdims=True)) - center * center + EPSILON)
    return ((grouped - center) * spread).reshape(layer.shape) * gain

def convolve(layer, weight):
    image = layer.reshape(-1, IMG_H, IMG_W, C)
    padded = jnp.pad(image, ((0, 0), (1, 1), (1, 1), (0, 0)))
    summed = jnp.zeros(image.shape, jnp.float32)
    for row_off in range(3):
        for col_off in range(3):
            tap_index = 3 * row_off + col_off
            summed = summed + product(padded[:, row_off:row_off + IMG_H, col_off:col_off + IMG_W, :], weight[tap_index * C:(tap_index + 1) * C])
    return summed.reshape(layer.shape)

def self_attend(pieces):
    queries, key_rows, value_rows = pieces
    scores = low_back(jnp.einsum('qhd,khd->hqk', queries, key_rows, precision=PRECISE) * HEAD ** (-0.5))
    attn_probs = low(jax.nn.softmax(scores, axis=-1))
    return low(low_back(jnp.einsum('hqk,khd->qhd', attn_probs, value_rows, precision=PRECISE)))

def cross_attend(pieces):
    queries, key_rows, value_rows, usable = pieces
    scores = low_back(jnp.einsum('qhd,khd->hqk', queries, key_rows, precision=PRECISE) * HEAD ** (-0.5))
    scores = jnp.where(usable[None, None, :] == 1, scores, MASKED)
    attn_probs = low(jax.nn.softmax(scores, axis=-1))
    return low(low_back(jnp.einsum('hqk,khd->qhd', attn_probs, value_rows, precision=PRECISE)))

def slot_forward(params, video_in, time_embed, text_embed, text_mask, video_mask, video_number, bucket_index):
    norm_gains, bias_table, conv_first, conv_second, film_weight, self_project, self_output, cross_query, cross_keyval, cross_output, time_project, time_output, feed_up, feed_down = params
    pixels = IMG_H * IMG_W
    heads_view = (N_FRAME, pixels, HEADS, HEAD)
    text_view = (N_FRAME, TEXT, HEADS, HEAD)
    current = video_in.reshape(N_FRAME, pixels, C)
    film_all = product(low(jax.nn.silu(time_embed)), film_weight)[:, None, :]
    act_one = low(jax.nn.silu(group_norm(current, norm_gains[:, 0])))
    conv_out = low_back(convolve(act_one, conv_first))
    hidden = conv_out * (1.0 + film_all[..., :C]) + film_all[..., C:]
    act_two = low(jax.nn.silu(group_norm(hidden, norm_gains[:, 1])))
    current = current + low_back(convolve(act_two, conv_second))
    project = low(low_back(product(low(layer_norm(current, norm_gains[:, 2])), self_project)))
    mixture = lax.map(jax.checkpoint(self_attend), (project[..., :C].reshape(heads_view), project[..., C:2 * C].reshape(heads_view), project[..., 2 * C:].reshape(heads_view)))
    current = current + low_back(product(mixture.reshape(N_FRAME, pixels, C), self_output))
    text_pairs = low(low_back(product(text_embed, cross_keyval)))
    queries = low(low_back(product(low(layer_norm(current, norm_gains[:, 3])), cross_query)))
    mixture = lax.map(jax.checkpoint(cross_attend), (queries.reshape(heads_view), text_pairs[..., :C].reshape(text_view), text_pairs[..., C:].reshape(text_view), text_mask))
    current = current + low_back(product(mixture.reshape(N_FRAME, pixels, C), cross_output))
    project = low(low_back(product(low(layer_norm(current, norm_gains[:, 4])), time_project)))
    frame_ids = jnp.arange(N_FRAME)
    positions = frame_ids % GROUP_LEN
    time_bias = jnp.transpose(bias_table[bucket_index[positions[:, None], positions[None, :]]], (2, 0, 1))
    same_group = frame_ids[:, None] // GROUP_LEN == frame_ids[None, :] // GROUP_LEN
    together = (video_mask[:, None] == 1) & (video_mask[None, :] == 1) & (video_number[:, None] == video_number[None, :])
    allowed = same_group & (together | (frame_ids[:, None] == frame_ids[None, :]))
    queries = project[..., :C].reshape(heads_view)
    key_rows = project[..., C:2 * C].reshape(heads_view)
    value_rows = project[..., 2 * C:].reshape(heads_view)
    scores = low_back(jnp.einsum('nphd,mphd->phnm', queries, key_rows, precision=PRECISE) * HEAD ** (-0.5) + time_bias[None])
    scores = jnp.where(allowed[None, None], scores, MASKED)
    attn_probs = low(jax.nn.softmax(scores, axis=-1))
    mixture = low(low_back(jnp.einsum('phnm,mphd->nphd', attn_probs, value_rows, precision=PRECISE)))
    current = current + low_back(product(mixture.reshape(N_FRAME, pixels, C), time_output))
    lifted = low_back(product(low(layer_norm(current, norm_gains[:, 5])), feed_up))
    current = current + low_back(product(low(jax.nn.gelu(lifted, approximate=True)), feed_down))
    return current.reshape(video_in.shape)

def reference(video_in, time_embed, text_embed, text_mask, video_mask, video_number, bucket_index, norm_gains, bias_table, conv_first, conv_second, film_weight, self_project, self_output, cross_query, cross_keyval, cross_output, time_project, time_output, feed_up, feed_down, cotangent):
    params = tuple((weight_in.astype(jnp.float32) for weight_in in (norm_gains, bias_table, conv_first, conv_second, film_weight, self_project, self_output, cross_query, cross_keyval, cross_output, time_project, time_output, feed_up, feed_down)))

    def one_slot(carried, inputs):
        slot_video, slot_time, slot_text, slot_mask, slot_live, slot_number, slot_cot = inputs

        def forward(weights, layer):
            return slot_forward(weights, layer, slot_time.astype(jnp.float32), slot_text.astype(jnp.float32), slot_mask, slot_live, slot_number, bucket_index)
        result, pull_back = jax.vjp(forward, params, slot_video.astype(jnp.float32))
        weight_grads, layer_grad = pull_back(slot_cot.astype(jnp.float32))
        carried = jax.tree.map(jnp.add, carried, weight_grads)
        return (carried, (result.astype(jnp.bfloat16), layer_grad.astype(jnp.bfloat16)))
    totals, outputs = lax.scan(one_slot, jax.tree.map(jnp.zeros_like, params), (video_in, time_embed, text_embed, text_mask, video_mask, video_number, cotangent))
    return (outputs[0], outputs[1], totals[0], totals[1], totals[2], totals[3], totals[4], totals[5], totals[6], totals[7], totals[8], totals[9], totals[10], totals[11], totals[12], totals[13])
```

```python
from typing import Any, NamedTuple

import jax
import jax.numpy as jnp
from jax import lax
from jax.experimental import pallas as pl
from jax.experimental.pallas import tpu as pltpu
from jax.sharding import Mesh
from jax.sharding import PartitionSpec as P

C = 320
HEADS = 5
HEAD = 64
GROUPS = 32
CTX = 1024
TEMB = 1280
TEXT = 128
IMG_H = 24
IMG_W = 48
FR_DEV = 2
GROUP_LEN = 16
NB = 32
FF = 1280
GELU_A = 0.7978845608028654
GELU_B = 0.044715


FRAME = "frame"
SPACE = "space"
HALF = "half"
QUAD = "quad"
CORE = "core"
EPSILON = 1e-05
MASKED = -1e30
SINGLE = jnp.float32
NARROW = jnp.bfloat16
PRECISE = lax.Precision.HIGHEST


def with_halo(block, sides, width):
    for axis, dim in sides:
        count = lax.axis_size(axis)
        forward = [(i, i + 1) for i in range(count - 1)]
        backward = [(target, source) for source, target in forward]
        low = lax.ppermute(
            lax.slice_in_dim(block, block.shape[dim] - width, None, axis=dim), axis, forward
        )
        high = lax.ppermute(lax.slice_in_dim(block, 0, width, axis=dim), axis, backward)
        block = jnp.concatenate([low, block, high], axis=dim)
    return block


def collect(item_one, item_two, item_three):
    row_full = (
        lax.all_gather(item_one, FRAME, axis=0, tiled=True),
        lax.all_gather(item_two, FRAME, axis=0, tiled=True),
        lax.all_gather(item_three, FRAME, axis=0, tiled=True),
    )
    return (
        lax.all_gather(row_full[0], SPACE, axis=1, tiled=True),
        lax.all_gather(row_full[1], SPACE, axis=1, tiled=True),
        lax.all_gather(row_full[2], SPACE, axis=1, tiled=True),
    )


def settle(item_one, item_two, item_three):
    column_sums = (
        lax.psum_scatter(
            item_one.astype(jnp.bfloat16), SPACE, scatter_dimension=1, tiled=True
        ).astype(jnp.float32),
        lax.psum_scatter(
            item_two.astype(jnp.bfloat16), SPACE, scatter_dimension=1, tiled=True
        ).astype(jnp.float32),
        lax.psum_scatter(
            item_three.astype(jnp.bfloat16), SPACE, scatter_dimension=1, tiled=True
        ).astype(jnp.float32),
    )
    return (
        lax.psum_scatter(
            column_sums[0].astype(jnp.bfloat16), FRAME, scatter_dimension=0, tiled=True
        ).astype(jnp.float32),
        lax.psum_scatter(
            column_sums[1].astype(jnp.bfloat16), FRAME, scatter_dimension=0, tiled=True
        ).astype(jnp.float32),
        lax.psum_scatter(
            column_sums[2].astype(jnp.bfloat16), FRAME, scatter_dimension=0, tiled=True
        ).astype(jnp.float32),
    )


def space_sums(item_one, item_two):
    return lax.psum((item_one, item_two), SPACE)


def columns_of(padded):
    height_here = padded.shape[1] - 2
    pieces = [
        padded[:, row_off : row_off + height_here, col_off : col_off + IMG_W, :]
        for row_off in range(3)
        for col_off in range(3)
    ]
    return jnp.concatenate(pieces, axis=-1).reshape(-1, 9 * C)


def convolve(activation, weight):
    slot_count, rows_here = (activation.shape[0], activation.shape[1])
    image = activation.reshape(slot_count, rows_here // IMG_W, IMG_W, C)
    rimmed = with_halo(image, ((SPACE, 1),), 1)
    padded = jnp.pad(rimmed, ((0, 0), (0, 0), (1, 1), (0, 0)))
    summed = jnp.dot(columns_of(padded), weight, preferred_element_type=SINGLE)
    return (summed.reshape(slot_count, rows_here, C), padded)


def convolve_back(grad_low, weight):
    flipped = weight.reshape(3, 3, C, C)[::-1, ::-1].transpose(0, 1, 3, 2).reshape(9 * C, C)
    summed, padded = convolve(grad_low, flipped)
    return summed


def weight_grad(left, right):
    return lax.dot_general(
        left.reshape(-1, left.shape[-1]),
        right.reshape(-1, right.shape[-1]),
        (((0,), (0,)), ((), ())),
        preferred_element_type=SINGLE,
    )


def back_project(grad_low, weight):
    return jnp.einsum("...o,io->...i", grad_low, weight, preferred_element_type=SINGLE)


def layer_norm(layer, gain):
    centered = layer - jnp.mean(layer, axis=-1, keepdims=True)
    return (
        centered * lax.rsqrt(jnp.mean(centered * centered, axis=-1, keepdims=True) + EPSILON) * gain
    )


def group_forward(layer):
    slot_count, rows_here = (layer.shape[0], layer.shape[1])
    grouped = layer.reshape(slot_count, rows_here, GROUPS, C // GROUPS)
    summed, squares = space_sums(
        jnp.sum(grouped, axis=(1, 3)), jnp.sum(grouped * grouped, axis=(1, 3))
    )
    members = IMG_H * IMG_W * (C // GROUPS)
    center = summed / members
    spread = lax.rsqrt(squares / members - center * center + EPSILON)
    normed = (grouped - center[:, None, :, None]) * spread[:, None, :, None]
    return (normed.reshape(slot_count, rows_here, C), spread)


def group_backward(normed, spread, upstream):
    slot_count, rows_here = (normed.shape[0], normed.shape[1])
    grad_groups = upstream.reshape(slot_count, rows_here, GROUPS, C // GROUPS)
    norm_groups = normed.reshape(slot_count, rows_here, GROUPS, C // GROUPS)
    summed, crossed = space_sums(
        jnp.sum(grad_groups, axis=(1, 3)), jnp.sum(grad_groups * norm_groups, axis=(1, 3))
    )
    members = IMG_H * IMG_W * (C // GROUPS)
    result = spread[:, None, :, None] * (
        grad_groups
        - summed[:, None, :, None] / members
        - norm_groups * crossed[:, None, :, None] / members
    )
    return result.reshape(slot_count, rows_here, C)


def masked_scores(queries, key_rows, usable):
    scores = jnp.einsum(
        "qhd,khd->hqk", queries, key_rows, preferred_element_type=SINGLE
    ) * HEAD ** (-0.5)
    return jnp.where(usable[None, None, :], scores, MASKED)


def attend_forward(queries, key_rows, value_rows, usable):
    scores = masked_scores(queries, key_rows, usable)
    highest = jnp.max(scores, axis=-1, keepdims=True)
    log_total = highest + jnp.log(jnp.sum(jnp.exp(scores - highest), axis=-1, keepdims=True))
    attn_probs = jnp.exp(scores - log_total).astype(NARROW)
    mixture = jnp.einsum(
        "hqk,khd->qhd", attn_probs, value_rows, preferred_element_type=SINGLE
    ).astype(NARROW)
    return (mixture, log_total[..., 0])


def attend_backward(queries, key_rows, value_rows, usable, log_total, grad_mixture):
    scores = masked_scores(queries, key_rows, usable)
    attn_probs = jnp.exp(scores - log_total[..., None])
    grad_probs = jnp.einsum("qhd,khd->hqk", grad_mixture, value_rows, preferred_element_type=SINGLE)
    row_inner = jnp.sum(grad_probs * attn_probs, axis=-1, keepdims=True)
    grad_scores = (attn_probs * (grad_probs - row_inner)).astype(NARROW)
    grad_queries = jnp.einsum(
        "hqk,khd->qhd", grad_scores, key_rows, preferred_element_type=SINGLE
    ) * HEAD ** (-0.5)
    grad_keys = jnp.einsum(
        "hqk,qhd->khd", grad_scores, queries, preferred_element_type=SINGLE
    ) * HEAD ** (-0.5)
    grad_values = jnp.einsum(
        "hqk,qhd->khd", attn_probs.astype(NARROW), grad_mixture, preferred_element_type=SINGLE
    )
    return (grad_queries, grad_keys, grad_values)


def time_scores(queries, gathered, time_bias, allowed):
    key_rows = gathered[..., :C].reshape(gathered.shape[0], gathered.shape[1], HEADS, HEAD)
    scores = (
        jnp.einsum("rhd,grhd->rhg", queries, key_rows, preferred_element_type=SINGLE)
        * HEAD ** (-0.5)
        + time_bias[None]
    )
    return (jnp.where(allowed[None, None, :], scores, MASKED), key_rows)


def shards(
    video_in,
    time_embed,
    text_embed,
    text_mask,
    video_mask,
    video_number,
    bucket_index,
    norm_gains,
    bias_table,
    conv_first,
    conv_second,
    film_weight,
    self_project,
    self_output,
    cross_query,
    cross_keyval,
    cross_output,
    time_project,
    time_output,
    feed_up,
    feed_down,
    cotangent,
):
    height_here = video_in.shape[2]
    rows_here = height_here * IMG_W
    text_here = text_embed.shape[2]
    frame_count = video_mask.shape[1]
    frame_index = lax.axis_index(FRAME)
    group_place = frame_index % GROUP_LEN
    heads_view = (FR_DEV, rows_here, HEADS, HEAD)
    every_key = jnp.ones((IMG_H * IMG_W,), jnp.bool_)
    frame_ids = jnp.arange(frame_count)
    place_ids = jnp.arange(GROUP_LEN)
    bucket_row = jnp.sum(jnp.where((place_ids == group_place)[:, None], bucket_index, 0), axis=0)
    key_buckets = jnp.sum(
        jnp.where((frame_ids % GROUP_LEN)[:, None] == place_ids[None, :], bucket_row[None, :], 0),
        axis=1,
    )
    key_table = (key_buckets[:, None] == jnp.arange(NB)[None, :]).astype(SINGLE)
    time_bias = jnp.dot(key_table, bias_table, precision=PRECISE, preferred_element_type=SINGLE).T

    def allowed_for(live_slot, number_slot):
        chooser = frame_ids[:, None] == frame_ids[None, :]
        live_keys = jnp.sum(jnp.where(chooser, live_slot[None, :], 0), axis=1)
        number_keys = jnp.sum(jnp.where(chooser, number_slot[None, :], 0), axis=1)
        own_frame = frame_ids == frame_index
        live_own = jnp.sum(jnp.where(own_frame, live_slot, 0))
        number_own = jnp.sum(jnp.where(own_frame, number_slot, 0))
        same_group = frame_ids // GROUP_LEN == frame_index // GROUP_LEN
        together = (live_keys == 1) & (live_own == 1) & (number_keys == number_own)
        return same_group & (together | (frame_ids == frame_index))

    def spread_keys(own_pair):
        return lax.all_gather(own_pair, FRAME, axis=0, tiled=True)

    def return_keys(spread_grads):
        return lax.psum_scatter(
            spread_grads.astype(jnp.bfloat16), FRAME, scatter_dimension=0, tiled=True
        ).astype(jnp.float32)

    def gather_keys(frame_pair, text_pair):
        return (
            lax.all_gather(frame_pair, SPACE, axis=0, tiled=True),
            lax.all_gather(text_pair, SPACE, axis=0, tiled=True),
        )

    def scatter_keys(frame_grads, text_grads):
        return (
            lax.psum_scatter(
                frame_grads.astype(jnp.bfloat16), SPACE, scatter_dimension=0, tiled=True
            ).astype(jnp.float32),
            lax.psum_scatter(
                text_grads.astype(jnp.bfloat16), SPACE, scatter_dimension=0, tiled=True
            ).astype(jnp.float32),
        )

    resid = video_in.reshape(FR_DEV, rows_here, C).astype(SINGLE)
    conv_one, film_full, conv_two = collect(conv_first, film_weight, conv_second)
    temb_act = jax.nn.silu(time_embed.reshape(FR_DEV, TEMB).astype(SINGLE)).astype(NARROW)
    film_all = jnp.dot(temb_act, film_full, preferred_element_type=SINGLE)
    film_scale = 1.0 + film_all[:, None, :C]
    film_shift = film_all[:, None, C:]
    normed_one, spread_one = group_forward(resid)
    pre_one = normed_one * norm_gains[:, 0]
    conv_out, pad_one = convolve(jax.nn.silu(pre_one).astype(NARROW), conv_one)
    hidden = conv_out * film_scale + film_shift
    normed_two, spread_two = group_forward(hidden)
    pre_two = normed_two * norm_gains[:, 1]
    branch_two, pad_two = convolve(jax.nn.silu(pre_two).astype(NARROW), conv_two)
    section_one = resid + branch_two
    kv_weight, qkv_weight, self_weight = collect(cross_keyval, self_project, self_output)
    text_kv = (
        jnp.dot(
            text_embed.reshape(FR_DEV * text_here, CTX), kv_weight, preferred_element_type=SINGLE
        )
        .astype(NARROW)
        .reshape(FR_DEV, text_here, 2 * C)
    )
    self_in = layer_norm(section_one, norm_gains[:, 2]).astype(NARROW)
    self_proj = jnp.dot(self_in, qkv_weight, preferred_element_type=SINGLE).astype(NARROW)

    def self_slot(inputs):
        proj_slot, text_slot = inputs
        frame_kv, text_full = gather_keys(proj_slot[:, C:], text_slot)
        mixture, log_total = attend_forward(
            proj_slot[:, :C].reshape(rows_here, HEADS, HEAD),
            frame_kv[:, :C].reshape(-1, HEADS, HEAD),
            frame_kv[:, C:].reshape(-1, HEADS, HEAD),
            every_key,
        )
        return (mixture, log_total, text_full)

    self_mixed, self_lse, text_all = lax.map(self_slot, (self_proj, text_kv))
    self_mixed = self_mixed.reshape(FR_DEV, rows_here, C)
    section_two = section_one + jnp.dot(self_mixed, self_weight, preferred_element_type=SINGLE)
    query_weight, cross_weight, time_weight = collect(cross_query, cross_output, time_project)
    cross_in = layer_norm(section_two, norm_gains[:, 3]).astype(NARROW)
    cross_queries = (
        jnp.dot(cross_in, query_weight, preferred_element_type=SINGLE)
        .astype(NARROW)
        .reshape(heads_view)
    )
    text_usable = text_mask.reshape(FR_DEV, TEXT) == 1
    text_keys = text_all[..., :C].reshape(FR_DEV, TEXT, HEADS, HEAD)
    text_values = text_all[..., C:].reshape(FR_DEV, TEXT, HEADS, HEAD)
    cross_mixed, cross_lse = jax.vmap(attend_forward)(
        cross_queries, text_keys, text_values, text_usable
    )
    cross_mixed = cross_mixed.reshape(FR_DEV, rows_here, C)
    section_three = section_two + jnp.dot(cross_mixed, cross_weight, preferred_element_type=SINGLE)
    time_in = layer_norm(section_three, norm_gains[:, 4]).astype(NARROW)
    time_proj = jnp.dot(time_in, time_weight, preferred_element_type=SINGLE).astype(NARROW)

    def time_slot(inputs):
        proj_slot, live_slot, number_slot = inputs
        gathered = spread_keys(proj_slot[None, :, C:])
        queries = proj_slot[:, :C].reshape(rows_here, HEADS, HEAD)
        scores, key_rows = time_scores(
            queries, gathered, time_bias, allowed_for(live_slot, number_slot)
        )
        value_rows = gathered[..., C:].reshape(key_rows.shape)
        highest = jnp.max(scores, axis=-1, keepdims=True)
        log_total = highest + jnp.log(jnp.sum(jnp.exp(scores - highest), axis=-1, keepdims=True))
        attn_probs = jnp.exp(scores - log_total).astype(NARROW)
        mixture = jnp.einsum(
            "rhg,grhd->rhd", attn_probs, value_rows, preferred_element_type=SINGLE
        ).astype(NARROW)
        return (mixture, log_total[..., 0])

    time_mixed, time_lse = lax.map(time_slot, (time_proj, video_mask, video_number))
    time_mixed = time_mixed.reshape(FR_DEV, rows_here, C)
    out_weight, inner_weight, outer_weight = collect(time_output, feed_up, feed_down)
    section_four = section_three + jnp.dot(time_mixed, out_weight, preferred_element_type=SINGLE)
    feed_in = layer_norm(section_four, norm_gains[:, 5]).astype(NARROW)
    lifted = jnp.dot(feed_in, inner_weight, preferred_element_type=SINGLE)
    activated = jax.nn.gelu(lifted, approximate=True).astype(NARROW)
    result = section_four + jnp.dot(activated, outer_weight, preferred_element_type=SINGLE)
    block_out = result.astype(NARROW).reshape(video_in.shape)
    carried = cotangent.reshape(FR_DEV, rows_here, C).astype(SINGLE)
    back_feed = carried.astype(NARROW)
    grad_down = weight_grad(activated, back_feed)
    grad_act = back_project(back_feed, outer_weight)
    value_gelu, pull_gelu = jax.vjp(lambda layer: jax.nn.gelu(layer, approximate=True), lifted)
    grad_lifted = pull_gelu(grad_act)[0].astype(NARROW)
    grad_up = weight_grad(feed_in, grad_lifted)
    value_norm, pull_norm = jax.vjp(layer_norm, section_four, norm_gains[:, 5])
    norm_part, gain_five = pull_norm(back_project(grad_lifted, inner_weight))
    carried = carried + norm_part
    back_time = carried.astype(NARROW)
    grad_time_out = weight_grad(time_mixed, back_time)
    grad_time_mixed = back_project(back_time, out_weight).astype(NARROW).reshape(heads_view)
    down_grads = settle(grad_time_out, grad_up, grad_down)

    def time_back(inputs):
        proj_slot, live_slot, number_slot, lse_slot, grad_slot = inputs
        gathered = spread_keys(proj_slot[None, :, C:])
        queries = proj_slot[:, :C].reshape(rows_here, HEADS, HEAD)
        scores, key_rows = time_scores(
            queries, gathered, time_bias, allowed_for(live_slot, number_slot)
        )
        value_rows = gathered[..., C:].reshape(key_rows.shape)
        attn_probs = jnp.exp(scores - lse_slot[..., None])
        grad_probs = jnp.einsum(
            "rhd,grhd->rhg", grad_slot, value_rows, preferred_element_type=SINGLE
        )
        row_inner = jnp.sum(grad_probs * attn_probs, axis=-1, keepdims=True)
        grad_scores = (attn_probs * (grad_probs - row_inner)).astype(NARROW)
        grad_queries = jnp.einsum(
            "rhg,grhd->rhd", grad_scores, key_rows, preferred_element_type=SINGLE
        ) * HEAD ** (-0.5)
        grad_keys = jnp.einsum(
            "rhg,rhd->grhd", grad_scores, queries, preferred_element_type=SINGLE
        ) * HEAD ** (-0.5)
        grad_values = jnp.einsum(
            "rhg,rhd->grhd", attn_probs.astype(NARROW), grad_slot, preferred_element_type=SINGLE
        )
        key_count = key_rows.shape[0]
        spread_grads = jnp.concatenate(
            [
                grad_keys.reshape(key_count, rows_here, C),
                grad_values.reshape(key_count, rows_here, C),
            ],
            -1,
        )
        own_grads = return_keys(spread_grads)[0]
        bias_grad = jnp.sum(grad_scores.astype(SINGLE), axis=0)
        return (jnp.concatenate([grad_queries.reshape(rows_here, C), own_grads], -1), bias_grad)

    grad_time_proj, bias_grads = lax.map(
        time_back, (time_proj, video_mask, video_number, time_lse, grad_time_mixed)
    )
    grad_table = jnp.dot(
        key_table.T, jnp.sum(bias_grads, axis=0).T, precision=PRECISE, preferred_element_type=SINGLE
    )
    grad_time_proj = grad_time_proj.astype(NARROW)
    grad_time_qkv = weight_grad(time_in, grad_time_proj)
    value_norm, pull_norm = jax.vjp(layer_norm, section_three, norm_gains[:, 4])
    norm_part, gain_four = pull_norm(back_project(grad_time_proj, time_weight))
    carried = carried + norm_part
    back_cross = carried.astype(NARROW)
    grad_cross_out = weight_grad(cross_mixed, back_cross)
    grad_cross_mixed = back_project(back_cross, cross_weight).astype(NARROW).reshape(heads_view)
    grad_cquery, grad_tkeys, grad_tvalues = jax.vmap(attend_backward)(
        cross_queries, text_keys, text_values, text_usable, cross_lse, grad_cross_mixed
    )
    grad_cquery = grad_cquery.reshape(FR_DEV, rows_here, C).astype(NARROW)
    grad_cross_q = weight_grad(cross_in, grad_cquery)
    value_norm, pull_norm = jax.vjp(layer_norm, section_two, norm_gains[:, 3])
    norm_part, gain_three = pull_norm(back_project(grad_cquery, query_weight))
    carried = carried + norm_part
    text_grads = jnp.concatenate(
        [grad_tkeys.reshape(FR_DEV, TEXT, C), grad_tvalues.reshape(FR_DEV, TEXT, C)], -1
    )
    middle_grads = settle(grad_cross_q, grad_cross_out, grad_time_qkv)
    back_self = carried.astype(NARROW)
    grad_self_out = weight_grad(self_mixed, back_self)
    grad_self_mixed = back_project(back_self, self_weight).astype(NARROW).reshape(heads_view)

    def self_back(inputs):
        proj_slot, text_slot, lse_slot, grad_slot, text_grad_slot = inputs
        frame_kv, text_again = gather_keys(proj_slot[:, C:], text_slot)
        grad_queries, grad_keys, grad_values = attend_backward(
            proj_slot[:, :C].reshape(rows_here, HEADS, HEAD),
            frame_kv[:, :C].reshape(-1, HEADS, HEAD),
            frame_kv[:, C:].reshape(-1, HEADS, HEAD),
            every_key,
            lse_slot,
            grad_slot,
        )
        frame_grads = jnp.concatenate([grad_keys.reshape(-1, C), grad_values.reshape(-1, C)], -1)
        own_frame, own_text = scatter_keys(frame_grads, text_grad_slot)
        return (jnp.concatenate([grad_queries.reshape(rows_here, C), own_frame], -1), own_text)

    grad_self_proj, grad_text_kv = lax.map(
        self_back, (self_proj, text_kv, self_lse, grad_self_mixed, text_grads)
    )
    grad_self_proj = grad_self_proj.astype(NARROW)
    grad_self_qkv = weight_grad(self_in, grad_self_proj)
    grad_keyval = weight_grad(
        text_embed.reshape(FR_DEV * text_here, CTX), grad_text_kv.astype(NARROW)
    )
    value_norm, pull_norm = jax.vjp(layer_norm, section_one, norm_gains[:, 2])
    norm_part, gain_two = pull_norm(back_project(grad_self_proj, qkv_weight))
    carried = carried + norm_part
    upper_grads = settle(grad_keyval, grad_self_qkv, grad_self_out)
    back_conv = carried.astype(NARROW)
    grad_conv_two = weight_grad(columns_of(pad_two), back_conv)
    grad_act_two = convolve_back(back_conv, conv_two)
    value_silu, pull_silu = jax.vjp(jax.nn.silu, pre_two)
    grad_pre_two = pull_silu(grad_act_two)[0]
    gain_one = jnp.sum(grad_pre_two * normed_two, axis=(0, 1))
    grad_hidden = group_backward(normed_two, spread_two, grad_pre_two * norm_gains[:, 1])
    grad_film = jnp.concatenate(
        [jnp.sum(grad_hidden * conv_out, axis=1), jnp.sum(grad_hidden, axis=1)], -1
    )
    grad_film_w = jnp.dot(
        temb_act.astype(SINGLE).T, grad_film, precision=PRECISE, preferred_element_type=SINGLE
    )
    back_first = (grad_hidden * film_scale).astype(NARROW)
    grad_conv_one = weight_grad(columns_of(pad_one), back_first)
    grad_act_one = convolve_back(back_first, conv_one)
    value_silu, pull_silu = jax.vjp(jax.nn.silu, pre_one)
    grad_pre_one = pull_silu(grad_act_one)[0]
    gain_zero = jnp.sum(grad_pre_one * normed_one, axis=(0, 1))
    carried = carried + group_backward(normed_one, spread_one, grad_pre_one * norm_gains[:, 0])
    input_grad = carried.astype(NARROW).reshape(video_in.shape)
    lower_grads = settle(grad_conv_one, grad_film_w, grad_conv_two)
    gain_stack = jnp.stack(
        [gain_zero, gain_one, gain_two, gain_three, gain_four, gain_five], axis=1
    )
    small_sums = lax.psum((gain_stack, grad_table), (FRAME, SPACE))
    return (
        block_out,
        input_grad,
        small_sums[0],
        small_sums[1],
        lower_grads[0],
        lower_grads[2],
        lower_grads[1],
        upper_grads[1],
        upper_grads[2],
        middle_grads[0],
        upper_grads[0],
        middle_grads[1],
        middle_grads[2],
        down_grads[0],
        down_grads[1],
        down_grads[2],
    )


PIX = IMG_H * IMG_W
CUBE = (QUAD, CORE, SPACE)
CHIPS = (QUAD, SPACE)
PAIR = (HALF, SPACE)
WORLD = (HALF, QUAD, CORE, SPACE)
SCALE = HEAD ** (-0.5)


def swap_space():
    return [(2 * a + b, 2 * b + a) for a in range(2) for b in range(2)]


def turn_space():
    return [(2 * a + b, 2 * (1 - b) + a) for a in range(2) for b in range(2)]


def pick(flag, pair):
    return jnp.where(flag == 0, pair[0], pair[1])


def to_slot(block, half, space):
    own = lax.ppermute(pick(space, block), PAIR, swap_space())
    other = lax.ppermute(pick(1 - space, block), PAIR, turn_space())
    return jnp.concatenate(
        [jnp.where(half == 0, own, other), jnp.where(half == 0, other, own)], axis=0
    )


def from_slot(frame, half, space):
    pieces = frame.reshape((2, frame.shape[0] // 2) + frame.shape[1:])
    own = lax.ppermute(pick(half, pieces), PAIR, [(d, s) for s, d in swap_space()])
    other = lax.ppermute(pick(1 - half, pieces), PAIR, [(d, s) for s, d in turn_space()])
    return jnp.stack([jnp.where(space == 0, own, other), jnp.where(space == 0, other, own)])


def meta_slot(block, space):
    return lax.ppermute(pick(space, block), PAIR, swap_space())


class Weights(NamedTuple):
    conv_first: Any
    conv_second: Any
    film_weight: Any
    self_project: Any
    self_output: Any
    cross_query: Any
    cross_keyval: Any
    cross_output: Any
    time_project: Any
    time_output: Any
    feed_up: Any
    feed_down: Any


def mm(a, b):
    return jnp.dot(a, b, preferred_element_type=SINGLE)


VMEM_BYTES = 58 * 1024 * 1024
STEP = 384
STEPS = PIX // STEP
NT = (((1,), (1,)), ((), ()))
TN = (((0,), (0,)), ((), ()))


def nt(a, b):
    return lax.dot_general(a, b, NT, preferred_element_type=SINGLE)


def tn(a, b):
    return lax.dot_general(a, b, TN, preferred_element_type=SINGLE)


def kernel_call(body, outs, scratch=(), flops=10**9):
    return pl.pallas_call(
        body,
        out_shape=[jax.ShapeDtypeStruct(s, d) for s, d in outs],
        scratch_shapes=[pltpu.VMEM(s, d) for s, d in scratch],
        compiler_params=pltpu.CompilerParams(vmem_limit_bytes=VMEM_BYTES),
        cost_estimate=pl.CostEstimate(flops=flops, bytes_accessed=10**7, transcendentals=0),
    )


def group_matrix():
    lanes = jnp.arange(C) // (C // GROUPS)
    return (lanes[:, None] == lanes[None, :]).astype(SINGLE)


def grouped(row, gmat):
    wide = jnp.broadcast_to(row, (8, C))
    return lax.dot_general(
        wide, gmat, (((1,), (0,)), ((), ())), precision=PRECISE, preferred_element_type=SINGLE
    )[:1]


def edge_masks(rows):
    col = lax.broadcasted_iota(jnp.int32, (rows, C), 0) % IMG_W
    return col != 0, col != IMG_W - 1


def spread_columns(cols_ref, start, act):
    not_first, not_last = edge_masks(STEP)
    left = jnp.where(not_first, pltpu.roll(act, 1, 0), 0.0)
    right = jnp.where(not_last, pltpu.roll(act, STEP - 1, 0), 0.0)
    cols_ref[pl.ds(start, STEP), :] = jnp.concatenate(
        [left.astype(NARROW), act.astype(NARROW), right.astype(NARROW)], axis=1
    )


def conv_rows(cols_ref, w_ref, start):
    total = None
    for i in range(3):
        part = mm(cols_ref[pl.ds(start + IMG_W * i, STEP), :], w_ref[3 * C * i : 3 * C * (i + 1), :])
        total = part if total is None else total + part
    return total


def gn_stats(total, square, gmat):
    members = PIX * (C // GROUPS)
    center = grouped(total, gmat) / members
    return center, lax.rsqrt(grouped(square, gmat) / members - center * center + EPSILON)


def unpack_tall(half, full_ref, out_ref, at, rows, cols):
    parts = BAND // cols
    tall = rows // parts
    for quad in range(4):
        pieces = []
        for frame in range(4 * quad, 4 * quad + 4):
            place = half if frame < 8 else 1 - half
            sides = [
                full_ref[2 * (frame % 8) + s, place, at : at + tall, :].astype(SINGLE) for s in range(2)
            ]
            pieces += [
                jnp.concatenate([side[:, cols * q : cols * (q + 1)] for side in sides], axis=1)
                for q in range(parts)
            ]
        out_ref[4 * rows * quad : 4 * rows * (quad + 1), :] = jnp.concatenate(pieces, axis=0).astype(NARROW)


def clear_border(cols_ref):
    border = jnp.zeros((IMG_W, 3 * C), NARROW)
    cols_ref[0:IMG_W, :] = border
    cols_ref[PIX + IMG_W :, :] = border


def conv_kernel(x_ref, w1_ref, w2_ref, temb_ref, wf_ref, gains_ref, gmat_ref,
                conv_out_ref, sec_ref, cols1_ref, cols2_ref, stats_ref, film_ref):
    film_ref[...] = mm(temb_ref[...], wf_ref[...])
    gmat = gmat_ref[...]
    clear_border(cols1_ref)
    clear_border(cols2_ref)
    total = jnp.zeros((1, C), SINGLE)
    square = jnp.zeros((1, C), SINGLE)
    for r in range(STEPS):
        x = x_ref[r * STEP : (r + 1) * STEP, :].astype(SINGLE)
        total += jnp.sum(x, axis=0, keepdims=True)
        square += jnp.sum(x * x, axis=0, keepdims=True)
    center, spread = gn_stats(total, square, gmat)
    stats_ref[0:1, :] = center
    stats_ref[1:2, :] = spread
    for r in range(STEPS):
        x = x_ref[r * STEP : (r + 1) * STEP, :].astype(SINGLE)
        pre = (x - center) * spread * gains_ref[0:1, :]
        spread_columns(cols1_ref, IMG_W + r * STEP, pre * (0.5 + 0.5 * jnp.tanh(0.5 * pre)))
    scale = 1.0 + film_ref[0:1, :C]
    shift = film_ref[0:1, C:]
    total = jnp.zeros((1, C), SINGLE)
    square = jnp.zeros((1, C), SINGLE)
    for r in range(STEPS):
        out = conv_rows(cols1_ref, w1_ref, r * STEP)
        conv_out_ref[r * STEP : (r + 1) * STEP, :] = out
        hidden = out * scale + shift
        total += jnp.sum(hidden, axis=0, keepdims=True)
        square += jnp.sum(hidden * hidden, axis=0, keepdims=True)
    center, spread = gn_stats(total, square, gmat)
    stats_ref[2:3, :] = center
    stats_ref[3:4, :] = spread
    for r in range(STEPS):
        hidden = conv_out_ref[r * STEP : (r + 1) * STEP, :] * scale + shift
        pre = (hidden - center) * spread * gains_ref[1:2, :]
        spread_columns(cols2_ref, IMG_W + r * STEP, pre * (0.5 + 0.5 * jnp.tanh(0.5 * pre)))
    for r in range(STEPS):
        out = conv_rows(cols2_ref, w2_ref, r * STEP)
        rows = slice(r * STEP, (r + 1) * STEP)
        sec_ref[rows, :] = x_ref[rows, :].astype(SINGLE) + out


def conv_block(x, w1, w2, temb, wf, gains, gmat):
    cols = (PIX + 2 * IMG_W, 3 * C)
    return kernel_call(
        conv_kernel,
        [((PIX, C), SINGLE), ((PIX, C), SINGLE), (cols, NARROW), (cols, NARROW), ((8, C), SINGLE), ((8, 2 * C), SINGLE)],
        flops=15 * 10**9,
    )(x, w1, w2, temb, wf, gains, gmat)


def ln_rows(layer, gain):
    centered = layer - jnp.mean(layer, axis=-1, keepdims=True)
    rstd = lax.rsqrt(jnp.mean(centered * centered, axis=-1, keepdims=True) + EPSILON)
    return centered * rstd, rstd


def attend_rows(q, k, v_one, usable):
    scores = nt(q, k)
    if usable is not None:
        scores = jnp.where(usable, scores, MASKED)
    highest = jnp.max(scores, axis=-1, keepdims=True)
    probs = jnp.exp(scores - highest).astype(NARROW)
    both = mm(probs, v_one)
    total = both[:, HEAD : HEAD + 1]
    return both[:, :HEAD] / total, highest + jnp.log(total)


def with_ones(v):
    return jnp.concatenate([v, jnp.ones(v.shape, v.dtype)], axis=1)


def attn_kernel(sec1_ref, gains_ref, wqkv_ref, wso_ref, text_ref, usable_ref, wkv_ref, wcq_ref,
                wco_ref, wtime_ref,
                proj_ref, mix_ref, lse_ref, sec2_ref, kv_ref, cq_ref, cmix_ref, clse_ref,
                sec3_ref, tproj_ref):
    for r in range(STEPS):
        rows = slice(r * STEP, (r + 1) * STEP)
        hat, rstd = ln_rows(sec1_ref[rows, :], None)
        proj_ref[rows, :] = mm((hat * gains_ref[2:3, :]).astype(NARROW), wqkv_ref[...]).astype(NARROW)
    kv_ref[...] = mm(text_ref[...], wkv_ref[...]).astype(NARROW)
    for h in range(HEADS):
        lanes = slice(h * HEAD, (h + 1) * HEAD)
        k = proj_ref[:, C + h * HEAD : C + (h + 1) * HEAD]
        v = with_ones(proj_ref[:, 2 * C + h * HEAD : 2 * C + (h + 1) * HEAD])
        for r in range(STEPS):
            rows = slice(r * STEP, (r + 1) * STEP)
            q = proj_ref[rows, lanes] * jnp.bfloat16(SCALE)
            mix, lse = attend_rows(q, k, v, None)
            mix_ref[rows, lanes] = mix
            lse_ref[rows, h : h + 1] = lse
    usable = jnp.broadcast_to(usable_ref[...], (STEP, TEXT)) == 1
    for r in range(STEPS):
        rows = slice(r * STEP, (r + 1) * STEP)
        sec2 = sec1_ref[rows, :] + mm(mix_ref[rows, :].astype(NARROW), wso_ref[...])
        sec2_ref[rows, :] = sec2
        hat, rstd = ln_rows(sec2, None)
        cq_ref[rows, :] = mm((hat * gains_ref[3:4, :]).astype(NARROW), wcq_ref[...]).astype(NARROW)
        for h in range(HEADS):
            lanes = slice(h * HEAD, (h + 1) * HEAD)
            k = kv_ref[:, lanes]
            v = with_ones(kv_ref[:, C + h * HEAD : C + (h + 1) * HEAD])
            mix, lse = attend_rows(cq_ref[rows, lanes] * jnp.bfloat16(SCALE), k, v, usable)
            cmix_ref[rows, lanes] = mix
            clse_ref[rows, h : h + 1] = lse
        sec3 = sec2 + mm(cmix_ref[rows, :].astype(NARROW), wco_ref[...])
        sec3_ref[rows, :] = sec3
        hat, rstd = ln_rows(sec3, None)
        tproj_ref[rows, :] = mm((hat * gains_ref[4:5, :]).astype(NARROW), wtime_ref[...]).astype(NARROW)


def attn_block(sec1, gains, wqkv, wso, text, usable, wkv, wcq, wco, wtime):
    full = ((PIX, C), SINGLE)
    low = ((PIX, C), NARROW)
    return kernel_call(
        attn_kernel,
        [((PIX, 3 * C), NARROW), full, ((PIX, 8), SINGLE), full, ((TEXT, 2 * C), NARROW), low,
         full, ((PIX, 8), SINGLE), full, ((PIX, 3 * C), NARROW)],
        flops=28 * 10**9,
    )(sec1, gains, wqkv, wso, text, usable, wkv, wcq, wco, wtime)


def ln_back_rows(layer, gain, upstream):
    hat, rstd = ln_rows(layer, gain)
    dx = upstream * gain
    part = rstd * (
        dx - jnp.mean(dx, axis=-1, keepdims=True) - hat * jnp.mean(dx * hat, axis=-1, keepdims=True)
    )
    return part, jnp.sum(upstream * hat, axis=0, keepdims=True), hat


def split_three(column):
    one = column.astype(NARROW)
    rest = column - one.astype(SINGLE)
    two = rest.astype(NARROW)
    return [one, two, (rest - two.astype(SINGLE)).astype(NARROW)]


def extended(rows, column):
    return jnp.concatenate([rows] + split_three(-column), axis=1)


def with_units(rows):
    return jnp.concatenate([rows, jnp.ones((rows.shape[0], 3), rows.dtype)], axis=1)


def attend_back(q, k_units, k, v_units, lse, grad, mix, usable):
    scores = nt(k_units, extended(q, lse))
    if usable is not None:
        scores = jnp.where(usable, scores, MASKED)
    probs = jnp.exp(scores)
    inner = jnp.sum(grad.astype(SINGLE) * mix, axis=-1, keepdims=True)
    grad_scores = (probs * nt(v_units, extended(grad, inner))).astype(NARROW)
    return tn(grad_scores, k) * SCALE, mm(grad_scores, q), mm(probs.astype(NARROW), grad)


def cross_back_kernel(carried_ref, gtime_ref, sec3_ref, sec2_ref, cq_ref, cmix_ref, clse_ref,
                      kv_ref, usable_ref, text_ref, gains_ref, wtime_ref, wco_ref, wcq_ref,
                      carried_out_ref, pack_ref, gain_ref,
                      hat_s, back_s, dq_s, dkv_s, da_s, db_s, dw_s):
    gain_ref[...] = jnp.zeros((8, C), SINGLE)
    dkv_s[...] = jnp.zeros((TEXT, 2 * C), SINGLE)
    usable = jnp.broadcast_to(usable_ref[...], (TEXT, STEP)) == 1
    for r in range(STEPS):
        rows = slice(r * STEP, (r + 1) * STEP)
        part, gain, hat = ln_back_rows(sec3_ref[rows, :], gains_ref[4:5, :], nt(gtime_ref[rows, :], wtime_ref[...]))
        gain_ref[1:2, :] += gain
        hat_s[rows, :] = (hat * gains_ref[4:5, :]).astype(NARROW)
        carried = carried_ref[rows, :] + part
        back_s[rows, :] = carried.astype(NARROW)
        gmix = nt(back_s[rows, :], wco_ref[...]).astype(NARROW)
        for h in range(HEADS):
            lanes = slice(h * HEAD, (h + 1) * HEAD)
            lanes_v = slice(C + h * HEAD, C + (h + 1) * HEAD)
            k = kv_ref[:, lanes]
            dq, dk, dv = attend_back(
                cq_ref[rows, lanes] * jnp.bfloat16(SCALE), with_units(k), k, with_units(kv_ref[:, lanes_v]),
                clse_ref[rows, h : h + 1], gmix[:, lanes], cmix_ref[rows, lanes], usable,
            )
            dq_s[rows, lanes] = dq.astype(NARROW)
            dkv_s[:, lanes] += dk
            dkv_s[:, lanes_v] += dv
        part, gain, hat = ln_back_rows(sec2_ref[rows, :], gains_ref[3:4, :], nt(dq_s[rows, :], wcq_ref[...]))
        gain_ref[0:1, :] += gain
        carried_out_ref[rows, :] = carried + part
    da_s[...] = tn(hat_s[...], gtime_ref[...])
    db_s[...] = tn(cmix_ref[...].astype(NARROW), back_s[...])
    bands_out(pack_ref, 52, db_s, 20, 160)
    for r in range(STEPS):
        rows = slice(r * STEP, (r + 1) * STEP)
        hat, rstd = ln_rows(sec2_ref[rows, :], None)
        hat_s[rows, :] = (hat * gains_ref[3:4, :]).astype(NARROW)
    db_s[...] = tn(hat_s[...], dq_s[...])
    pair_out(pack_ref, 32, da_s, db_s)
    dw_s[...] = tn(text_ref[...], dkv_s[...].astype(NARROW))
    bands_out(pack_ref, 0, dw_s, 64, 320)


def cross_back(*args):
    low = ((PIX, C), NARROW)
    return kernel_call(
        cross_back_kernel,
        [((PIX, C), SINGLE), (packed_shape(64), NARROW), ((8, C), SINGLE)],
        [low, low, low, ((TEXT, 2 * C), SINGLE), ((C, 3 * C), SINGLE), ((C, C), SINGLE), ((CTX, 2 * C), SINGLE)],
        flops=26 * 10**9,
    )(*args)


def self_back_kernel(carried_ref, sec1_ref, proj_ref, mix_ref, lse_ref, gains_ref, wqkv_ref, wso_ref,
                     carried_out_ref, pack_ref, gain_ref,
                     back_s, gmix_s, dproj_s, hat_s, dk_s, dv_s, da_s, db_s):
    gain_ref[...] = jnp.zeros((8, C), SINGLE)
    for r in range(STEPS):
        rows = slice(r * STEP, (r + 1) * STEP)
        back_s[rows, :] = carried_ref[rows, :].astype(NARROW)
        gmix_s[rows, :] = nt(back_s[rows, :], wso_ref[...]).astype(NARROW)
    db_s[...] = tn(mix_ref[...].astype(NARROW), back_s[...])
    for h in range(HEADS):
        lanes = slice(h * HEAD, (h + 1) * HEAD)
        lanes_k = slice(C + h * HEAD, C + (h + 1) * HEAD)
        lanes_v = slice(2 * C + h * HEAD, 2 * C + (h + 1) * HEAD)
        k = proj_ref[:, lanes_k]
        k_units = with_units(k)
        v_units = with_units(proj_ref[:, lanes_v])
        for r in range(STEPS):
            rows = slice(r * STEP, (r + 1) * STEP)
            dq, dk, dv = attend_back(
                proj_ref[rows, lanes] * jnp.bfloat16(SCALE), k_units, k, v_units,
                lse_ref[rows, h : h + 1], gmix_s[rows, lanes], mix_ref[rows, lanes], None,
            )
            dproj_s[rows, lanes] = dq.astype(NARROW)
            if r == 0:
                dk_s[...] = dk
                dv_s[...] = dv
            else:
                dk_s[...] += dk
                dv_s[...] += dv
        dproj_s[:, lanes_k] = dk_s[...].astype(NARROW)
        dproj_s[:, lanes_v] = dv_s[...].astype(NARROW)
    for r in range(STEPS):
        rows = slice(r * STEP, (r + 1) * STEP)
        part, gain, hat = ln_back_rows(sec1_ref[rows, :], gains_ref[2:3, :], nt(dproj_s[rows, :], wqkv_ref[...]))
        gain_ref[0:1, :] += gain
        hat_s[rows, :] = (hat * gains_ref[2:3, :]).astype(NARROW)
        carried_out_ref[rows, :] = carried_ref[rows, :] + part
    da_s[...] = tn(hat_s[...], dproj_s[...])
    pair_out(pack_ref, 0, da_s, db_s)


def self_back_block(*args):
    low = ((PIX, C), NARROW)
    return kernel_call(
        self_back_kernel,
        [((PIX, C), SINGLE), (packed_shape(24), NARROW), ((8, C), SINGLE)],
        [low, low, ((PIX, 3 * C), NARROW), low, ((PIX, HEAD), SINGLE), ((PIX, HEAD), SINGLE),
         ((C, 3 * C), SINGLE), ((C, C), SINGLE)],
        flops=29 * 10**9,
    )(*args)


def feed_kernel(sec3_ref, mix_ref, cot_ref, gains_ref, wto_ref, wup_ref, wdown_ref,
                out_ref, carried_ref, gmix_ref, pack_ref, gain_ref,
                hat_s, act_s, lift_s, back_s, d_s, dw_s):
    gain_ref[...] = jnp.zeros((8, C), SINGLE)
    for r in range(STEPS):
        rows = slice(r * STEP, (r + 1) * STEP)
        sec4 = sec3_ref[rows, :] + mm(mix_ref[rows, :], wto_ref[...])
        hat, rstd = ln_rows(sec4, None)
        hat_s[rows, :] = (hat * gains_ref[5:6, :]).astype(NARROW)
        lifted = mm(hat_s[rows, :], wup_ref[...])
        cube = lifted * lifted
        inner = jnp.tanh(GELU_A * lifted * (1.0 + GELU_B * cube))
        gate = 0.5 + 0.5 * inner
        act_s[rows, :] = (lifted * gate).astype(NARROW)
        slope = gate + (0.5 * GELU_A) * lifted * (1.0 - inner * inner) * (1.0 + (3.0 * GELU_B) * cube)
        grad_act = nt(cot_ref[rows, :], wdown_ref[...])
        lift_s[rows, :] = (grad_act * slope).astype(NARROW)
        out_ref[rows, :] = (sec4 + mm(act_s[rows, :], wdown_ref[...])).astype(NARROW)
        part, gain, hat = ln_back_rows(sec4, gains_ref[5:6, :], nt(lift_s[rows, :], wup_ref[...]))
        gain_ref[0:1, :] += gain
        carried = cot_ref[rows, :].astype(SINGLE) + part
        carried_ref[rows, :] = carried
        back_s[rows, :] = carried.astype(NARROW)
        gmix_ref[rows, :] = nt(back_s[rows, :], wto_ref[...]).astype(NARROW)
    dw_s[...] = tn(hat_s[...], lift_s[...])
    bands_out(pack_ref, 0, dw_s, 20, 640)
    d_s[...] = tn(act_s[...], cot_ref[...])
    bands_out(pack_ref, 20, d_s, 80, 160)
    d_s[0:C, :] = tn(mix_ref[...], back_s[...])
    bands_out(pack_ref, 40, d_s, 20, 160)


def feed_block(*args):
    low = ((PIX, C), NARROW)
    wide = ((PIX, FF), NARROW)
    return kernel_call(
        feed_kernel,
        [low, ((PIX, C), SINGLE), low, (packed_shape(48), NARROW), ((8, C), SINGLE)],
        [low, wide, wide, low, ((FF, C), SINGLE), ((C, FF), SINGLE)],
        flops=20 * 10**9,
    )(*args)


def untile(tile):
    return tile.reshape(16, 8, tile.shape[-1])


def time_kernel(qkv_ref, bias_ref, low_ref, mix_ref, lse_ref, wide_s):
    wide_s[...] = qkv_ref[...].astype(SINGLE)
    for b in range(PIX // 16 // 8):
        tile = wide_s[:, 8 * b : 8 * b + 8, :].reshape(128, 3 * C).astype(NARROW)
        mixes = []
        for h in range(HEADS):
            q = tile[:, h * HEAD : (h + 1) * HEAD] * jnp.bfloat16(SCALE)
            k = tile[:, C + h * HEAD : C + (h + 1) * HEAD]
            v = with_ones(tile[:, 2 * C + h * HEAD : 2 * C + (h + 1) * HEAD])
            scores = nt(q, k) + bias_ref[h]
            highest = jnp.max(scores, axis=-1, keepdims=True)
            both = mm(jnp.exp(scores - highest).astype(NARROW), v)
            total = both[:, HEAD : HEAD + 1]
            mixes.append(both[:, :HEAD] / total)
            lse_ref[128 * b : 128 * b + 128, h : h + 1] = highest + jnp.log(total)
        mix_ref[:, 8 * b : 8 * b + 8, :] = untile(jnp.concatenate(mixes, axis=1))
    low_ref[...] = mix_ref[...].astype(NARROW)


def time_block(qkv, bias):
    rows = PIX // 16
    return kernel_call(
        time_kernel,
        [((16, rows, C), NARROW), ((16, rows, C), SINGLE), ((PIX, 8), SINGLE)],
        [((16, rows, 3 * C), SINGLE)],
        flops=15 * 10**9,
    )(qkv, bias)


def time_back_kernel(qkv_ref, bias_ref, mix_ref, lse_ref, grad_ref, dqkv_ref, dbias_ref, wide_s, grad_s, out_s):
    dbias_ref[...] = jnp.zeros((HEADS, 128, 128), SINGLE)
    wide_s[...] = qkv_ref[...].astype(SINGLE)
    grad_s[...] = grad_ref[...].astype(SINGLE)
    for b in range(PIX // 16 // 8):
        part = slice(8 * b, 8 * b + 8)
        tile = wide_s[:, part, :].reshape(128, 3 * C).astype(NARROW)
        grads = grad_s[:, part, :].reshape(128, C)
        inners = grads * mix_ref[:, part, :].reshape(128, C)
        grads = grads.astype(NARROW)
        dqs, dks, dvs = [], [], []
        for h in range(HEADS):
            lanes = slice(h * HEAD, (h + 1) * HEAD)
            q = tile[:, lanes] * jnp.bfloat16(SCALE)
            k = tile[:, C + h * HEAD : C + (h + 1) * HEAD]
            v = tile[:, 2 * C + h * HEAD : 2 * C + (h + 1) * HEAD]
            g = grads[:, lanes]
            lse = lse_ref[128 * b : 128 * b + 128, h : h + 1]
            probs = jnp.exp(nt(with_units(k), extended(q, lse)) + bias_ref[h])
            inner = jnp.sum(inners[:, lanes], axis=-1, keepdims=True)
            ds = (probs * nt(with_units(v), extended(g, inner))).astype(NARROW)
            dbias_ref[h] += ds.astype(SINGLE)
            dqs.append(tn(ds, k) * SCALE)
            dks.append(mm(ds, q))
            dvs.append(mm(probs.astype(NARROW), g))
        out_s[:, part, :] = untile(jnp.concatenate(dqs + dks + dvs, axis=1))
    dqkv_ref[...] = out_s[...].astype(NARROW)


def time_back_block(qkv, bias_t, mix, lse, grad):
    wide = ((16, PIX // 16, 3 * C), SINGLE)
    return kernel_call(
        time_back_kernel,
        [((16, PIX // 16, 3 * C), NARROW), ((HEADS, 128, 128), SINGLE)],
        [wide, ((16, PIX // 16, C), SINGLE), wide],
        flops=25 * 10**9,
    )(qkv, bias_t, mix, lse, grad)


def conv_back_rows(y_s, r):
    not_first, not_last = edge_masks(STEP)
    base = r * STEP
    sides = []
    for j in range(3):
        total = None
        for i in range(3):
            lanes = slice((3 * i + j) * C, (3 * i + j + 1) * C)
            part = y_s[pl.ds(base + IMG_W * (2 - i), STEP), lanes]
            total = part if total is None else total + part
        sides.append(total)
    from_next = jnp.where(not_last, pltpu.roll(sides[0], STEP - 1, 0), 0.0)
    from_prev = jnp.where(not_first, pltpu.roll(sides[2], 1, 0), 0.0)
    return from_next + sides[1] + from_prev


def conv_weight_grad(cols_ref, back_s, d_s):
    for i in range(3):
        d_s[3 * C * i : 3 * C * (i + 1), :] = tn(cols_ref[pl.ds(IMG_W * i, PIX), :], back_s[...])


def conv_input_products(back_s, w_ref, y_s):
    border = jnp.zeros((IMG_W, 9 * C), SINGLE)
    y_s[0:IMG_W, :] = border
    y_s[PIX + IMG_W :, :] = border
    for r in range(STEPS):
        y_s[pl.ds(IMG_W + r * STEP, STEP), :] = nt(back_s[r * STEP : (r + 1) * STEP, :], w_ref[...])


def silu_slope(pre):
    gate = 0.5 + 0.5 * jnp.tanh(0.5 * pre)
    return gate * (1.0 + pre * (1.0 - gate))


def second_weight_kernel(carried_ref, cols2_ref, upper_ref, pack_ref, back_ref, d_s):
    pack_ref[:, :, :, 0:24, :] = upper_ref[...]
    for r in range(STEPS):
        rows = slice(r * STEP, (r + 1) * STEP)
        back_ref[rows, :] = carried_ref[rows, :].astype(NARROW)
    conv_weight_grad(cols2_ref, back_ref, d_s)
    bands_out(pack_ref, 24, d_s, 180, 160)


def second_weight(carried, cols2, upper):
    return kernel_call(
        second_weight_kernel, [(packed_shape(72), NARROW), ((PIX, C), NARROW)], [((9 * C, C), SINGLE)],
        flops=9 * 10**9,
    )(carried, cols2, upper)


def second_back_kernel(back_s, conv_out_ref, stats_ref, film_ref, gains_ref, gmat_ref,
                       w2_ref, hidden_ref, back_ref, sums_ref, y_s):
    conv_input_products(back_s, w2_ref, y_s)
    scale = 1.0 + film_ref[0:1, :C]
    shift = film_ref[0:1, C:]
    center, spread, gain = stats_ref[2:3, :], stats_ref[3:4, :], gains_ref[1:2, :]
    zero = jnp.zeros((1, C), SINGLE)
    gain_sum, total, crossed = zero, zero, zero
    for r in range(STEPS):
        rows = slice(r * STEP, (r + 1) * STEP)
        normed = (conv_out_ref[rows, :] * scale + shift - center) * spread
        grad_pre = conv_back_rows(y_s, r) * silu_slope(normed * gain)
        gain_sum += jnp.sum(grad_pre * normed, axis=0, keepdims=True)
        grad = grad_pre * gain
        hidden_ref[rows, :] = grad
        total += jnp.sum(grad, axis=0, keepdims=True)
        crossed += jnp.sum(grad * normed, axis=0, keepdims=True)
    members = PIX * (C // GROUPS)
    total = grouped(total, gmat_ref[...]) / members
    crossed = grouped(crossed, gmat_ref[...]) / members
    film_one, film_two = zero, zero
    for r in range(STEPS):
        rows = slice(r * STEP, (r + 1) * STEP)
        conv_out = conv_out_ref[rows, :]
        normed = (conv_out * scale + shift - center) * spread
        hidden = spread * (hidden_ref[rows, :] - total - normed * crossed)
        film_one += jnp.sum(hidden * conv_out, axis=0, keepdims=True)
        film_two += jnp.sum(hidden, axis=0, keepdims=True)
        back_ref[rows, :] = (hidden * scale).astype(NARROW)
    sums_ref[...] = jnp.zeros((8, C), SINGLE)
    sums_ref[0:1, :] = gain_sum
    sums_ref[1:2, :] = film_one
    sums_ref[2:3, :] = film_two


def second_back(*args):
    return kernel_call(
        second_back_kernel,
        [((PIX, C), SINGLE), ((PIX, C), NARROW), ((8, C), SINGLE)],
        [((PIX + 2 * IMG_W, 9 * C), SINGLE)],
        flops=9 * 10**9,
    )(*args)


def first_weight_kernel(cols1_ref, back_ref, pack_ref, d_s):
    conv_weight_grad(cols1_ref, back_ref, d_s)
    bands_out(pack_ref, 0, d_s, 180, 160)


def first_weight(cols1, back):
    return kernel_call(
        first_weight_kernel, [(packed_shape(48), NARROW)], [((9 * C, C), SINGLE)], flops=9 * 10**9
    )(cols1, back)[0]


def small_kernel(half_ref, got_ref, own_ref, other_ref, small_ref):
    half = half_ref[0]

    def film(place):
        both = got_ref[:, place, :]
        return lax.dot_general(
            both[:, C : C + 80], both[:, :C], TN, precision=PRECISE, preferred_element_type=SINGLE
        )

    own_ref[...] = film(half)
    other_ref[...] = film(1 - half).astype(NARROW)
    total = got_ref[0]
    for s in range(1, 16):
        total += got_ref[s]
    small_ref[...] = total


def small_settle(temb, sums_d, sums_e, gain_a, gain_b, gain_c, grad_table, half_vec):
    grad_film = jnp.concatenate([sums_d[1:2], sums_d[2:3]]).reshape(1, 1, 2, 1, C)
    cut = temb[0].astype(SINGLE).reshape(2, 8, 1, 1, 80).transpose(1, 2, 0, 3, 4)
    factors = jnp.concatenate(
        [jnp.broadcast_to(grad_film.transpose(0, 2, 1, 3, 4), (8, 2, 2, 1, C)),
         jnp.broadcast_to(cut, (8, 2, 2, 1, 80)), jnp.zeros((8, 2, 2, 1, BAND - C - 80), SINGLE)],
        axis=-1,
    ).reshape(16, 2, BAND)
    table_row = jnp.pad(grad_table.reshape(1, -1), ((0, 0), (0, C - NB * HEADS)))
    rows = jnp.concatenate([sums_e[0:1], sums_d[0:1], gain_c[0:1], gain_b[0:2], gain_a[0:1], table_row])
    rows = jnp.broadcast_to(jnp.pad(rows, ((0, 0), (0, BAND - C))), (16, 7, BAND))
    pad = jnp.zeros((16, 7, BAND), SINGLE)
    got = lax.all_to_all(jnp.concatenate([factors, rows, pad], axis=1), CUBE, 0, 0, tiled=True)
    own, other, small = smem_call(
        small_kernel, 1, [((80, C), SINGLE), ((80, C), NARROW), ((16, BAND), SINGLE)], flops=2 * 10**9
    )(half_vec, got)
    swap = [(0, 1), (1, 0)]
    return own, lax.ppermute(other, HALF, swap), small + lax.ppermute(small, HALF, swap)


def finish_kernel(down, down_r, middle, middle_r, upper, upper_r, first, first_r,
                  film, film_r, *outs):
    w = Weights(*outs)
    total = down[...] + down_r[...].astype(SINGLE)
    bands_in(total, 0, w.feed_up, 20, 640)
    bands_in(total, 20, w.feed_down, 80, 160)
    bands_in(total, 40, w.time_output, 20, 160)
    total = middle[...] + middle_r[...].astype(SINGLE)
    bands_in(total, 0, w.cross_keyval, 64, 320)
    w.time_project[...] = total[32:52, 0:480]
    w.cross_query[...] = total[32:52, 480:640]
    bands_in(total, 52, w.cross_output, 20, 160)
    total = upper[...] + upper_r[...].astype(SINGLE)
    w.self_project[...] = total[0:20, 0:480]
    w.self_output[...] = total[0:20, 480:640]
    bands_in(total, 24, w.conv_second, 180, 160)
    bands_in(first[...] + first_r[...].astype(SINGLE), 0, w.conv_first, 180, 160)
    w.film_weight[...] = film[...] + film_r[...].astype(SINGLE)


def finish(*groups):
    shapes = Weights(
        conv_first=(180, 160), conv_second=(180, 160), film_weight=(80, C), self_project=(20, 480),
        self_output=(20, 160), cross_query=(20, 160), cross_keyval=(64, C), cross_output=(20, 160),
        time_project=(20, 480), time_output=(20, 160), feed_up=(20, BAND), feed_down=(80, 160),
    )
    return Weights(*kernel_call(finish_kernel, [(s, SINGLE) for s in shapes])(*groups))


def first_back_kernel(carried_ref, x_ref, stats_ref, gains_ref, gmat_ref, w1_ref, back_ref,
                      grad_ref, sums_ref, y_s, pre_s):
    conv_input_products(back_ref, w1_ref, y_s)
    center, spread, gain = stats_ref[0:1, :], stats_ref[1:2, :], gains_ref[0:1, :]
    zero = jnp.zeros((1, C), SINGLE)
    gain_sum, total, crossed = zero, zero, zero
    for r in range(STEPS):
        rows = slice(r * STEP, (r + 1) * STEP)
        normed = (x_ref[rows, :].astype(SINGLE) - center) * spread
        grad_pre = conv_back_rows(y_s, r) * silu_slope(normed * gain)
        gain_sum += jnp.sum(grad_pre * normed, axis=0, keepdims=True)
        grad = grad_pre * gain
        pre_s[rows, :] = grad
        total += jnp.sum(grad, axis=0, keepdims=True)
        crossed += jnp.sum(grad * normed, axis=0, keepdims=True)
    members = PIX * (C // GROUPS)
    total = grouped(total, gmat_ref[...]) / members
    crossed = grouped(crossed, gmat_ref[...]) / members
    for r in range(STEPS):
        rows = slice(r * STEP, (r + 1) * STEP)
        normed = (x_ref[rows, :].astype(SINGLE) - center) * spread
        grad = spread * (pre_s[rows, :] - total - normed * crossed)
        grad_ref[rows, :] = (carried_ref[rows, :] + grad).astype(NARROW)
    sums_ref[...] = jnp.zeros((8, C), SINGLE)
    sums_ref[0:1, :] = gain_sum


def first_back(*args):
    return kernel_call(
        first_back_kernel,
        [((PIX, C), NARROW), ((8, C), SINGLE)],
        [((PIX + 2 * IMG_W, 9 * C), SINGLE), ((PIX, C), SINGLE)],
        flops=11 * 10**9,
    )(*args)


BAND = 640
QUARTER = 160
PACK_ROWS = 272


def smem_call(body, n_in, outs, scratch=(), flops=10**9):
    specs = [pl.BlockSpec(memory_space=pltpu.SMEM)] + [pl.BlockSpec(memory_space=pltpu.VMEM)] * n_in
    return pl.pallas_call(
        body,
        in_specs=specs,
        out_shape=[jax.ShapeDtypeStruct(s, d) for s, d in outs],
        scratch_shapes=[pltpu.VMEM(s, d) for s, d in scratch],
        compiler_params=pltpu.CompilerParams(vmem_limit_bytes=VMEM_BYTES),
        cost_estimate=pl.CostEstimate(flops=flops, bytes_accessed=10**7, transcendentals=0),
    )


def side_by_side(out, at, ref, cols):
    parts = BAND // cols
    tall = ref.shape[0] // parts
    wide = ref[...].astype(SINGLE)
    out[at : at + tall, :] = jnp.concatenate(
        [wide[tall * q : tall * (q + 1), :] for q in range(parts)], axis=1
    ).astype(NARROW)


def pack_kernel(*refs):
    w = Weights(*refs[:12])
    out = refs[12]
    out[...] = jnp.zeros((PACK_ROWS, BAND), NARROW)
    side_by_side(out, 0, w.conv_first, 160)
    side_by_side(out, 48, w.conv_second, 160)
    side_by_side(out, 96, w.film_weight, 320)
    side_by_side(out, 136, w.cross_keyval, 320)
    out[168:188, 0:480] = w.self_project[...]
    out[168:188, 480:640] = w.self_output[...]
    out[192:212, 0:480] = w.time_project[...]
    out[192:212, 480:640] = w.time_output[...]
    out[216:236, :] = w.feed_up[...]
    side_by_side(out, 240, w.feed_down, 160)
    side_by_side(out, 260, w.cross_query, 160)
    side_by_side(out, 265, w.cross_output, 160)


def pack_weights(w):
    return kernel_call(pack_kernel, [((PACK_ROWS, BAND), NARROW)])(*w)[0]


def unpack_kernel(half_ref, full_ref, *outs):
    w = Weights(*outs)
    half = half_ref[0]
    unpack_tall(half, full_ref, w.conv_first, 0, 180, 160)
    unpack_tall(half, full_ref, w.conv_second, 48, 180, 160)
    unpack_tall(half, full_ref, w.film_weight, 96, 80, 320)
    unpack_tall(half, full_ref, w.cross_keyval, 136, 64, 320)
    unpack_tall(half, full_ref, w.feed_up, 216, 20, 640)
    unpack_tall(half, full_ref, w.feed_down, 240, 80, 160)
    unpack_tall(half, full_ref, w.cross_query, 260, 20, 160)
    unpack_tall(half, full_ref, w.cross_output, 265, 20, 160)
    for out, at, c0, cols in (
        (w.self_project, 168, 0, 480), (w.self_output, 168, 480, 160),
        (w.time_project, 192, 0, 480), (w.time_output, 192, 480, 160),
    ):
        for quad in range(4):
            parts = []
            for f in range(4 * quad, 4 * quad + 4):
                place = half if f < 8 else 1 - half
                parts.append(jnp.concatenate(
                    [full_ref[2 * (f % 8) + s, place, at : at + 20, c0 : c0 + cols].astype(SINGLE) for s in range(2)],
                    axis=1,
                ))
            out[80 * quad : 80 * (quad + 1), :] = jnp.concatenate(parts, axis=0).astype(NARROW)


def unpack_weights(half_vec, full):
    shapes = [
        (9 * C, C), (9 * C, C), (TEMB, 2 * C), (C, 3 * C), (C, C), (C, C), (CTX, 2 * C), (C, C), (C, 3 * C),
        (C, C), (C, FF), (FF, C),
    ]
    out = smem_call(unpack_kernel, 1, [(s, NARROW) for s in shapes], flops=10 * 10**9)(half_vec, full)
    return Weights(*out)


def packed_shape(rows):
    return (2, 8, 2, rows, BAND)


def bands_out(out_ref, at, grad_ref, rows, cols):
    parts = BAND // cols
    tall = rows // parts
    for f in range(16):
        for s in range(2):
            lanes = slice(s * cols, (s + 1) * cols)
            pieces = [
                grad_ref[rows * f + tall * q : rows * f + tall * (q + 1), lanes] for q in range(parts)
            ]
            piece = pieces[0] if parts == 1 else jnp.concatenate(pieces, axis=1)
            out_ref[f % 2, 2 * (f % 8 // 2) + s, f // 8, at : at + tall, :] = piece.astype(NARROW)


def pair_out(out_ref, at, wide_ref, thin_ref):
    for f in range(16):
        for s in range(2):
            piece = jnp.concatenate(
                [wide_ref[20 * f : 20 * f + 20, 480 * s : 480 * s + 480],
                 thin_ref[20 * f : 20 * f + 20, 160 * s : 160 * s + 160]],
                axis=1,
            )
            out_ref[f % 2, 2 * (f % 8 // 2) + s, f // 8, at : at + 20, :] = piece.astype(NARROW)


def bands_in(total, at, out_ref, rows, cols):
    parts = BAND // cols
    tall = rows // parts
    for q in range(parts):
        out_ref[tall * q : tall * (q + 1), :] = total[at : at + tall, cols * q : cols * (q + 1)]


def reduce_kernel(half_ref, got_ref, own_ref, other_ref):
    half = half_ref[0]
    own = got_ref[0, half].astype(SINGLE)
    other = got_ref[0, 1 - half].astype(SINGLE)
    for s in range(1, 8):
        own += got_ref[s, half].astype(SINGLE)
        other += got_ref[s, 1 - half].astype(SINGLE)
    own_ref[...] = own
    other_ref[...] = other.astype(NARROW)


def chip_sum(packed, core):
    got = lax.ppermute(pick(1 - core, packed), CORE, [(0, 1), (1, 0)])
    return (pick(core, packed).astype(SINGLE) + got.astype(SINGLE)).astype(NARROW)


def chip_swap(chip):
    return lax.all_to_all(chip, CHIPS, 0, 0, tiled=True)


def reduce_half(got, half_vec):
    shape = got.shape[2:]
    own, other = smem_call(reduce_kernel, 1, [(shape, SINGLE), (shape, NARROW)], flops=2 * 10**9)(half_vec, got)
    return own, lax.ppermute(other, HALF, [(0, 1), (1, 0)])


def time_setup(video_mask, video_number, bucket_index, bias_table, half):
    order = jnp.array([8 * (g % 2) + g // 2 for g in range(16)])
    live = pick(half, video_mask)
    number = pick(half, video_number)
    same = (live[:, None] == 1) & (live[None, :] == 1) & (number[:, None] == number[None, :])
    same = same | (jnp.arange(16)[:, None] == jnp.arange(16)[None, :])
    bucket = bucket_index[order][:, order]
    one_hot = (bucket.reshape(-1, 1) == jnp.arange(NB)[None, :]).astype(SINGLE)
    table = jnp.dot(one_hot, bias_table, precision=PRECISE).reshape(16, 16, HEADS).transpose(2, 0, 1)
    small = jnp.where(same[order][:, order][None], table, MASKED)
    pixel = jnp.arange(8)
    wide = jnp.where(
        (pixel[:, None] == pixel[None, :])[None, None, :, None, :], small[:, :, None, :, None], MASKED
    )
    return wide.reshape(HEADS, 128, 128), one_hot


def swap_frames(block, rows):
    return lax.all_to_all(block.reshape(16, rows, block.shape[-1]), CUBE, 0, 0, tiled=True)


def fast_shards(
    video_in, time_embed, text_embed, text_mask, video_mask, video_number, bucket_index,
    norm_gains, bias_table, conv_first, conv_second, film_weight, self_project, self_output,
    cross_query, cross_keyval, cross_output, time_project, time_output, feed_up, feed_down,
    cotangent,
):
    half = lax.axis_index(HALF)
    space = lax.axis_index(SPACE)
    core = lax.axis_index(CORE)
    gains = norm_gains.T
    half_vec = jnp.full((1,), half, jnp.int32)
    packed = pack_weights(Weights(
        conv_first=conv_first, conv_second=conv_second, film_weight=film_weight,
        self_project=self_project, self_output=self_output, cross_query=cross_query,
        cross_keyval=cross_keyval, cross_output=cross_output, time_project=time_project,
        time_output=time_output, feed_up=feed_up, feed_down=feed_down,
    ))
    other = lax.ppermute(packed, HALF, [(0, 1), (1, 0)])
    full = lax.all_gather(jnp.stack([packed, other]), CUBE, axis=0, tiled=False)
    video_in, other = lax.optimization_barrier((video_in, other))
    x = to_slot(video_in.reshape(FR_DEV, -1, C), half, space)
    text_embed, cotangent, full = lax.optimization_barrier((text_embed, cotangent, full))
    w = unpack_weights(half_vec, full)
    cot = to_slot(cotangent.reshape(FR_DEV, -1, C), half, space)
    text = to_slot(text_embed.reshape(FR_DEV, -1, CTX), half, space)
    temb = meta_slot(time_embed.reshape(FR_DEV, 1, TEMB), space)
    usable = meta_slot(text_mask.reshape(FR_DEV, 1, TEXT), space)[0] == 1
    temb_act = jax.nn.silu(temb.astype(SINGLE)).astype(NARROW)
    bias, one_hot = time_setup(video_mask, video_number, bucket_index, bias_table, half)
    gmat = group_matrix()

    temb_act = jnp.broadcast_to(temb_act, (8, TEMB))
    conv_out, sec1, cols1, cols2, stats, film = conv_block(
        x, w.conv_first, w.conv_second, temb_act, w.film_weight, gains, gmat
    )
    proj, mix, lse, sec2, text_kv, cq, cmix, clse, sec3, time_proj = attn_block(
        sec1, gains, w.self_project, w.self_output, text, usable[None, :], w.cross_keyval,
        w.cross_query, w.cross_output, w.time_project,
    )
    time_qkv = swap_frames(time_proj, PIX // 16)
    time_low, time_mix_t, time_lse = time_block(time_qkv, bias)
    time_mix = swap_frames(time_low, PIX // 16).reshape(PIX, C)
    result, carried, grad_time_mix, packed, gain_a = feed_block(
        sec3, time_mix, cot, gains, w.time_output, w.feed_up, w.feed_down
    )
    grad_mix_t = swap_frames(grad_time_mix, PIX // 16)
    packed, result, grad_mix_t = lax.optimization_barrier((packed, result, grad_mix_t))
    chip_down = chip_sum(packed, core)
    chip_down, grad_mix_t = lax.optimization_barrier((chip_down, grad_mix_t))
    down = chip_swap(chip_down)
    grad_qkv_t, bias_grad = time_back_block(time_qkv, bias.transpose(0, 2, 1), time_mix_t, time_lse, grad_mix_t)
    grad_qkv_t, down = lax.optimization_barrier((grad_qkv_t, down))
    grad_time_proj = swap_frames(grad_qkv_t, PIX // 16).reshape(PIX, 3 * C)
    grad_time_proj, result, down = lax.optimization_barrier((grad_time_proj, result, down))
    block_out = from_slot(result, half, space).reshape(video_in.shape)
    small = jnp.sum(bias_grad.reshape(HEADS, 16, 8, 16, 8), axis=(2, 4)).transpose(2, 1, 0)
    grad_table = jnp.dot(one_hot.T, small.reshape(-1, HEADS), precision=PRECISE)
    carried, packed, gain_b = cross_back(
        carried, grad_time_proj, sec3, sec2, cq, cmix, clse, text_kv, usable[:, None], text, gains,
        w.time_project, w.cross_output, w.cross_query,
    )
    carried, packed, block_out, down, grad_table = lax.optimization_barrier(
        (carried, packed, block_out, down, grad_table)
    )
    down = reduce_half(down, half_vec)
    chip_middle = chip_sum(packed, core)
    carried, chip_middle = lax.optimization_barrier((carried, chip_middle))
    middle = chip_swap(chip_middle)
    carried, packed, gain_c = self_back_block(
        carried, sec1, proj, mix, lse, gains, w.self_project, w.self_output
    )
    packed, back_second = second_weight(carried, cols2, packed)
    back_second, middle, packed = lax.optimization_barrier((back_second, middle, packed))
    middle = reduce_half(middle, half_vec)
    chip_upper = chip_sum(packed, core)
    _, back_first, sums_d = second_back(
        back_second, conv_out, stats, film, gains, gmat, w.conv_second
    )
    back_first, chip_upper, sums_d = lax.optimization_barrier((back_first, chip_upper, sums_d))
    upper = chip_swap(chip_upper)
    packed = first_weight(cols1, back_first)
    chip_first = chip_sum(packed, core)
    back_first, chip_first = lax.optimization_barrier((back_first, chip_first))
    first = chip_swap(chip_first)
    grad_x, sums_e = first_back(carried, x, stats, gains, gmat, w.conv_first, back_first)
    input_grad = from_slot(grad_x, half, space).reshape(video_in.shape)
    film_own, film_got, small = small_settle(
        temb_act, sums_d, sums_e, gain_a, gain_b, gain_c, grad_table, half_vec
    )
    upper = reduce_half(upper, half_vec)
    first = reduce_half(first, half_vec)
    gain_sum = small[2:8, :C].T
    out = finish(*down, *middle, *upper, *first, film_own, film_got)
    return (
        block_out, input_grad, gain_sum, small[8, : NB * HEADS].reshape(NB, HEADS),
        out.conv_first, out.conv_second, out.film_weight, out.self_project, out.self_output,
        out.cross_query, out.cross_keyval, out.cross_output, out.time_project, out.time_output,
        out.feed_up, out.feed_down,
    )


def fast_solution(mesh):
    split = Mesh(mesh.devices.reshape(2, 4, 2, 2), WORLD)
    frames = (HALF, QUAD, CORE)
    image = P(None, frames, SPACE, None, None)
    weight = P(frames, SPACE)
    placed = (
        image, P(None, frames, None), P(None, frames, SPACE, None), P(None, frames, None),
        P(), P(), P(), P(), P(),
    ) + (weight,) * 12 + (image,)
    return jax.shard_map(
        fast_shards, mesh=split, in_specs=placed,
        out_specs=(image, image, P(), P()) + (weight,) * 12, check_vma=False,
    )


def solution(mesh):
    if mesh.shape[FRAME] == GROUP_LEN and mesh.shape[SPACE] == FR_DEV:
        return fast_solution(mesh)
    placed = (
        P(None, FRAME, SPACE, None, None),
        P(None, FRAME, None),
        P(None, FRAME, SPACE, None),
        P(None, FRAME, None),
        P(),
        P(),
        P(),
        P(),
        P(),
        P(FRAME, SPACE),
        P(FRAME, SPACE),
        P(FRAME, SPACE),
        P(FRAME, SPACE),
        P(FRAME, SPACE),
        P(FRAME, SPACE),
        P(FRAME, SPACE),
        P(FRAME, SPACE),
        P(FRAME, SPACE),
        P(FRAME, SPACE),
        P(FRAME, SPACE),
        P(FRAME, SPACE),
        P(None, FRAME, SPACE, None, None),
    )
    return jax.shard_map(
        shards,
        mesh=mesh,
        in_specs=placed,
        out_specs=(
            P(None, FRAME, SPACE, None, None),
            P(None, FRAME, SPACE, None, None),
            P(),
            P(),
            P(FRAME, SPACE),
            P(FRAME, SPACE),
            P(FRAME, SPACE),
            P(FRAME, SPACE),
            P(FRAME, SPACE),
            P(FRAME, SPACE),
            P(FRAME, SPACE),
            P(FRAME, SPACE),
            P(FRAME, SPACE),
            P(FRAME, SPACE),
            P(FRAME, SPACE),
            P(FRAME, SPACE),
        ),
        check_vma=False,
    )
```

```python
from typing import Any, NamedTuple

import jax
import jax.numpy as jnp
from jax import lax
from jax.experimental import pallas as pl
from jax.experimental.pallas import tpu as pltpu
from jax.sharding import Mesh
from jax.sharding import PartitionSpec as P

C = 320
HEADS = 5
HEAD = 64
GROUPS = 32
CTX = 1024
TEMB = 1280
TEXT = 128
IMG_H = 24
IMG_W = 48
FR_DEV = 2
GROUP_LEN = 16
NB = 32
FF = 1280
GELU_A = 0.7978845608028654
GELU_B = 0.044715


FRAME = "frame"
SPACE = "space"
HALF = "half"
QUAD = "quad"
CORE = "core"
EPSILON = 1e-05
MASKED = -1e30
SINGLE = jnp.float32
NARROW = jnp.bfloat16
PRECISE = lax.Precision.HIGHEST


def with_halo(block, sides, width):
    for axis, dim in sides:
        count = lax.axis_size(axis)
        forward = [(i, i + 1) for i in range(count - 1)]
        backward = [(target, source) for source, target in forward]
        low = lax.ppermute(
            lax.slice_in_dim(block, block.shape[dim] - width, None, axis=dim), axis, forward
        )
        high = lax.ppermute(lax.slice_in_dim(block, 0, width, axis=dim), axis, backward)
        block = jnp.concatenate([low, block, high], axis=dim)
    return block


def collect(item_one, item_two, item_three):
    row_full = (
        lax.all_gather(item_one, FRAME, axis=0, tiled=True),
        lax.all_gather(item_two, FRAME, axis=0, tiled=True),
        lax.all_gather(item_three, FRAME, axis=0, tiled=True),
    )
    return (
        lax.all_gather(row_full[0], SPACE, axis=1, tiled=True),
        lax.all_gather(row_full[1], SPACE, axis=1, tiled=True),
        lax.all_gather(row_full[2], SPACE, axis=1, tiled=True),
    )


def settle(item_one, item_two, item_three):
    column_sums = (
        lax.psum_scatter(
            item_one.astype(jnp.bfloat16), SPACE, scatter_dimension=1, tiled=True
        ).astype(jnp.float32),
        lax.psum_scatter(
            item_two.astype(jnp.bfloat16), SPACE, scatter_dimension=1, tiled=True
        ).astype(jnp.float32),
        lax.psum_scatter(
            item_three.astype(jnp.bfloat16), SPACE, scatter_dimension=1, tiled=True
        ).astype(jnp.float32),
    )
    return (
        lax.psum_scatter(
            column_sums[0].astype(jnp.bfloat16), FRAME, scatter_dimension=0, tiled=True
        ).astype(jnp.float32),
        lax.psum_scatter(
            column_sums[1].astype(jnp.bfloat16), FRAME, scatter_dimension=0, tiled=True
        ).astype(jnp.float32),
        lax.psum_scatter(
            column_sums[2].astype(jnp.bfloat16), FRAME, scatter_dimension=0, tiled=True
        ).astype(jnp.float32),
    )


def space_sums(item_one, item_two):
    return lax.psum((item_one, item_two), SPACE)


def columns_of(padded):
    height_here = padded.shape[1] - 2
    pieces = [
        padded[:, row_off : row_off + height_here, col_off : col_off + IMG_W, :]
        for row_off in range(3)
        for col_off in range(3)
    ]
    return jnp.concatenate(pieces, axis=-1).reshape(-1, 9 * C)


def convolve(activation, weight):
    slot_count, rows_here = (activation.shape[0], activation.shape[1])
    image = activation.reshape(slot_count, rows_here // IMG_W, IMG_W, C)
    rimmed = with_halo(image, ((SPACE, 1),), 1)
    padded = jnp.pad(rimmed, ((0, 0), (0, 0), (1, 1), (0, 0)))
    summed = jnp.dot(columns_of(padded), weight, preferred_element_type=SINGLE)
    return (summed.reshape(slot_count, rows_here, C), padded)


def convolve_back(grad_low, weight):
    flipped = weight.reshape(3, 3, C, C)[::-1, ::-1].transpose(0, 1, 3, 2).reshape(9 * C, C)
    summed, padded = convolve(grad_low, flipped)
    return summed


def weight_grad(left, right):
    return lax.dot_general(
        left.reshape(-1, left.shape[-1]),
        right.reshape(-1, right.shape[-1]),
        (((0,), (0,)), ((), ())),
        preferred_element_type=SINGLE,
    )


def back_project(grad_low, weight):
    return jnp.einsum("...o,io->...i", grad_low, weight, preferred_element_type=SINGLE)


def layer_norm(layer, gain):
    centered = layer - jnp.mean(layer, axis=-1, keepdims=True)
    return (
        centered * lax.rsqrt(jnp.mean(centered * centered, axis=-1, keepdims=True) + EPSILON) * gain
    )


def group_forward(layer):
    slot_count, rows_here = (layer.shape[0], layer.shape[1])
    grouped = layer.reshape(slot_count, rows_here, GROUPS, C // GROUPS)
    summed, squares = space_sums(
        jnp.sum(grouped, axis=(1, 3)), jnp.sum(grouped * grouped, axis=(1, 3))
    )
    members = IMG_H * IMG_W * (C // GROUPS)
    center = summed / members
    spread = lax.rsqrt(squares / members - center * center + EPSILON)
    normed = (grouped - center[:, None, :, None]) * spread[:, None, :, None]
    return (normed.reshape(slot_count, rows_here, C), spread)


def group_backward(normed, spread, upstream):
    slot_count, rows_here = (normed.shape[0], normed.shape[1])
    grad_groups = upstream.reshape(slot_count, rows_here, GROUPS, C // GROUPS)
    norm_groups = normed.reshape(slot_count, rows_here, GROUPS, C // GROUPS)
    summed, crossed = space_sums(
        jnp.sum(grad_groups, axis=(1, 3)), jnp.sum(grad_groups * norm_groups, axis=(1, 3))
    )
    members = IMG_H * IMG_W * (C // GROUPS)
    result = spread[:, None, :, None] * (
        grad_groups
        - summed[:, None, :, None] / members
        - norm_groups * crossed[:, None, :, None] / members
    )
    return result.reshape(slot_count, rows_here, C)


def masked_scores(queries, key_rows, usable):
    scores = jnp.einsum(
        "qhd,khd->hqk", queries, key_rows, preferred_element_type=SINGLE
    ) * HEAD ** (-0.5)
    return jnp.where(usable[None, None, :], scores, MASKED)


def attend_forward(queries, key_rows, value_rows, usable):
    scores = masked_scores(queries, key_rows, usable)
    highest = jnp.max(scores, axis=-1, keepdims=True)
    log_total = highest + jnp.log(jnp.sum(jnp.exp(scores - highest), axis=-1, keepdims=True))
    attn_probs = jnp.exp(scores - log_total).astype(NARROW)
    mixture = jnp.einsum(
        "hqk,khd->qhd", attn_probs, value_rows, preferred_element_type=SINGLE
    ).astype(NARROW)
    return (mixture, log_total[..., 0])


def attend_backward(queries, key_rows, value_rows, usable, log_total, grad_mixture):
    scores = masked_scores(queries, key_rows, usable)
    attn_probs = jnp.exp(scores - log_total[..., None])
    grad_probs = jnp.einsum("qhd,khd->hqk", grad_mixture, value_rows, preferred_element_type=SINGLE)
    row_inner = jnp.sum(grad_probs * attn_probs, axis=-1, keepdims=True)
    grad_scores = (attn_probs * (grad_probs - row_inner)).astype(NARROW)
    grad_queries = jnp.einsum(
        "hqk,khd->qhd", grad_scores, key_rows, preferred_element_type=SINGLE
    ) * HEAD ** (-0.5)
    grad_keys = jnp.einsum(
        "hqk,qhd->khd", grad_scores, queries, preferred_element_type=SINGLE
    ) * HEAD ** (-0.5)
    grad_values = jnp.einsum(
        "hqk,qhd->khd", attn_probs.astype(NARROW), grad_mixture, preferred_element_type=SINGLE
    )
    return (grad_queries, grad_keys, grad_values)


def time_scores(queries, gathered, time_bias, allowed):
    key_rows = gathered[..., :C].reshape(gathered.shape[0], gathered.shape[1], HEADS, HEAD)
    scores = (
        jnp.einsum("rhd,grhd->rhg", queries, key_rows, preferred_element_type=SINGLE)
        * HEAD ** (-0.5)
        + time_bias[None]
    )
    return (jnp.where(allowed[None, None, :], scores, MASKED), key_rows)


def shards(
    video_in,
    time_embed,
    text_embed,
    text_mask,
    video_mask,
    video_number,
    bucket_index,
    norm_gains,
    bias_table,
    conv_first,
    conv_second,
    film_weight,
    self_project,
    self_output,
    cross_query,
    cross_keyval,
    cross_output,
    time_project,
    time_output,
    feed_up,
    feed_down,
    cotangent,
):
    height_here = video_in.shape[2]
    rows_here = height_here * IMG_W
    text_here = text_embed.shape[2]
    frame_count = video_mask.shape[1]
    frame_index = lax.axis_index(FRAME)
    group_place = frame_index % GROUP_LEN
    heads_view = (FR_DEV, rows_here, HEADS, HEAD)
    every_key = jnp.ones((IMG_H * IMG_W,), jnp.bool_)
    frame_ids = jnp.arange(frame_count)
    place_ids = jnp.arange(GROUP_LEN)
    bucket_row = jnp.sum(jnp.where((place_ids == group_place)[:, None], bucket_index, 0), axis=0)
    key_buckets = jnp.sum(
        jnp.where((frame_ids % GROUP_LEN)[:, None] == place_ids[None, :], bucket_row[None, :], 0),
        axis=1,
    )
    key_table = (key_buckets[:, None] == jnp.arange(NB)[None, :]).astype(SINGLE)
    time_bias = jnp.dot(key_table, bias_table, precision=PRECISE, preferred_element_type=SINGLE).T

    def allowed_for(live_slot, number_slot):
        chooser = frame_ids[:, None] == frame_ids[None, :]
        live_keys = jnp.sum(jnp.where(chooser, live_slot[None, :], 0), axis=1)
        number_keys = jnp.sum(jnp.where(chooser, number_slot[None, :], 0), axis=1)
        own_frame = frame_ids == frame_index
        live_own = jnp.sum(jnp.where(own_frame, live_slot, 0))
        number_own = jnp.sum(jnp.where(own_frame, number_slot, 0))
        same_group = frame_ids // GROUP_LEN == frame_index // GROUP_LEN
        together = (live_keys == 1) & (live_own == 1) & (number_keys == number_own)
        return same_group & (together | (frame_ids == frame_index))

    def spread_keys(own_pair):
        return lax.all_gather(own_pair, FRAME, axis=0, tiled=True)

    def return_keys(spread_grads):
        return lax.psum_scatter(
            spread_grads.astype(jnp.bfloat16), FRAME, scatter_dimension=0, tiled=True
        ).astype(jnp.float32)

    def gather_keys(frame_pair, text_pair):
        return (
            lax.all_gather(frame_pair, SPACE, axis=0, tiled=True),
            lax.all_gather(text_pair, SPACE, axis=0, tiled=True),
        )

    def scatter_keys(frame_grads, text_grads):
        return (
            lax.psum_scatter(
                frame_grads.astype(jnp.bfloat16), SPACE, scatter_dimension=0, tiled=True
            ).astype(jnp.float32),
            lax.psum_scatter(
                text_grads.astype(jnp.bfloat16), SPACE, scatter_dimension=0, tiled=True
            ).astype(jnp.float32),
        )

    resid = video_in.reshape(FR_DEV, rows_here, C).astype(SINGLE)
    conv_one, film_full, conv_two = collect(conv_first, film_weight, conv_second)
    temb_act = jax.nn.silu(time_embed.reshape(FR_DEV, TEMB).astype(SINGLE)).astype(NARROW)
    film_all = jnp.dot(temb_act, film_full, preferred_element_type=SINGLE)
    film_scale = 1.0 + film_all[:, None, :C]
    film_shift = film_all[:, None, C:]
    normed_one, spread_one = group_forward(resid)
    pre_one = normed_one * norm_gains[:, 0]
    conv_out, pad_one = convolve(jax.nn.silu(pre_one).astype(NARROW), conv_one)
    hidden = conv_out * film_scale + film_shift
    normed_two, spread_two = group_forward(hidden)
    pre_two = normed_two * norm_gains[:, 1]
    branch_two, pad_two = convolve(jax.nn.silu(pre_two).astype(NARROW), conv_two)
    section_one = resid + branch_two
    kv_weight, qkv_weight, self_weight = collect(cross_keyval, self_project, self_output)
    text_kv = (
        jnp.dot(
            text_embed.reshape(FR_DEV * text_here, CTX), kv_weight, preferred_element_type=SINGLE
        )
        .astype(NARROW)
        .reshape(FR_DEV, text_here, 2 * C)
    )
    self_in = layer_norm(section_one, norm_gains[:, 2]).astype(NARROW)
    self_proj = jnp.dot(self_in, qkv_weight, preferred_element_type=SINGLE).astype(NARROW)

    def self_slot(inputs):
        proj_slot, text_slot = inputs
        frame_kv, text_full = gather_keys(proj_slot[:, C:], text_slot)
        mixture, log_total = attend_forward(
            proj_slot[:, :C].reshape(rows_here, HEADS, HEAD),
            frame_kv[:, :C].reshape(-1, HEADS, HEAD),
            frame_kv[:, C:].reshape(-1, HEADS, HEAD),
            every_key,
        )
        return (mixture, log_total, text_full)

    self_mixed, self_lse, text_all = lax.map(self_slot, (self_proj, text_kv))
    self_mixed = self_mixed.reshape(FR_DEV, rows_here, C)
    section_two = section_one + jnp.dot(self_mixed, self_weight, preferred_element_type=SINGLE)
    query_weight, cross_weight, time_weight = collect(cross_query, cross_output, time_project)
    cross_in = layer_norm(section_two, norm_gains[:, 3]).astype(NARROW)
    cross_queries = (
        jnp.dot(cross_in, query_weight, preferred_element_type=SINGLE)
        .astype(NARROW)
        .reshape(heads_view)
    )
    text_usable = text_mask.reshape(FR_DEV, TEXT) == 1
    text_keys = text_all[..., :C].reshape(FR_DEV, TEXT, HEADS, HEAD)
    text_values = text_all[..., C:].reshape(FR_DEV, TEXT, HEADS, HEAD)
    cross_mixed, cross_lse = jax.vmap(attend_forward)(
        cross_queries, text_keys, text_values, text_usable
    )
    cross_mixed = cross_mixed.reshape(FR_DEV, rows_here, C)
    section_three = section_two + jnp.dot(cross_mixed, cross_weight, preferred_element_type=SINGLE)
    time_in = layer_norm(section_three, norm_gains[:, 4]).astype(NARROW)
    time_proj = jnp.dot(time_in, time_weight, preferred_element_type=SINGLE).astype(NARROW)

    def time_slot(inputs):
        proj_slot, live_slot, number_slot = inputs
        gathered = spread_keys(proj_slot[None, :, C:])
        queries = proj_slot[:, :C].reshape(rows_here, HEADS, HEAD)
        scores, key_rows = time_scores(
            queries, gathered, time_bias, allowed_for(live_slot, number_slot)
        )
        value_rows = gathered[..., C:].reshape(key_rows.shape)
        highest = jnp.max(scores, axis=-1, keepdims=True)
        log_total = highest + jnp.log(jnp.sum(jnp.exp(scores - highest), axis=-1, keepdims=True))
        attn_probs = jnp.exp(scores - log_total).astype(NARROW)
        mixture = jnp.einsum(
            "rhg,grhd->rhd", attn_probs, value_rows, preferred_element_type=SINGLE
        ).astype(NARROW)
        return (mixture, log_total[..., 0])

    time_mixed, time_lse = lax.map(time_slot, (time_proj, video_mask, video_number))
    time_mixed = time_mixed.reshape(FR_DEV, rows_here, C)
    out_weight, inner_weight, outer_weight = collect(time_output, feed_up, feed_down)
    section_four = section_three + jnp.dot(time_mixed, out_weight, preferred_element_type=SINGLE)
    feed_in = layer_norm(section_four, norm_gains[:, 5]).astype(NARROW)
    lifted = jnp.dot(feed_in, inner_weight, preferred_element_type=SINGLE)
    activated = jax.nn.gelu(lifted, approximate=True).astype(NARROW)
    result = section_four + jnp.dot(activated, outer_weight, preferred_element_type=SINGLE)
    block_out = result.astype(NARROW).reshape(video_in.shape)
    carried = cotangent.reshape(FR_DEV, rows_here, C).astype(SINGLE)
    back_feed = carried.astype(NARROW)
    grad_down = weight_grad(activated, back_feed)
    grad_act = back_project(back_feed, outer_weight)
    value_gelu, pull_gelu = jax.vjp(lambda layer: jax.nn.gelu(layer, approximate=True), lifted)
    grad_lifted = pull_gelu(grad_act)[0].astype(NARROW)
    grad_up = weight_grad(feed_in, grad_lifted)
    value_norm, pull_norm = jax.vjp(layer_norm, section_four, norm_gains[:, 5])
    norm_part, gain_five = pull_norm(back_project(grad_lifted, inner_weight))
    carried = carried + norm_part
    back_time = carried.astype(NARROW)
    grad_time_out = weight_grad(time_mixed, back_time)
    grad_time_mixed = back_project(back_time, out_weight).astype(NARROW).reshape(heads_view)
    down_grads = settle(grad_time_out, grad_up, grad_down)

    def time_back(inputs):
        proj_slot, live_slot, number_slot, lse_slot, grad_slot = inputs
        gathered = spread_keys(proj_slot[None, :, C:])
        queries = proj_slot[:, :C].reshape(rows_here, HEADS, HEAD)
        scores, key_rows = time_scores(
            queries, gathered, time_bias, allowed_for(live_slot, number_slot)
        )
        value_rows = gathered[..., C:].reshape(key_rows.shape)
        attn_probs = jnp.exp(scores - lse_slot[..., None])
        grad_probs = jnp.einsum(
            "rhd,grhd->rhg", grad_slot, value_rows, preferred_element_type=SINGLE
        )
        row_inner = jnp.sum(grad_probs * attn_probs, axis=-1, keepdims=True)
        grad_scores = (attn_probs * (grad_probs - row_inner)).astype(NARROW)
        grad_queries = jnp.einsum(
            "rhg,grhd->rhd", grad_scores, key_rows, preferred_element_type=SINGLE
        ) * HEAD ** (-0.5)
        grad_keys = jnp.einsum(
            "rhg,rhd->grhd", grad_scores, queries, preferred_element_type=SINGLE
        ) * HEAD ** (-0.5)
        grad_values = jnp.einsum(
            "rhg,rhd->grhd", attn_probs.astype(NARROW), grad_slot, preferred_element_type=SINGLE
        )
        key_count = key_rows.shape[0]
        spread_grads = jnp.concatenate(
            [
                grad_keys.reshape(key_count, rows_here, C),
                grad_values.reshape(key_count, rows_here, C),
            ],
            -1,
        )
        own_grads = return_keys(spread_grads)[0]
        bias_grad = jnp.sum(grad_scores.astype(SINGLE), axis=0)
        return (jnp.concatenate([grad_queries.reshape(rows_here, C), own_grads], -1), bias_grad)

    grad_time_proj, bias_grads = lax.map(
        time_back, (time_proj, video_mask, video_number, time_lse, grad_time_mixed)
    )
    grad_table = jnp.dot(
        key_table.T, jnp.sum(bias_grads, axis=0).T, precision=PRECISE, preferred_element_type=SINGLE
    )
    grad_time_proj = grad_time_proj.astype(NARROW)
    grad_time_qkv = weight_grad(time_in, grad_time_proj)
    value_norm, pull_norm = jax.vjp(layer_norm, section_three, norm_gains[:, 4])
    norm_part, gain_four = pull_norm(back_project(grad_time_proj, time_weight))
    carried = carried + norm_part
    back_cross = carried.astype(NARROW)
    grad_cross_out = weight_grad(cross_mixed, back_cross)
    grad_cross_mixed = back_project(back_cross, cross_weight).astype(NARROW).reshape(heads_view)
    grad_cquery, grad_tkeys, grad_tvalues = jax.vmap(attend_backward)(
        cross_queries, text_keys, text_values, text_usable, cross_lse, grad_cross_mixed
    )
    grad_cquery = grad_cquery.reshape(FR_DEV, rows_here, C).astype(NARROW)
    grad_cross_q = weight_grad(cross_in, grad_cquery)
    value_norm, pull_norm = jax.vjp(layer_norm, section_two, norm_gains[:, 3])
    norm_part, gain_three = pull_norm(back_project(grad_cquery, query_weight))
    carried = carried + norm_part
    text_grads = jnp.concatenate(
        [grad_tkeys.reshape(FR_DEV, TEXT, C), grad_tvalues.reshape(FR_DEV, TEXT, C)], -1
    )
    middle_grads = settle(grad_cross_q, grad_cross_out, grad_time_qkv)
    back_self = carried.astype(NARROW)
    grad_self_out = weight_grad(self_mixed, back_self)
    grad_self_mixed = back_project(back_self, self_weight).astype(NARROW).reshape(heads_view)

    def self_back(inputs):
        proj_slot, text_slot, lse_slot, grad_slot, text_grad_slot = inputs
        frame_kv, text_again = gather_keys(proj_slot[:, C:], text_slot)
        grad_queries, grad_keys, grad_values = attend_backward(
            proj_slot[:, :C].reshape(rows_here, HEADS, HEAD),
            frame_kv[:, :C].reshape(-1, HEADS, HEAD),
            frame_kv[:, C:].reshape(-1, HEADS, HEAD),
            every_key,
            lse_slot,
            grad_slot,
        )
        frame_grads = jnp.concatenate([grad_keys.reshape(-1, C), grad_values.reshape(-1, C)], -1)
        own_frame, own_text = scatter_keys(frame_grads, text_grad_slot)
        return (jnp.concatenate([grad_queries.reshape(rows_here, C), own_frame], -1), own_text)

    grad_self_proj, grad_text_kv = lax.map(
        self_back, (self_proj, text_kv, self_lse, grad_self_mixed, text_grads)
    )
    grad_self_proj = grad_self_proj.astype(NARROW)
    grad_self_qkv = weight_grad(self_in, grad_self_proj)
    grad_keyval = weight_grad(
        text_embed.reshape(FR_DEV * text_here, CTX), grad_text_kv.astype(NARROW)
    )
    value_norm, pull_norm = jax.vjp(layer_norm, section_one, norm_gains[:, 2])
    norm_part, gain_two = pull_norm(back_project(grad_self_proj, qkv_weight))
    carried = carried + norm_part
    upper_grads = settle(grad_keyval, grad_self_qkv, grad_self_out)
    back_conv = carried.astype(NARROW)
    grad_conv_two = weight_grad(columns_of(pad_two), back_conv)
    grad_act_two = convolve_back(back_conv, conv_two)
    value_silu, pull_silu = jax.vjp(jax.nn.silu, pre_two)
    grad_pre_two = pull_silu(grad_act_two)[0]
    gain_one = jnp.sum(grad_pre_two * normed_two, axis=(0, 1))
    grad_hidden = group_backward(normed_two, spread_two, grad_pre_two * norm_gains[:, 1])
    grad_film = jnp.concatenate(
        [jnp.sum(grad_hidden * conv_out, axis=1), jnp.sum(grad_hidden, axis=1)], -1
    )
    grad_film_w = jnp.dot(
        temb_act.astype(SINGLE).T, grad_film, precision=PRECISE, preferred_element_type=SINGLE
    )
    back_first = (grad_hidden * film_scale).astype(NARROW)
    grad_conv_one = weight_grad(columns_of(pad_one), back_first)
    grad_act_one = convolve_back(back_first, conv_one)
    value_silu, pull_silu = jax.vjp(jax.nn.silu, pre_one)
    grad_pre_one = pull_silu(grad_act_one)[0]
    gain_zero = jnp.sum(grad_pre_one * normed_one, axis=(0, 1))
    carried = carried + group_backward(normed_one, spread_one, grad_pre_one * norm_gains[:, 0])
    input_grad = carried.astype(NARROW).reshape(video_in.shape)
    lower_grads = settle(grad_conv_one, grad_film_w, grad_conv_two)
    gain_stack = jnp.stack(
        [gain_zero, gain_one, gain_two, gain_three, gain_four, gain_five], axis=1
    )
    small_sums = lax.psum((gain_stack, grad_table), (FRAME, SPACE))
    return (
        block_out,
        input_grad,
        small_sums[0],
        small_sums[1],
        lower_grads[0],
        lower_grads[2],
        lower_grads[1],
        upper_grads[1],
        upper_grads[2],
        middle_grads[0],
        upper_grads[0],
        middle_grads[1],
        middle_grads[2],
        down_grads[0],
        down_grads[1],
        down_grads[2],
    )


PIX = IMG_H * IMG_W
CUBE = (QUAD, CORE, SPACE)
CHIPS = (QUAD, SPACE)
TRIO = (HALF, CORE, SPACE)
WORLD = (HALF, QUAD, CORE, SPACE)
SCALE = HEAD ** (-0.5)


def moves(turn):
    return [
        (4 * a + 2 * c + b, 4 * (b ^ turn) + 2 * c + (a ^ c))
        for a in range(2)
        for c in range(2)
        for b in range(2)
    ]


def back(pairs):
    return [(target, source) for source, target in pairs]


def pick(flag, pair):
    return jnp.where(flag == 0, pair[0], pair[1])


def to_slot(block, half, space):
    own = lax.ppermute(pick(space, block), TRIO, moves(0))
    other = lax.ppermute(pick(1 - space, block), TRIO, moves(1))
    return jnp.concatenate(
        [jnp.where(half == 0, own, other), jnp.where(half == 0, other, own)], axis=0
    )


def send_back(frame, half):
    pieces = frame.reshape((2, frame.shape[0] // 2) + frame.shape[1:])
    own = lax.ppermute(pick(half, pieces), TRIO, back(moves(0)))
    other = lax.ppermute(pick(1 - half, pieces), TRIO, back(moves(1)))
    return own, other


def both_slots(own, other, space):
    return jnp.stack([jnp.where(space == 0, own, other), jnp.where(space == 0, other, own)])


def meta_slot(block, space):
    return lax.ppermute(pick(space, block), TRIO, moves(0))


class Weights(NamedTuple):
    conv_first: Any
    conv_second: Any
    film_weight: Any
    self_project: Any
    self_output: Any
    cross_query: Any
    cross_keyval: Any
    cross_output: Any
    time_project: Any
    time_output: Any
    feed_up: Any
    feed_down: Any


def mm(a, b):
    return jnp.dot(a, b, preferred_element_type=SINGLE)


VMEM_BYTES = 58 * 1024 * 1024
STEP = 384
STEPS = PIX // STEP
NT = (((1,), (1,)), ((), ()))
TN = (((0,), (0,)), ((), ()))


def nt(a, b):
    return lax.dot_general(a, b, NT, preferred_element_type=SINGLE)


def tn(a, b):
    return lax.dot_general(a, b, TN, preferred_element_type=SINGLE)


def kernel_call(body, outs, scratch=(), flops=10**9):
    return pl.pallas_call(
        body,
        out_shape=[jax.ShapeDtypeStruct(s, d) for s, d in outs],
        scratch_shapes=[pltpu.VMEM(s, d) for s, d in scratch],
        compiler_params=pltpu.CompilerParams(vmem_limit_bytes=VMEM_BYTES),
        cost_estimate=pl.CostEstimate(flops=flops, bytes_accessed=10**7, transcendentals=0),
    )


def group_matrix():
    lanes = jnp.arange(C) // (C // GROUPS)
    return (lanes[:, None] == lanes[None, :]).astype(SINGLE)


def grouped(row, gmat):
    wide = jnp.broadcast_to(row, (8, C))
    return lax.dot_general(
        wide, gmat, (((1,), (0,)), ((), ())), precision=PRECISE, preferred_element_type=SINGLE
    )[:1]


def edge_masks(rows):
    col = lax.broadcasted_iota(jnp.int32, (rows, C), 0) % IMG_W
    return col != 0, col != IMG_W - 1


def spread_columns(cols_ref, start, act):
    not_first, not_last = edge_masks(STEP)
    left = jnp.where(not_first, pltpu.roll(act, 1, 0), 0.0)
    right = jnp.where(not_last, pltpu.roll(act, STEP - 1, 0), 0.0)
    cols_ref[pl.ds(start, STEP), :] = jnp.concatenate(
        [left.astype(NARROW), act.astype(NARROW), right.astype(NARROW)], axis=1
    )


def conv_rows(cols_ref, w_ref, start):
    total = None
    for i in range(3):
        part = mm(cols_ref[pl.ds(start + IMG_W * i, STEP), :], w_ref[3 * C * i : 3 * C * (i + 1), :])
        total = part if total is None else total + part
    return total


def gn_stats(total, square, gmat):
    members = PIX * (C // GROUPS)
    center = grouped(total, gmat) / members
    return center, lax.rsqrt(grouped(square, gmat) / members - center * center + EPSILON)


def unpack_tall(half, full_ref, out_ref, at, rows, cols):
    parts = BAND // cols
    tall = rows // parts
    for quad in range(4):
        pieces = []
        for frame in range(4 * quad, 4 * quad + 4):
            place = half if frame < 8 else 1 - half
            sides = [
                full_ref[2 * (frame % 8) + s, place, at : at + tall, :].astype(SINGLE) for s in range(2)
            ]
            pieces += [
                jnp.concatenate([side[:, cols * q : cols * (q + 1)] for side in sides], axis=1)
                for q in range(parts)
            ]
        out_ref[4 * rows * quad : 4 * rows * (quad + 1), :] = jnp.concatenate(pieces, axis=0).astype(NARROW)


def clear_border(cols_ref):
    border = jnp.zeros((IMG_W, 3 * C), NARROW)
    cols_ref[0:IMG_W, :] = border
    cols_ref[PIX + IMG_W :, :] = border


def conv_kernel(x_ref, w1_ref, w2_ref, temb_ref, wf_ref, gains_ref, gmat_ref,
                conv_out_ref, sec_ref, cols1_ref, cols2_ref, stats_ref, film_ref):
    film_ref[...] = mm(temb_ref[...], wf_ref[...])
    gmat = gmat_ref[...]
    clear_border(cols1_ref)
    clear_border(cols2_ref)
    total = jnp.zeros((1, C), SINGLE)
    square = jnp.zeros((1, C), SINGLE)
    for r in range(STEPS):
        x = x_ref[r * STEP : (r + 1) * STEP, :].astype(SINGLE)
        total += jnp.sum(x, axis=0, keepdims=True)
        square += jnp.sum(x * x, axis=0, keepdims=True)
    center, spread = gn_stats(total, square, gmat)
    stats_ref[0:1, :] = center
    stats_ref[1:2, :] = spread
    for r in range(STEPS):
        x = x_ref[r * STEP : (r + 1) * STEP, :].astype(SINGLE)
        pre = (x - center) * spread * gains_ref[0:1, :]
        spread_columns(cols1_ref, IMG_W + r * STEP, pre * (0.5 + 0.5 * jnp.tanh(0.5 * pre)))
    scale = 1.0 + film_ref[0:1, :C]
    shift = film_ref[0:1, C:]
    total = jnp.zeros((1, C), SINGLE)
    square = jnp.zeros((1, C), SINGLE)
    for r in range(STEPS):
        out = conv_rows(cols1_ref, w1_ref, r * STEP)
        conv_out_ref[r * STEP : (r + 1) * STEP, :] = out
        hidden = out * scale + shift
        total += jnp.sum(hidden, axis=0, keepdims=True)
        square += jnp.sum(hidden * hidden, axis=0, keepdims=True)
    center, spread = gn_stats(total, square, gmat)
    stats_ref[2:3, :] = center
    stats_ref[3:4, :] = spread
    for r in range(STEPS):
        hidden = conv_out_ref[r * STEP : (r + 1) * STEP, :] * scale + shift
        pre = (hidden - center) * spread * gains_ref[1:2, :]
        spread_columns(cols2_ref, IMG_W + r * STEP, pre * (0.5 + 0.5 * jnp.tanh(0.5 * pre)))
    for r in range(STEPS):
        out = conv_rows(cols2_ref, w2_ref, r * STEP)
        rows = slice(r * STEP, (r + 1) * STEP)
        sec_ref[rows, :] = x_ref[rows, :].astype(SINGLE) + out


def conv_block(x, w1, w2, temb, wf, gains, gmat):
    cols = (PIX + 2 * IMG_W, 3 * C)
    return kernel_call(
        conv_kernel,
        [((PIX, C), SINGLE), ((PIX, C), SINGLE), (cols, NARROW), (cols, NARROW), ((8, C), SINGLE), ((8, 2 * C), SINGLE)],
        flops=15 * 10**9,
    )(x, w1, w2, temb, wf, gains, gmat)


def ln_rows(layer, gain):
    centered = layer - jnp.mean(layer, axis=-1, keepdims=True)
    rstd = lax.rsqrt(jnp.mean(centered * centered, axis=-1, keepdims=True) + EPSILON)
    return centered * rstd, rstd


def attend_rows(q, k, v_one, usable):
    scores = nt(q, k)
    if usable is not None:
        scores = jnp.where(usable, scores, MASKED)
    highest = jnp.max(scores, axis=-1, keepdims=True)
    probs = jnp.exp(scores - highest).astype(NARROW)
    both = mm(probs, v_one)
    total = both[:, HEAD : HEAD + 1]
    return both[:, :HEAD] / total, highest + jnp.log(total)


def with_ones(v):
    return jnp.concatenate([v, jnp.ones(v.shape, v.dtype)], axis=1)


def staged(count, front, rest):
    ahead = front(0)
    for i in range(count):
        now = ahead
        if i + 1 < count:
            ahead = front(i + 1)
        rest(i, now)


def head_lanes(h):
    return slice(h * HEAD, (h + 1) * HEAD)


def attn_kernel(sec1_ref, gains_ref, wqkv_ref, wso_ref, text_ref, usable_ref, wkv_ref, wcq_ref,
                wco_ref, wtime_ref,
                proj_ref, mix_ref, lse_ref, sec2_ref, kv_ref, cq_ref, cmix_ref, clse_ref,
                sec3_ref, tproj_ref):
    for r in range(STEPS):
        rows = slice(r * STEP, (r + 1) * STEP)
        hat, rstd = ln_rows(sec1_ref[rows, :], None)
        proj_ref[rows, :] = mm((hat * gains_ref[2:3, :]).astype(NARROW), wqkv_ref[...]).astype(NARROW)
    kv_ref[...] = mm(text_ref[...], wkv_ref[...]).astype(NARROW)
    for h in range(HEADS):
        lanes = slice(h * HEAD, (h + 1) * HEAD)
        k = proj_ref[:, C + h * HEAD : C + (h + 1) * HEAD]
        v = with_ones(proj_ref[:, 2 * C + h * HEAD : 2 * C + (h + 1) * HEAD])
        for r in range(STEPS):
            rows = slice(r * STEP, (r + 1) * STEP)
            q = proj_ref[rows, lanes] * jnp.bfloat16(SCALE)
            mix, lse = attend_rows(q, k, v, None)
            mix_ref[rows, lanes] = mix
            lse_ref[rows, h : h + 1] = lse
    usable = jnp.broadcast_to(usable_ref[...], (STEP, TEXT)) == 1
    for r in range(STEPS):
        rows = slice(r * STEP, (r + 1) * STEP)
        sec2 = sec1_ref[rows, :] + mm(mix_ref[rows, :].astype(NARROW), wso_ref[...])
        sec2_ref[rows, :] = sec2
        hat, rstd = ln_rows(sec2, None)
        cq_ref[rows, :] = mm((hat * gains_ref[3:4, :]).astype(NARROW), wcq_ref[...]).astype(NARROW)
        for h in range(HEADS):
            lanes = slice(h * HEAD, (h + 1) * HEAD)
            k = kv_ref[:, lanes]
            v = with_ones(kv_ref[:, C + h * HEAD : C + (h + 1) * HEAD])
            mix, lse = attend_rows(cq_ref[rows, lanes] * jnp.bfloat16(SCALE), k, v, usable)
            cmix_ref[rows, lanes] = mix
            clse_ref[rows, h : h + 1] = lse
        sec3 = sec2 + mm(cmix_ref[rows, :].astype(NARROW), wco_ref[...])
        sec3_ref[rows, :] = sec3
        hat, rstd = ln_rows(sec3, None)
        tproj_ref[rows, :] = mm((hat * gains_ref[4:5, :]).astype(NARROW), wtime_ref[...]).astype(NARROW)


def attn_block(sec1, gains, wqkv, wso, text, usable, wkv, wcq, wco, wtime):
    full = ((PIX, C), SINGLE)
    low = ((PIX, C), NARROW)
    return kernel_call(
        attn_kernel,
        [((PIX, 3 * C), NARROW), full, ((PIX, 8), SINGLE), full, ((TEXT, 2 * C), NARROW), low,
         full, ((PIX, 8), SINGLE), full, ((PIX, 3 * C), NARROW)],
        flops=28 * 10**9,
    )(sec1, gains, wqkv, wso, text, usable, wkv, wcq, wco, wtime)


def ln_back_rows(layer, gain, upstream):
    hat, rstd = ln_rows(layer, gain)
    dx = upstream * gain
    part = rstd * (
        dx - jnp.mean(dx, axis=-1, keepdims=True) - hat * jnp.mean(dx * hat, axis=-1, keepdims=True)
    )
    return part, jnp.sum(upstream * hat, axis=0, keepdims=True), hat


def split_three(column):
    one = column.astype(NARROW)
    rest = column - one.astype(SINGLE)
    two = rest.astype(NARROW)
    return [one, two, (rest - two.astype(SINGLE)).astype(NARROW)]


def extended(rows, column):
    return jnp.concatenate([rows] + split_three(-column), axis=1)


def with_units(rows):
    return jnp.concatenate([rows, jnp.ones((rows.shape[0], 3), rows.dtype)], axis=1)


def back_front(q, k, v, lse, grad, mix):
    inner = jnp.sum(grad.astype(SINGLE) * mix, axis=-1, keepdims=True)
    return nt(with_units(k), extended(q, lse)), nt(with_units(v), extended(grad, inner))


def cross_back_kernel(carried_ref, gtime_ref, sec3_ref, sec2_ref, cq_ref, cmix_ref, clse_ref,
                      kv_ref, usable_ref, text_ref, gains_ref, wtime_ref, wco_ref, wcq_ref,
                      carried_out_ref, pack_ref, gain_ref,
                      hat_s, back_s, dq_s, dkv_s, da_s, db_s, dw_s, gmix_s):
    gain_ref[...] = jnp.zeros((8, C), SINGLE)
    usable = jnp.broadcast_to(usable_ref[...], (TEXT, PIX)) == 1
    part, gain, hat = ln_back_rows(sec3_ref[...], gains_ref[4:5, :], nt(gtime_ref[...], wtime_ref[...]))
    gain_ref[1:2, :] = gain
    hat_s[...] = (hat * gains_ref[4:5, :]).astype(NARROW)
    carried = carried_ref[...] + part
    carried_out_ref[...] = carried
    back_s[...] = carried.astype(NARROW)
    gmix_s[...] = nt(back_s[...], wco_ref[...]).astype(NARROW)

    def front(h):
        lanes = head_lanes(h)
        return back_front(
            cq_ref[:, lanes] * jnp.bfloat16(SCALE), kv_ref[:, lanes],
            kv_ref[:, C + h * HEAD : C + (h + 1) * HEAD], clse_ref[:, h : h + 1], gmix_s[:, lanes], cmix_ref[:, lanes],
        )

    def rest(h, pair):
        lanes = head_lanes(h)
        scores, grad_probs = pair
        probs = jnp.exp(jnp.where(usable, scores, MASKED))
        grad_scores = (probs * grad_probs).astype(NARROW)
        dq_s[:, lanes] = (tn(grad_scores, kv_ref[:, lanes]) * SCALE).astype(NARROW)
        dkv_s[:, lanes] = mm(grad_scores, cq_ref[:, lanes] * jnp.bfloat16(SCALE))
        dkv_s[:, C + h * HEAD : C + (h + 1) * HEAD] = mm(probs.astype(NARROW), gmix_s[:, lanes])

    staged(HEADS, front, rest)
    da_s[...] = tn(hat_s[...], gtime_ref[...])
    db_s[...] = tn(cmix_ref[...].astype(NARROW), back_s[...])
    bands_out(pack_ref, 52, db_s, 20, 160)
    part, gain, hat = ln_back_rows(sec2_ref[...], gains_ref[3:4, :], nt(dq_s[...], wcq_ref[...]))
    gain_ref[0:1, :] = gain
    carried_out_ref[...] += part
    hat_s[...] = (hat * gains_ref[3:4, :]).astype(NARROW)
    db_s[...] = tn(hat_s[...], dq_s[...])
    pair_out(pack_ref, 32, da_s, db_s)
    dw_s[...] = tn(text_ref[...], dkv_s[...].astype(NARROW))
    bands_out(pack_ref, 0, dw_s, 64, 320)


def cross_back(*args):
    low = ((PIX, C), NARROW)
    return kernel_call(
        cross_back_kernel,
        [((PIX, C), SINGLE), (packed_shape(64), NARROW), ((8, C), SINGLE)],
        [low, low, low, ((TEXT, 2 * C), SINGLE), ((C, 3 * C), SINGLE), ((C, C), SINGLE), ((CTX, 2 * C), SINGLE), low],
        flops=26 * 10**9,
    )(*args)


def self_back_kernel(carried_ref, sec1_ref, proj_ref, mix_ref, lse_ref, gains_ref, wqkv_ref, wso_ref,
                     carried_out_ref, pack_ref, gain_ref,
                     back_s, gmix_s, dproj_s, hat_s, dk_s, dv_s, da_s, db_s):
    gain_ref[...] = jnp.zeros((8, C), SINGLE)
    back_s[...] = carried_ref[...].astype(NARROW)
    gmix_s[...] = nt(back_s[...], wso_ref[...]).astype(NARROW)
    db_s[...] = tn(mix_ref[...].astype(NARROW), back_s[...])

    def spots(i):
        h, r = divmod(i, STEPS)
        return slice(r * STEP, (r + 1) * STEP), head_lanes(h), head_lanes(HEADS + h), head_lanes(2 * HEADS + h), h, r

    def front(i):
        rows, lanes, lanes_k, lanes_v, h, r = spots(i)
        return back_front(
            proj_ref[rows, lanes] * jnp.bfloat16(SCALE), proj_ref[:, lanes_k], proj_ref[:, lanes_v],
            lse_ref[rows, h : h + 1], gmix_s[rows, lanes], mix_ref[rows, lanes],
        )

    def rest(i, pair):
        rows, lanes, lanes_k, lanes_v, h, r = spots(i)
        scores, grad_probs = pair
        probs = jnp.exp(scores)
        grad_scores = (probs * grad_probs).astype(NARROW)
        dproj_s[rows, lanes] = (tn(grad_scores, proj_ref[:, lanes_k]) * SCALE).astype(NARROW)
        dk = mm(grad_scores, proj_ref[rows, lanes] * jnp.bfloat16(SCALE))
        dv = mm(probs.astype(NARROW), gmix_s[rows, lanes])
        if r > 0:
            dk += dk_s[...]
            dv += dv_s[...]
        if r < STEPS - 1:
            dk_s[...] = dk
            dv_s[...] = dv
        else:
            dproj_s[:, lanes_k] = dk.astype(NARROW)
            dproj_s[:, lanes_v] = dv.astype(NARROW)

    staged(HEADS * STEPS, front, rest)
    part, gain, hat = ln_back_rows(sec1_ref[...], gains_ref[2:3, :], nt(dproj_s[...], wqkv_ref[...]))
    gain_ref[0:1, :] = gain
    hat_s[...] = (hat * gains_ref[2:3, :]).astype(NARROW)
    carried_out_ref[...] = carried_ref[...] + part
    da_s[...] = tn(hat_s[...], dproj_s[...])
    pair_out(pack_ref, 0, da_s, db_s)


def self_back_block(*args):
    low = ((PIX, C), NARROW)
    return kernel_call(
        self_back_kernel,
        [((PIX, C), SINGLE), (packed_shape(24), NARROW), ((8, C), SINGLE)],
        [low, low, ((PIX, 3 * C), NARROW), low, ((PIX, HEAD), SINGLE), ((PIX, HEAD), SINGLE),
         ((C, 3 * C), SINGLE), ((C, C), SINGLE)],
        flops=29 * 10**9,
    )(*args)


def feed_kernel(sec3_ref, mix_ref, cot_ref, gains_ref, wto_ref, wup_ref, wdown_ref,
                out_ref, carried_ref, gmix_ref, pack_ref, gain_ref,
                hat_s, act_s, lift_s, back_s, d_s, dw_s):
    gain_ref[...] = jnp.zeros((8, C), SINGLE)
    for r in range(1):
        rows = slice(0, PIX)
        sec4 = sec3_ref[rows, :] + mm(mix_ref[rows, :], wto_ref[...])
        hat, rstd = ln_rows(sec4, None)
        hat_s[rows, :] = (hat * gains_ref[5:6, :]).astype(NARROW)
        lifted = mm(hat_s[rows, :], wup_ref[...])
        cube = lifted * lifted
        inner = jnp.tanh(GELU_A * lifted * (1.0 + GELU_B * cube))
        gate = 0.5 + 0.5 * inner
        act_s[rows, :] = (lifted * gate).astype(NARROW)
        slope = gate + (0.5 * GELU_A) * lifted * (1.0 - inner * inner) * (1.0 + (3.0 * GELU_B) * cube)
        grad_act = nt(cot_ref[rows, :], wdown_ref[...])
        lift_s[rows, :] = (grad_act * slope).astype(NARROW)
        out_ref[rows, :] = (sec4 + mm(act_s[rows, :], wdown_ref[...])).astype(NARROW)
        part, gain, hat = ln_back_rows(sec4, gains_ref[5:6, :], nt(lift_s[rows, :], wup_ref[...]))
        gain_ref[0:1, :] += gain
        carried = cot_ref[rows, :].astype(SINGLE) + part
        carried_ref[rows, :] = carried
        back_s[rows, :] = carried.astype(NARROW)
        gmix_ref[rows, :] = nt(back_s[rows, :], wto_ref[...]).astype(NARROW)
    dw_s[...] = tn(hat_s[...], lift_s[...])
    bands_out(pack_ref, 0, dw_s, 20, 640)
    d_s[...] = tn(act_s[...], cot_ref[...])
    bands_out(pack_ref, 20, d_s, 80, 160)
    d_s[0:C, :] = tn(mix_ref[...], back_s[...])
    bands_out(pack_ref, 40, d_s, 20, 160)


def feed_block(*args):
    low = ((PIX, C), NARROW)
    wide = ((PIX, FF), NARROW)
    return kernel_call(
        feed_kernel,
        [low, ((PIX, C), SINGLE), low, (packed_shape(48), NARROW), ((8, C), SINGLE)],
        [low, wide, wide, low, ((FF, C), SINGLE), ((C, FF), SINGLE)],
        flops=20 * 10**9,
    )(*args)


def untile(tile):
    return tile.reshape(16, 8, tile.shape[-1])


def time_kernel(qkv_ref, bias_ref, low_ref, mix_ref, lse_ref, wide_s):
    wide_s[...] = qkv_ref[...].astype(SINGLE)

    def front(b):
        tile = wide_s[:, 8 * b : 8 * b + 8, :].reshape(128, 3 * C).astype(NARROW)
        scores = [
            nt(tile[:, head_lanes(h)] * jnp.bfloat16(SCALE), tile[:, head_lanes(HEADS + h)]) for h in range(HEADS)
        ]
        return jnp.concatenate(scores, axis=0) + bias_ref[...], tile

    def rest(b, pair):
        scores, tile = pair
        highest = jnp.max(scores, axis=-1, keepdims=True)
        probs = jnp.exp(scores - highest).astype(NARROW)
        both = jnp.concatenate(
            [mm(probs[128 * h : 128 * h + 128], with_ones(tile[:, head_lanes(2 * HEADS + h)])) for h in range(HEADS)],
            axis=0,
        )
        total = both[:, HEAD : HEAD + 1]
        mix = both[:, :HEAD] / total
        lse = highest + jnp.log(total)
        cut = [slice(128 * h, 128 * h + 128) for h in range(HEADS)]
        for h in range(HEADS):
            lse_ref[128 * b : 128 * b + 128, h : h + 1] = lse[cut[h]]
        mix_ref[:, 8 * b : 8 * b + 8, :] = untile(jnp.concatenate([mix[c] for c in cut], axis=1))

    staged(PIX // 16 // 8, front, rest)
    low_ref[...] = mix_ref[...].astype(NARROW)


def time_block(qkv, bias):
    rows = PIX // 16
    return kernel_call(
        time_kernel,
        [((16, rows, C), NARROW), ((16, rows, C), SINGLE), ((PIX, 8), SINGLE)],
        [((16, rows, 3 * C), SINGLE)],
        flops=15 * 10**9,
    )(qkv, bias)


def time_back_kernel(qkv_ref, bias_ref, mix_ref, lse_ref, grad_ref, fold_ref, dqkv_ref, small_ref,
                     wide_s, grad_s, out_s, dbias_s):
    dbias_s[...] = jnp.zeros((HEADS * 128, 128), SINGLE)
    wide_s[...] = qkv_ref[...].astype(SINGLE)
    grad_s[...] = grad_ref[...].astype(SINGLE)

    def front(b):
        part = slice(8 * b, 8 * b + 8)
        tile = wide_s[:, part, :].reshape(128, 3 * C).astype(NARROW)
        grads = grad_s[:, part, :].reshape(128, C)
        inners = grads * mix_ref[:, part, :].reshape(128, C)
        grads = grads.astype(NARROW)
        scores, grad_probs, qs, gs = [], [], [], []
        for h in range(HEADS):
            q = tile[:, head_lanes(h)] * jnp.bfloat16(SCALE)
            g = grads[:, head_lanes(h)]
            lse = lse_ref[128 * b : 128 * b + 128, h : h + 1]
            inner = jnp.sum(inners[:, head_lanes(h)], axis=-1, keepdims=True)
            scores.append(nt(with_units(tile[:, head_lanes(HEADS + h)]), extended(q, lse)))
            grad_probs.append(nt(with_units(tile[:, head_lanes(2 * HEADS + h)]), extended(g, inner)))
            qs.append(q)
            gs.append(g)
        return jnp.concatenate(scores, axis=0) + bias_ref[...], jnp.concatenate(grad_probs, axis=0), tile, qs, gs

    def rest(b, held):
        scores, grad_probs, tile, qs, gs = held
        probs = jnp.exp(scores)
        ds = (probs * grad_probs).astype(NARROW)
        dbias_s[...] += ds.astype(SINGLE)
        probs = probs.astype(NARROW)
        cut = [slice(128 * h, 128 * h + 128) for h in range(HEADS)]
        dqs = [tn(ds[cut[h]], tile[:, head_lanes(HEADS + h)]) * SCALE for h in range(HEADS)]
        dks = [mm(ds[cut[h]], qs[h]) for h in range(HEADS)]
        dvs = [mm(probs[cut[h]], gs[h]) for h in range(HEADS)]
        out_s[:, 8 * b : 8 * b + 8, :] = untile(jnp.concatenate(dqs + dks + dvs, axis=1))

    staged(PIX // 16 // 8, front, rest)
    dqkv_ref[...] = out_s[...].astype(NARROW)
    fold = fold_ref[...]
    for h in range(HEADS):
        rows = lax.dot_general(
            fold, dbias_s[128 * h : 128 * h + 128, :], TN, precision=PRECISE, preferred_element_type=SINGLE
        )
        small_ref[h] = jnp.dot(rows, fold, precision=PRECISE, preferred_element_type=SINGLE)


def time_back_block(qkv, bias_t, mix, lse, grad):
    fold = (jnp.arange(128)[:, None] // 8 == jnp.arange(16)[None, :]).astype(SINGLE)
    wide = ((16, PIX // 16, 3 * C), SINGLE)
    return kernel_call(
        time_back_kernel,
        [((16, PIX // 16, 3 * C), NARROW), ((HEADS, 16, 16), SINGLE)],
        [wide, ((16, PIX // 16, C), SINGLE), wide, ((HEADS * 128, 128), SINGLE)],
        flops=25 * 10**9,
    )(qkv, bias_t, mix, lse, grad, fold)


def conv_back_rows(y_s, r):
    not_first, not_last = edge_masks(STEP)
    base = r * STEP
    sides = []
    for j in range(3):
        total = None
        for i in range(3):
            lanes = slice((3 * i + j) * C, (3 * i + j + 1) * C)
            part = y_s[pl.ds(base + IMG_W * (2 - i), STEP), lanes]
            total = part if total is None else total + part
        sides.append(total)
    from_next = jnp.where(not_last, pltpu.roll(sides[0], STEP - 1, 0), 0.0)
    from_prev = jnp.where(not_first, pltpu.roll(sides[2], 1, 0), 0.0)
    return from_next + sides[1] + from_prev


def conv_weight_grad(cols_ref, back_s, d_s):
    for i in range(3):
        d_s[3 * C * i : 3 * C * (i + 1), :] = tn(cols_ref[pl.ds(IMG_W * i, PIX), :], back_s[...])


def conv_input_products(back_s, w_ref, y_s):
    border = jnp.zeros((IMG_W, 9 * C), SINGLE)
    y_s[0:IMG_W, :] = border
    y_s[PIX + IMG_W :, :] = border
    for r in range(STEPS):
        y_s[pl.ds(IMG_W + r * STEP, STEP), :] = nt(back_s[r * STEP : (r + 1) * STEP, :], w_ref[...])


def silu_slope(pre):
    gate = 0.5 + 0.5 * jnp.tanh(0.5 * pre)
    return gate * (1.0 + pre * (1.0 - gate))


def second_weight_kernel(carried_ref, cols2_ref, upper_ref, pack_ref, back_ref, d_s):
    pack_ref[:, :, :, 0:24, :] = upper_ref[...]
    for r in range(STEPS):
        rows = slice(r * STEP, (r + 1) * STEP)
        back_ref[rows, :] = carried_ref[rows, :].astype(NARROW)
    conv_weight_grad(cols2_ref, back_ref, d_s)
    bands_out(pack_ref, 24, d_s, 180, 160)


def second_weight(carried, cols2, upper):
    return kernel_call(
        second_weight_kernel, [(packed_shape(72), NARROW), ((PIX, C), NARROW)], [((9 * C, C), SINGLE)],
        flops=9 * 10**9,
    )(carried, cols2, upper)


def second_back_kernel(back_s, conv_out_ref, stats_ref, film_ref, gains_ref, gmat_ref,
                       w2_ref, hidden_ref, back_ref, sums_ref, y_s):
    conv_input_products(back_s, w2_ref, y_s)
    scale = 1.0 + film_ref[0:1, :C]
    shift = film_ref[0:1, C:]
    center, spread, gain = stats_ref[2:3, :], stats_ref[3:4, :], gains_ref[1:2, :]
    zero = jnp.zeros((1, C), SINGLE)
    gain_sum, total, crossed = zero, zero, zero
    for r in range(STEPS):
        rows = slice(r * STEP, (r + 1) * STEP)
        normed = (conv_out_ref[rows, :] * scale + shift - center) * spread
        grad_pre = conv_back_rows(y_s, r) * silu_slope(normed * gain)
        gain_sum += jnp.sum(grad_pre * normed, axis=0, keepdims=True)
        grad = grad_pre * gain
        hidden_ref[rows, :] = grad
        total += jnp.sum(grad, axis=0, keepdims=True)
        crossed += jnp.sum(grad * normed, axis=0, keepdims=True)
    members = PIX * (C // GROUPS)
    total = grouped(total, gmat_ref[...]) / members
    crossed = grouped(crossed, gmat_ref[...]) / members
    film_one, film_two = zero, zero
    for r in range(STEPS):
        rows = slice(r * STEP, (r + 1) * STEP)
        conv_out = conv_out_ref[rows, :]
        normed = (conv_out * scale + shift - center) * spread
        hidden = spread * (hidden_ref[rows, :] - total - normed * crossed)
        film_one += jnp.sum(hidden * conv_out, axis=0, keepdims=True)
        film_two += jnp.sum(hidden, axis=0, keepdims=True)
        back_ref[rows, :] = (hidden * scale).astype(NARROW)
    sums_ref[...] = jnp.zeros((8, C), SINGLE)
    sums_ref[0:1, :] = gain_sum
    sums_ref[1:2, :] = film_one
    sums_ref[2:3, :] = film_two


def second_back(*args):
    return kernel_call(
        second_back_kernel,
        [((PIX, C), SINGLE), ((PIX, C), NARROW), ((8, C), SINGLE)],
        [((PIX + 2 * IMG_W, 9 * C), SINGLE)],
        flops=9 * 10**9,
    )(*args)


def first_weight_kernel(cols1_ref, back_ref, pack_ref, d_s):
    conv_weight_grad(cols1_ref, back_ref, d_s)
    bands_out(pack_ref, 0, d_s, 180, 160)


def first_weight(cols1, back):
    return kernel_call(
        first_weight_kernel, [(packed_shape(48), NARROW)], [((9 * C, C), SINGLE)], flops=9 * 10**9
    )(cols1, back)[0]


def small_kernel(half_ref, got_ref, own_ref, other_ref, small_ref):
    half = half_ref[0]

    def film(place):
        both = got_ref[:, place, :]
        return lax.dot_general(
            both[:, C : C + 80], both[:, :C], TN, precision=PRECISE, preferred_element_type=SINGLE
        )

    own_ref[...] = film(half)
    other_ref[...] = film(1 - half).astype(NARROW)
    total = got_ref[0]
    for s in range(1, 16):
        total += got_ref[s]
    small_ref[...] = total


def small_pack_kernel(temb_ref, sums_d, sums_e, gain_a, gain_b, gain_c, table_ref, out_ref):
    out_ref[...] = jnp.zeros((16, 16, BAND), SINGLE)
    temb = temb_ref[0:1, :].astype(SINGLE)
    same = jnp.concatenate(
        [sums_e[0:1, :], sums_d[0:1, :], gain_c[0:1, :], gain_b[0:2, :], gain_a[0:1, :], table_ref[...]], axis=0
    )
    for j in range(16):
        for h in range(2):
            at = 80 * (8 * h + j // 2)
            out_ref[j, h : h + 1, 0 : C + 80] = jnp.concatenate(
                [sums_d[1 + j % 2 : 2 + j % 2, :], temb[:, at : at + 80]], axis=1
            )
        out_ref[j, 2:9, 0:C] = same


def small_swap(temb, sums_d, sums_e, gain_a, gain_b, gain_c, grad_table):
    table_row = jnp.pad(grad_table.reshape(1, -1), ((0, 0), (0, C - NB * HEADS)))
    packed = kernel_call(small_pack_kernel, [((16, 16, BAND), SINGLE)])(
        temb, sums_d, sums_e, gain_a, gain_b, gain_c, table_row
    )[0]
    return lax.all_to_all(packed, CUBE, 0, 0, tiled=True)


def small_settle(got, half_vec):
    own, other, small = smem_call(
        small_kernel, 1, [((80, C), SINGLE), ((80, C), NARROW), ((16, BAND), SINGLE)], flops=2 * 10**9
    )(half_vec, got)
    swap = [(0, 1), (1, 0)]
    return own, lax.ppermute(other, HALF, swap), small + lax.ppermute(small, HALF, swap)


def finish_kernel(down, down_r, middle, middle_r, upper, upper_r, first, first_r,
                  film, film_r, *outs):
    w = Weights(*outs)
    total = down[...] + down_r[...].astype(SINGLE)
    bands_in(total, 0, w.feed_up, 20, 640)
    bands_in(total, 20, w.feed_down, 80, 160)
    bands_in(total, 40, w.time_output, 20, 160)
    total = middle[...] + middle_r[...].astype(SINGLE)
    bands_in(total, 0, w.cross_keyval, 64, 320)
    w.time_project[...] = total[32:52, 0:480]
    w.cross_query[...] = total[32:52, 480:640]
    bands_in(total, 52, w.cross_output, 20, 160)
    total = upper[...] + upper_r[...].astype(SINGLE)
    w.self_project[...] = total[0:20, 0:480]
    w.self_output[...] = total[0:20, 480:640]
    bands_turned(total, 24, w.conv_second, 180, 160)
    bands_turned(first[...] + first_r[...].astype(SINGLE), 0, w.conv_first, 180, 160)
    w.film_weight[...] = film[...] + film_r[...].astype(SINGLE)


def finish(*groups):
    shapes = Weights(
        conv_first=(160, 180), conv_second=(160, 180), film_weight=(80, C), self_project=(20, 480),
        self_output=(20, 160), cross_query=(20, 160), cross_keyval=(64, C), cross_output=(20, 160),
        time_project=(20, 480), time_output=(20, 160), feed_up=(20, BAND), feed_down=(80, 160),
    )
    out = Weights(*kernel_call(finish_kernel, [(s, SINGLE) for s in shapes])(*groups))
    return out._replace(conv_first=out.conv_first.T, conv_second=out.conv_second.T)


def first_back_kernel(carried_ref, x_ref, stats_ref, gains_ref, gmat_ref, w1_ref, back_ref,
                      grad_ref, sums_ref, y_s, pre_s):
    conv_input_products(back_ref, w1_ref, y_s)
    center, spread, gain = stats_ref[0:1, :], stats_ref[1:2, :], gains_ref[0:1, :]
    zero = jnp.zeros((1, C), SINGLE)
    gain_sum, total, crossed = zero, zero, zero
    for r in range(STEPS):
        rows = slice(r * STEP, (r + 1) * STEP)
        normed = (x_ref[rows, :].astype(SINGLE) - center) * spread
        grad_pre = conv_back_rows(y_s, r) * silu_slope(normed * gain)
        gain_sum += jnp.sum(grad_pre * normed, axis=0, keepdims=True)
        grad = grad_pre * gain
        pre_s[rows, :] = grad
        total += jnp.sum(grad, axis=0, keepdims=True)
        crossed += jnp.sum(grad * normed, axis=0, keepdims=True)
    members = PIX * (C // GROUPS)
    total = grouped(total, gmat_ref[...]) / members
    crossed = grouped(crossed, gmat_ref[...]) / members
    for r in range(STEPS):
        rows = slice(r * STEP, (r + 1) * STEP)
        normed = (x_ref[rows, :].astype(SINGLE) - center) * spread
        grad = spread * (pre_s[rows, :] - total - normed * crossed)
        grad_ref[rows, :] = (carried_ref[rows, :] + grad).astype(NARROW)
    sums_ref[...] = jnp.zeros((8, C), SINGLE)
    sums_ref[0:1, :] = gain_sum


def first_back(*args):
    return kernel_call(
        first_back_kernel,
        [((PIX, C), NARROW), ((8, C), SINGLE)],
        [((PIX + 2 * IMG_W, 9 * C), SINGLE), ((PIX, C), SINGLE)],
        flops=11 * 10**9,
    )(*args)


BAND = 640
QUARTER = 160
PACK_ROWS = 272


def smem_call(body, n_in, outs, scratch=(), flops=10**9):
    specs = [pl.BlockSpec(memory_space=pltpu.SMEM)] + [pl.BlockSpec(memory_space=pltpu.VMEM)] * n_in
    return pl.pallas_call(
        body,
        in_specs=specs,
        out_shape=[jax.ShapeDtypeStruct(s, d) for s, d in outs],
        scratch_shapes=[pltpu.VMEM(s, d) for s, d in scratch],
        compiler_params=pltpu.CompilerParams(vmem_limit_bytes=VMEM_BYTES),
        cost_estimate=pl.CostEstimate(flops=flops, bytes_accessed=10**7, transcendentals=0),
    )


def side_by_side(out, at, ref, cols):
    parts = BAND // cols
    tall = ref.shape[0] // parts
    wide = ref[...].astype(SINGLE)
    out[at : at + tall, :] = jnp.concatenate(
        [wide[tall * q : tall * (q + 1), :] for q in range(parts)], axis=1
    ).astype(NARROW)


def pack_kernel(*refs):
    w = Weights(*refs[:12])
    out = refs[12]
    out[...] = jnp.zeros((PACK_ROWS, BAND), NARROW)
    side_by_side(out, 0, w.conv_first[...].astype(SINGLE).T, 160)
    side_by_side(out, 48, w.conv_second[...].astype(SINGLE).T, 160)
    side_by_side(out, 96, w.film_weight, 320)
    side_by_side(out, 136, w.cross_keyval, 320)
    out[168:188, 0:480] = w.self_project[...]
    out[168:188, 480:640] = w.self_output[...]
    out[192:212, 0:480] = w.time_project[...]
    out[192:212, 480:640] = w.time_output[...]
    out[216:236, :] = w.feed_up[...]
    side_by_side(out, 240, w.feed_down, 160)
    side_by_side(out, 260, w.cross_query, 160)
    side_by_side(out, 265, w.cross_output, 160)


def pack_weights(w):
    w = w._replace(conv_first=w.conv_first.T, conv_second=w.conv_second.T)
    return kernel_call(pack_kernel, [((PACK_ROWS, BAND), NARROW)])(*w)[0]


def unpack_pair(half, full_ref, wide, thin, at):
    for out, c0, cols in ((wide, 0, 480), (thin, 480, 160)):
        for quad in range(4):
            parts = []
            for f in range(4 * quad, 4 * quad + 4):
                place = half if f < 8 else 1 - half
                parts.append(jnp.concatenate(
                    [full_ref[2 * (f % 8) + s, place, at : at + 20, c0 : c0 + cols].astype(SINGLE) for s in range(2)],
                    axis=1,
                ))
            out[80 * quad : 80 * (quad + 1), :] = jnp.concatenate(parts, axis=0).astype(NARROW)


def unpack_kernel(half_ref, full_ref, first, second, film, wide, thin, query, keyval, mixed, time, time_out):
    half = half_ref[0]
    unpack_tall(half, full_ref, first, 0, 180, 160)
    unpack_tall(half, full_ref, second, 48, 180, 160)
    unpack_tall(half, full_ref, film, 96, 80, 320)
    unpack_tall(half, full_ref, keyval, 136, 64, 320)
    unpack_tall(half, full_ref, query, 260, 20, 160)
    unpack_tall(half, full_ref, mixed, 265, 20, 160)
    unpack_pair(half, full_ref, wide, thin, 168)
    unpack_pair(half, full_ref, time, time_out, 192)


def unpack_late_kernel(half_ref, full_ref, up, down):
    half = half_ref[0]
    unpack_tall(half, full_ref, up, 216, 20, 640)
    unpack_tall(half, full_ref, down, 240, 80, 160)


def unpacked(body, shapes, half_vec, full):
    return smem_call(body, 1, [(s, NARROW) for s in shapes], flops=3 * len(shapes) // 2 * 10**9)(half_vec, full)


def packed_shape(rows):
    return (2, 8, 2, rows, BAND)


def bands_out(out_ref, at, grad_ref, rows, cols):
    parts = BAND // cols
    tall = rows // parts
    for f in range(16):
        for s in range(2):
            lanes = slice(s * cols, (s + 1) * cols)
            pieces = [
                grad_ref[rows * f + tall * q : rows * f + tall * (q + 1), lanes] for q in range(parts)
            ]
            piece = pieces[0] if parts == 1 else jnp.concatenate(pieces, axis=1)
            out_ref[f % 2, 2 * (f % 8 // 2) + s, f // 8, at : at + tall, :] = piece.astype(NARROW)


def pair_out(out_ref, at, wide_ref, thin_ref):
    for f in range(16):
        for s in range(2):
            piece = jnp.concatenate(
                [wide_ref[20 * f : 20 * f + 20, 480 * s : 480 * s + 480],
                 thin_ref[20 * f : 20 * f + 20, 160 * s : 160 * s + 160]],
                axis=1,
            )
            out_ref[f % 2, 2 * (f % 8 // 2) + s, f // 8, at : at + 20, :] = piece.astype(NARROW)


def bands_turned(total, at, out_ref, rows, cols):
    parts = BAND // cols
    tall = rows // parts
    out_ref[...] = jnp.concatenate(
        [total[at : at + tall, cols * q : cols * (q + 1)] for q in range(parts)], axis=0
    ).T


def bands_in(total, at, out_ref, rows, cols):
    parts = BAND // cols
    tall = rows // parts
    for q in range(parts):
        out_ref[tall * q : tall * (q + 1), :] = total[at : at + tall, cols * q : cols * (q + 1)]


def reduce_kernel(half_ref, got_ref, own_ref, other_ref):
    half = half_ref[0]
    own = got_ref[0, half].astype(SINGLE)
    other = got_ref[0, 1 - half].astype(SINGLE)
    for s in range(1, 8):
        own += got_ref[s, half].astype(SINGLE)
        other += got_ref[s, 1 - half].astype(SINGLE)
    own_ref[...] = own
    other_ref[...] = other.astype(NARROW)


def chip_sum(packed, core):
    got = lax.ppermute(pick(1 - core, packed), CORE, [(0, 1), (1, 0)])
    return (pick(core, packed).astype(SINGLE) + got.astype(SINGLE)).astype(NARROW)


def chip_swap(chip):
    return lax.all_to_all(chip, CHIPS, 0, 0, tiled=True)


def reduce_half(got, half_vec):
    shape = got.shape[2:]
    own, other = smem_call(reduce_kernel, 1, [(shape, SINGLE), (shape, NARROW)], flops=2 * 10**9)(half_vec, got)
    return own, lax.ppermute(other, HALF, [(0, 1), (1, 0)])


def time_setup(video_mask, video_number, bucket_index, bias_table, half):
    order = jnp.array([8 * ((g % 2) ^ (g // 2 % 2)) + g // 2 for g in range(16)])
    live = pick(half, video_mask)
    number = pick(half, video_number)
    same = (live[:, None] == 1) & (live[None, :] == 1) & (number[:, None] == number[None, :])
    same = same | (jnp.arange(16)[:, None] == jnp.arange(16)[None, :])
    bucket = bucket_index[order][:, order]
    one_hot = (bucket.reshape(-1, 1) == jnp.arange(NB)[None, :]).astype(SINGLE)
    table = jnp.dot(one_hot, bias_table, precision=PRECISE).reshape(16, 16, HEADS).transpose(2, 0, 1)
    small = jnp.where(same[order][:, order][None], table, MASKED)
    pixel = jnp.arange(8)
    wide = jnp.where(
        (pixel[:, None] == pixel[None, :])[None, None, :, None, :], small[:, :, None, :, None], MASKED
    )
    return wide.reshape(HEADS * 128, 128), one_hot


def swap_frames(block, rows):
    return lax.all_to_all(block.reshape(16, rows, block.shape[-1]), CUBE, 0, 0, tiled=True)


def fast_shards(
    video_in, time_embed, text_embed, text_mask, video_mask, video_number, bucket_index,
    norm_gains, bias_table, conv_first, conv_second, film_weight, self_project, self_output,
    cross_query, cross_keyval, cross_output, time_project, time_output, feed_up, feed_down,
    cotangent,
):
    half = lax.axis_index(HALF)
    space = lax.axis_index(SPACE)
    core = lax.axis_index(CORE)
    gains = norm_gains.T
    half_vec = jnp.full((1,), half, jnp.int32)
    packed = pack_weights(Weights(
        conv_first=conv_first, conv_second=conv_second, film_weight=film_weight,
        self_project=self_project, self_output=self_output, cross_query=cross_query,
        cross_keyval=cross_keyval, cross_output=cross_output, time_project=time_project,
        time_output=time_output, feed_up=feed_up, feed_down=feed_down,
    ))
    other = lax.ppermute(packed, HALF, [(0, 1), (1, 0)])
    full = lax.all_gather(jnp.stack([packed, other]), CUBE, axis=0, tiled=False)
    video_in, text_embed, other = lax.optimization_barrier((video_in, text_embed, other))
    x = to_slot(video_in.reshape(FR_DEV, -1, C), half, space)
    text = to_slot(text_embed.reshape(FR_DEV, -1, CTX), half, space)
    x, text, full = lax.optimization_barrier((x, text, full))
    cotangent, full = lax.optimization_barrier((cotangent, full))
    now = unpacked(
        unpack_kernel,
        [(9 * C, C), (9 * C, C), (TEMB, 2 * C), (C, 3 * C), (C, C), (C, C), (CTX, 2 * C), (C, C),
         (C, 3 * C), (C, C)],
        half_vec, full,
    )
    cot = to_slot(cotangent.reshape(FR_DEV, -1, C), half, space)
    w = Weights(*now, None, None)
    temb = meta_slot(time_embed.reshape(FR_DEV, 1, TEMB), space)
    usable = meta_slot(text_mask.reshape(FR_DEV, 1, TEXT), space)[0] == 1
    temb_act = jax.nn.silu(temb.astype(SINGLE)).astype(NARROW)
    bias, one_hot = time_setup(video_mask, video_number, bucket_index, bias_table, half)
    gmat = group_matrix()

    temb_act = jnp.broadcast_to(temb_act, (8, TEMB))
    conv_out, sec1, cols1, cols2, stats, film = conv_block(
        x, w.conv_first, w.conv_second, temb_act, w.film_weight, gains, gmat
    )
    proj, mix, lse, sec2, text_kv, cq, cmix, clse, sec3, time_proj = attn_block(
        sec1, gains, w.self_project, w.self_output, text, usable[None, :], w.cross_keyval,
        w.cross_query, w.cross_output, w.time_project,
    )
    time_proj, cot, full = lax.optimization_barrier((time_proj, cot, full))
    time_qkv = swap_frames(time_proj, PIX // 16)
    w_up, w_down = unpacked(unpack_late_kernel, [(C, FF), (FF, C)], half_vec, full)
    time_low, time_mix_t, time_lse = time_block(time_qkv, bias)
    time_mix = swap_frames(time_low, PIX // 16).reshape(PIX, C)
    result, carried, grad_time_mix, packed, gain_a = feed_block(
        sec3, time_mix, cot, gains, w.time_output, w_up, w_down
    )
    grad_mix_t = swap_frames(grad_time_mix, PIX // 16)
    chip_down = chip_sum(packed, core)
    chip_down, grad_mix_t = lax.optimization_barrier((chip_down, grad_mix_t))
    down = chip_swap(chip_down)
    grad_qkv_t, bias_grad = time_back_block(time_qkv, bias.reshape(HEADS, 128, 128).transpose(0, 2, 1).reshape(HEADS * 128, 128), time_mix_t, time_lse, grad_mix_t)
    grad_qkv_t, down = lax.optimization_barrier((grad_qkv_t, down))
    grad_time_proj = swap_frames(grad_qkv_t, PIX // 16).reshape(PIX, 3 * C)
    grad_time_proj, result, down = lax.optimization_barrier((grad_time_proj, result, down))
    block_out = both_slots(*send_back(result, half), space).reshape(video_in.shape)
    small = bias_grad.transpose(2, 1, 0)
    grad_table = jnp.dot(one_hot.T, small.reshape(-1, HEADS), precision=PRECISE)
    carried, packed, gain_b = cross_back(
        carried, grad_time_proj, sec3, sec2, cq, cmix, clse, text_kv, usable[:, None], text, gains,
        w.time_project, w.cross_output, w.cross_query,
    )
    carried, packed, block_out, down, grad_table = lax.optimization_barrier(
        (carried, packed, block_out, down, grad_table)
    )
    down = reduce_half(down, half_vec)
    chip_middle = chip_sum(packed, core)
    carried, chip_middle = lax.optimization_barrier((carried, chip_middle))
    middle = chip_swap(chip_middle)
    carried, packed, gain_c = self_back_block(
        carried, sec1, proj, mix, lse, gains, w.self_project, w.self_output
    )
    packed, back_second = second_weight(carried, cols2, packed)
    chip_upper = chip_sum(packed, core)
    back_second, middle, chip_upper = lax.optimization_barrier((back_second, middle, chip_upper))
    middle = reduce_half(middle, half_vec)
    upper = chip_swap(chip_upper)
    _, back_first, sums_d = second_back(
        back_second, conv_out, stats, film, gains, gmat, w.conv_second
    )
    grad_x, sums_e = first_back(carried, x, stats, gains, gmat, w.conv_first, back_first)
    own, other = send_back(grad_x, half)
    small_got = small_swap(temb_act, sums_d, sums_e, gain_a, gain_b, gain_c, grad_table)
    back_first, upper, grad_x = lax.optimization_barrier((back_first, upper, grad_x))
    packed = first_weight(cols1, back_first)
    packed, small_got, own = lax.optimization_barrier((packed, small_got, own))
    chip_first = chip_sum(packed, core)
    upper = reduce_half(upper, half_vec)
    first = chip_swap(chip_first)
    small_got, other = lax.optimization_barrier((small_got, other))
    film_own, film_got, small = small_settle(small_got, half_vec)
    input_grad = both_slots(own, other, space).reshape(video_in.shape)
    first = reduce_half(first, half_vec)
    gain_sum = small[2:8, :C].T
    out = finish(*down, *middle, *upper, *first, film_own, film_got)
    return (
        block_out, input_grad, gain_sum, small[8, : NB * HEADS].reshape(NB, HEADS),
        out.conv_first, out.conv_second, out.film_weight, out.self_project, out.self_output,
        out.cross_query, out.cross_keyval, out.cross_output, out.time_project, out.time_output,
        out.feed_up, out.feed_down,
    )


def fast_solution(mesh):
    split = Mesh(mesh.devices.reshape(2, 4, 2, 2), WORLD)
    frames = (HALF, QUAD, CORE)
    image = P(None, frames, SPACE, None, None)
    weight = P(frames, SPACE)
    placed = (
        image, P(None, frames, None), P(None, frames, SPACE, None), P(None, frames, None),
        P(), P(), P(), P(), P(),
    ) + (weight,) * 12 + (image,)
    return jax.shard_map(
        fast_shards, mesh=split, in_specs=placed,
        out_specs=(image, image, P(), P()) + (weight,) * 12, check_vma=False,
    )


def solution(mesh):
    if mesh.shape[FRAME] == GROUP_LEN and mesh.shape[SPACE] == FR_DEV:
        return fast_solution(mesh)
    placed = (
        P(None, FRAME, SPACE, None, None),
        P(None, FRAME, None),
        P(None, FRAME, SPACE, None),
        P(None, FRAME, None),
        P(),
        P(),
        P(),
        P(),
        P(),
        P(FRAME, SPACE),
        P(FRAME, SPACE),
        P(FRAME, SPACE),
        P(FRAME, SPACE),
        P(FRAME, SPACE),
        P(FRAME, SPACE),
        P(FRAME, SPACE),
        P(FRAME, SPACE),
        P(FRAME, SPACE),
        P(FRAME, SPACE),
        P(FRAME, SPACE),
        P(FRAME, SPACE),
        P(None, FRAME, SPACE, None, None),
    )
    return jax.shard_map(
        shards,
        mesh=mesh,
        in_specs=placed,
        out_specs=(
            P(None, FRAME, SPACE, None, None),
            P(None, FRAME, SPACE, None, None),
            P(),
            P(),
            P(FRAME, SPACE),
            P(FRAME, SPACE),
            P(FRAME, SPACE),
            P(FRAME, SPACE),
            P(FRAME, SPACE),
            P(FRAME, SPACE),
            P(FRAME, SPACE),
            P(FRAME, SPACE),
            P(FRAME, SPACE),
            P(FRAME, SPACE),
            P(FRAME, SPACE),
            P(FRAME, SPACE),
        ),
        check_vma=False,
    )
```

```python
from typing import Any, NamedTuple

import jax
import jax.numpy as jnp
from jax import lax
from jax.experimental import pallas as pl
from jax.experimental.pallas import tpu as pltpu
from jax.sharding import Mesh
from jax.sharding import PartitionSpec as P

C = 320
HEADS = 5
HEAD = 64
GROUPS = 32
CTX = 1024
TEMB = 1280
TEXT = 128
IMG_H = 24
IMG_W = 48
FR_DEV = 2
GROUP_LEN = 16
NB = 32
FF = 1280
GELU_A = 0.7978845608028654
GELU_B = 0.044715


FRAME = "frame"
SPACE = "space"
HALF = "half"
QUAD = "quad"
CORE = "core"
EPSILON = 1e-05
MASKED = -1e30
SINGLE = jnp.float32
NARROW = jnp.bfloat16
PRECISE = lax.Precision.HIGHEST


def with_halo(block, sides, width):
    for axis, dim in sides:
        count = lax.axis_size(axis)
        forward = [(i, i + 1) for i in range(count - 1)]
        backward = [(target, source) for source, target in forward]
        low = lax.ppermute(
            lax.slice_in_dim(block, block.shape[dim] - width, None, axis=dim), axis, forward
        )
        high = lax.ppermute(lax.slice_in_dim(block, 0, width, axis=dim), axis, backward)
        block = jnp.concatenate([low, block, high], axis=dim)
    return block


def collect(item_one, item_two, item_three):
    row_full = (
        lax.all_gather(item_one, FRAME, axis=0, tiled=True),
        lax.all_gather(item_two, FRAME, axis=0, tiled=True),
        lax.all_gather(item_three, FRAME, axis=0, tiled=True),
    )
    return (
        lax.all_gather(row_full[0], SPACE, axis=1, tiled=True),
        lax.all_gather(row_full[1], SPACE, axis=1, tiled=True),
        lax.all_gather(row_full[2], SPACE, axis=1, tiled=True),
    )


def settle(item_one, item_two, item_three):
    column_sums = (
        lax.psum_scatter(
            item_one.astype(jnp.bfloat16), SPACE, scatter_dimension=1, tiled=True
        ).astype(jnp.float32),
        lax.psum_scatter(
            item_two.astype(jnp.bfloat16), SPACE, scatter_dimension=1, tiled=True
        ).astype(jnp.float32),
        lax.psum_scatter(
            item_three.astype(jnp.bfloat16), SPACE, scatter_dimension=1, tiled=True
        ).astype(jnp.float32),
    )
    return (
        lax.psum_scatter(
            column_sums[0].astype(jnp.bfloat16), FRAME, scatter_dimension=0, tiled=True
        ).astype(jnp.float32),
        lax.psum_scatter(
            column_sums[1].astype(jnp.bfloat16), FRAME, scatter_dimension=0, tiled=True
        ).astype(jnp.float32),
        lax.psum_scatter(
            column_sums[2].astype(jnp.bfloat16), FRAME, scatter_dimension=0, tiled=True
        ).astype(jnp.float32),
    )


def space_sums(item_one, item_two):
    return lax.psum((item_one, item_two), SPACE)


def columns_of(padded):
    height_here = padded.shape[1] - 2
    pieces = [
        padded[:, row_off : row_off + height_here, col_off : col_off + IMG_W, :]
        for row_off in range(3)
        for col_off in range(3)
    ]
    return jnp.concatenate(pieces, axis=-1).reshape(-1, 9 * C)


def convolve(activation, weight):
    slot_count, rows_here = (activation.shape[0], activation.shape[1])
    image = activation.reshape(slot_count, rows_here // IMG_W, IMG_W, C)
    rimmed = with_halo(image, ((SPACE, 1),), 1)
    padded = jnp.pad(rimmed, ((0, 0), (0, 0), (1, 1), (0, 0)))
    summed = jnp.dot(columns_of(padded), weight, preferred_element_type=SINGLE)
    return (summed.reshape(slot_count, rows_here, C), padded)


def convolve_back(grad_low, weight):
    flipped = weight.reshape(3, 3, C, C)[::-1, ::-1].transpose(0, 1, 3, 2).reshape(9 * C, C)
    summed, padded = convolve(grad_low, flipped)
    return summed


def weight_grad(left, right):
    return lax.dot_general(
        left.reshape(-1, left.shape[-1]),
        right.reshape(-1, right.shape[-1]),
        (((0,), (0,)), ((), ())),
        preferred_element_type=SINGLE,
    )


def back_project(grad_low, weight):
    return jnp.einsum("...o,io->...i", grad_low, weight, preferred_element_type=SINGLE)


def layer_norm(layer, gain):
    centered = layer - jnp.mean(layer, axis=-1, keepdims=True)
    return (
        centered * lax.rsqrt(jnp.mean(centered * centered, axis=-1, keepdims=True) + EPSILON) * gain
    )


def group_forward(layer):
    slot_count, rows_here = (layer.shape[0], layer.shape[1])
    grouped = layer.reshape(slot_count, rows_here, GROUPS, C // GROUPS)
    summed, squares = space_sums(
        jnp.sum(grouped, axis=(1, 3)), jnp.sum(grouped * grouped, axis=(1, 3))
    )
    members = IMG_H * IMG_W * (C // GROUPS)
    center = summed / members
    spread = lax.rsqrt(squares / members - center * center + EPSILON)
    normed = (grouped - center[:, None, :, None]) * spread[:, None, :, None]
    return (normed.reshape(slot_count, rows_here, C), spread)


def group_backward(normed, spread, upstream):
    slot_count, rows_here = (normed.shape[0], normed.shape[1])
    grad_groups = upstream.reshape(slot_count, rows_here, GROUPS, C // GROUPS)
    norm_groups = normed.reshape(slot_count, rows_here, GROUPS, C // GROUPS)
    summed, crossed = space_sums(
        jnp.sum(grad_groups, axis=(1, 3)), jnp.sum(grad_groups * norm_groups, axis=(1, 3))
    )
    members = IMG_H * IMG_W * (C // GROUPS)
    result = spread[:, None, :, None] * (
        grad_groups
        - summed[:, None, :, None] / members
        - norm_groups * crossed[:, None, :, None] / members
    )
    return result.reshape(slot_count, rows_here, C)


def masked_scores(queries, key_rows, usable):
    scores = jnp.einsum(
        "qhd,khd->hqk", queries, key_rows, preferred_element_type=SINGLE
    ) * HEAD ** (-0.5)
    return jnp.where(usable[None, None, :], scores, MASKED)


def attend_forward(queries, key_rows, value_rows, usable):
    scores = masked_scores(queries, key_rows, usable)
    highest = jnp.max(scores, axis=-1, keepdims=True)
    log_total = highest + jnp.log(jnp.sum(jnp.exp(scores - highest), axis=-1, keepdims=True))
    attn_probs = jnp.exp(scores - log_total).astype(NARROW)
    mixture = jnp.einsum(
        "hqk,khd->qhd", attn_probs, value_rows, preferred_element_type=SINGLE
    ).astype(NARROW)
    return (mixture, log_total[..., 0])


def attend_backward(queries, key_rows, value_rows, usable, log_total, grad_mixture):
    scores = masked_scores(queries, key_rows, usable)
    attn_probs = jnp.exp(scores - log_total[..., None])
    grad_probs = jnp.einsum("qhd,khd->hqk", grad_mixture, value_rows, preferred_element_type=SINGLE)
    row_inner = jnp.sum(grad_probs * attn_probs, axis=-1, keepdims=True)
    grad_scores = (attn_probs * (grad_probs - row_inner)).astype(NARROW)
    grad_queries = jnp.einsum(
        "hqk,khd->qhd", grad_scores, key_rows, preferred_element_type=SINGLE
    ) * HEAD ** (-0.5)
    grad_keys = jnp.einsum(
        "hqk,qhd->khd", grad_scores, queries, preferred_element_type=SINGLE
    ) * HEAD ** (-0.5)
    grad_values = jnp.einsum(
        "hqk,qhd->khd", attn_probs.astype(NARROW), grad_mixture, preferred_element_type=SINGLE
    )
    return (grad_queries, grad_keys, grad_values)


def time_scores(queries, gathered, time_bias, allowed):
    key_rows = gathered[..., :C].reshape(gathered.shape[0], gathered.shape[1], HEADS, HEAD)
    scores = (
        jnp.einsum("rhd,grhd->rhg", queries, key_rows, preferred_element_type=SINGLE)
        * HEAD ** (-0.5)
        + time_bias[None]
    )
    return (jnp.where(allowed[None, None, :], scores, MASKED), key_rows)


def shards(
    video_in,
    time_embed,
    text_embed,
    text_mask,
    video_mask,
    video_number,
    bucket_index,
    norm_gains,
    bias_table,
    conv_first,
    conv_second,
    film_weight,
    self_project,
    self_output,
    cross_query,
    cross_keyval,
    cross_output,
    time_project,
    time_output,
    feed_up,
    feed_down,
    cotangent,
):
    height_here = video_in.shape[2]
    rows_here = height_here * IMG_W
    text_here = text_embed.shape[2]
    frame_count = video_mask.shape[1]
    frame_index = lax.axis_index(FRAME)
    group_place = frame_index % GROUP_LEN
    heads_view = (FR_DEV, rows_here, HEADS, HEAD)
    every_key = jnp.ones((IMG_H * IMG_W,), jnp.bool_)
    frame_ids = jnp.arange(frame_count)
    place_ids = jnp.arange(GROUP_LEN)
    bucket_row = jnp.sum(jnp.where((place_ids == group_place)[:, None], bucket_index, 0), axis=0)
    key_buckets = jnp.sum(
        jnp.where((frame_ids % GROUP_LEN)[:, None] == place_ids[None, :], bucket_row[None, :], 0),
        axis=1,
    )
    key_table = (key_buckets[:, None] == jnp.arange(NB)[None, :]).astype(SINGLE)
    time_bias = jnp.dot(key_table, bias_table, precision=PRECISE, preferred_element_type=SINGLE).T

    def allowed_for(live_slot, number_slot):
        chooser = frame_ids[:, None] == frame_ids[None, :]
        live_keys = jnp.sum(jnp.where(chooser, live_slot[None, :], 0), axis=1)
        number_keys = jnp.sum(jnp.where(chooser, number_slot[None, :], 0), axis=1)
        own_frame = frame_ids == frame_index
        live_own = jnp.sum(jnp.where(own_frame, live_slot, 0))
        number_own = jnp.sum(jnp.where(own_frame, number_slot, 0))
        same_group = frame_ids // GROUP_LEN == frame_index // GROUP_LEN
        together = (live_keys == 1) & (live_own == 1) & (number_keys == number_own)
        return same_group & (together | (frame_ids == frame_index))

    def spread_keys(own_pair):
        return lax.all_gather(own_pair, FRAME, axis=0, tiled=True)

    def return_keys(spread_grads):
        return lax.psum_scatter(
            spread_grads.astype(jnp.bfloat16), FRAME, scatter_dimension=0, tiled=True
        ).astype(jnp.float32)

    def gather_keys(frame_pair, text_pair):
        return (
            lax.all_gather(frame_pair, SPACE, axis=0, tiled=True),
            lax.all_gather(text_pair, SPACE, axis=0, tiled=True),
        )

    def scatter_keys(frame_grads, text_grads):
        return (
            lax.psum_scatter(
                frame_grads.astype(jnp.bfloat16), SPACE, scatter_dimension=0, tiled=True
            ).astype(jnp.float32),
            lax.psum_scatter(
                text_grads.astype(jnp.bfloat16), SPACE, scatter_dimension=0, tiled=True
            ).astype(jnp.float32),
        )

    resid = video_in.reshape(FR_DEV, rows_here, C).astype(SINGLE)
    conv_one, film_full, conv_two = collect(conv_first, film_weight, conv_second)
    temb_act = jax.nn.silu(time_embed.reshape(FR_DEV, TEMB).astype(SINGLE)).astype(NARROW)
    film_all = jnp.dot(temb_act, film_full, preferred_element_type=SINGLE)
    film_scale = 1.0 + film_all[:, None, :C]
    film_shift = film_all[:, None, C:]
    normed_one, spread_one = group_forward(resid)
    pre_one = normed_one * norm_gains[:, 0]
    conv_out, pad_one = convolve(jax.nn.silu(pre_one).astype(NARROW), conv_one)
    hidden = conv_out * film_scale + film_shift
    normed_two, spread_two = group_forward(hidden)
    pre_two = normed_two * norm_gains[:, 1]
    branch_two, pad_two = convolve(jax.nn.silu(pre_two).astype(NARROW), conv_two)
    section_one = resid + branch_two
    kv_weight, qkv_weight, self_weight = collect(cross_keyval, self_project, self_output)
    text_kv = (
        jnp.dot(
            text_embed.reshape(FR_DEV * text_here, CTX), kv_weight, preferred_element_type=SINGLE
        )
        .astype(NARROW)
        .reshape(FR_DEV, text_here, 2 * C)
    )
    self_in = layer_norm(section_one, norm_gains[:, 2]).astype(NARROW)
    self_proj = jnp.dot(self_in, qkv_weight, preferred_element_type=SINGLE).astype(NARROW)

    def self_slot(inputs):
        proj_slot, text_slot = inputs
        frame_kv, text_full = gather_keys(proj_slot[:, C:], text_slot)
        mixture, log_total = attend_forward(
            proj_slot[:, :C].reshape(rows_here, HEADS, HEAD),
            frame_kv[:, :C].reshape(-1, HEADS, HEAD),
            frame_kv[:, C:].reshape(-1, HEADS, HEAD),
            every_key,
        )
        return (mixture, log_total, text_full)

    self_mixed, self_lse, text_all = lax.map(self_slot, (self_proj, text_kv))
    self_mixed = self_mixed.reshape(FR_DEV, rows_here, C)
    section_two = section_one + jnp.dot(self_mixed, self_weight, preferred_element_type=SINGLE)
    query_weight, cross_weight, time_weight = collect(cross_query, cross_output, time_project)
    cross_in = layer_norm(section_two, norm_gains[:, 3]).astype(NARROW)
    cross_queries = (
        jnp.dot(cross_in, query_weight, preferred_element_type=SINGLE)
        .astype(NARROW)
        .reshape(heads_view)
    )
    text_usable = text_mask.reshape(FR_DEV, TEXT) == 1
    text_keys = text_all[..., :C].reshape(FR_DEV, TEXT, HEADS, HEAD)
    text_values = text_all[..., C:].reshape(FR_DEV, TEXT, HEADS, HEAD)
    cross_mixed, cross_lse = jax.vmap(attend_forward)(
        cross_queries, text_keys, text_values, text_usable
    )
    cross_mixed = cross_mixed.reshape(FR_DEV, rows_here, C)
    section_three = section_two + jnp.dot(cross_mixed, cross_weight, preferred_element_type=SINGLE)
    time_in = layer_norm(section_three, norm_gains[:, 4]).astype(NARROW)
    time_proj = jnp.dot(time_in, time_weight, preferred_element_type=SINGLE).astype(NARROW)

    def time_slot(inputs):
        proj_slot, live_slot, number_slot = inputs
        gathered = spread_keys(proj_slot[None, :, C:])
        queries = proj_slot[:, :C].reshape(rows_here, HEADS, HEAD)
        scores, key_rows = time_scores(
            queries, gathered, time_bias, allowed_for(live_slot, number_slot)
        )
        value_rows = gathered[..., C:].reshape(key_rows.shape)
        highest = jnp.max(scores, axis=-1, keepdims=True)
        log_total = highest + jnp.log(jnp.sum(jnp.exp(scores - highest), axis=-1, keepdims=True))
        attn_probs = jnp.exp(scores - log_total).astype(NARROW)
        mixture = jnp.einsum(
            "rhg,grhd->rhd", attn_probs, value_rows, preferred_element_type=SINGLE
        ).astype(NARROW)
        return (mixture, log_total[..., 0])

    time_mixed, time_lse = lax.map(time_slot, (time_proj, video_mask, video_number))
    time_mixed = time_mixed.reshape(FR_DEV, rows_here, C)
    out_weight, inner_weight, outer_weight = collect(time_output, feed_up, feed_down)
    section_four = section_three + jnp.dot(time_mixed, out_weight, preferred_element_type=SINGLE)
    feed_in = layer_norm(section_four, norm_gains[:, 5]).astype(NARROW)
    lifted = jnp.dot(feed_in, inner_weight, preferred_element_type=SINGLE)
    activated = jax.nn.gelu(lifted, approximate=True).astype(NARROW)
    result = section_four + jnp.dot(activated, outer_weight, preferred_element_type=SINGLE)
    block_out = result.astype(NARROW).reshape(video_in.shape)
    carried = cotangent.reshape(FR_DEV, rows_here, C).astype(SINGLE)
    back_feed = carried.astype(NARROW)
    grad_down = weight_grad(activated, back_feed)
    grad_act = back_project(back_feed, outer_weight)
    value_gelu, pull_gelu = jax.vjp(lambda layer: jax.nn.gelu(layer, approximate=True), lifted)
    grad_lifted = pull_gelu(grad_act)[0].astype(NARROW)
    grad_up = weight_grad(feed_in, grad_lifted)
    value_norm, pull_norm = jax.vjp(layer_norm, section_four, norm_gains[:, 5])
    norm_part, gain_five = pull_norm(back_project(grad_lifted, inner_weight))
    carried = carried + norm_part
    back_time = carried.astype(NARROW)
    grad_time_out = weight_grad(time_mixed, back_time)
    grad_time_mixed = back_project(back_time, out_weight).astype(NARROW).reshape(heads_view)
    down_grads = settle(grad_time_out, grad_up, grad_down)

    def time_back(inputs):
        proj_slot, live_slot, number_slot, lse_slot, grad_slot = inputs
        gathered = spread_keys(proj_slot[None, :, C:])
        queries = proj_slot[:, :C].reshape(rows_here, HEADS, HEAD)
        scores, key_rows = time_scores(
            queries, gathered, time_bias, allowed_for(live_slot, number_slot)
        )
        value_rows = gathered[..., C:].reshape(key_rows.shape)
        attn_probs = jnp.exp(scores - lse_slot[..., None])
        grad_probs = jnp.einsum(
            "rhd,grhd->rhg", grad_slot, value_rows, preferred_element_type=SINGLE
        )
        row_inner = jnp.sum(grad_probs * attn_probs, axis=-1, keepdims=True)
        grad_scores = (attn_probs * (grad_probs - row_inner)).astype(NARROW)
        grad_queries = jnp.einsum(
            "rhg,grhd->rhd", grad_scores, key_rows, preferred_element_type=SINGLE
        ) * HEAD ** (-0.5)
        grad_keys = jnp.einsum(
            "rhg,rhd->grhd", grad_scores, queries, preferred_element_type=SINGLE
        ) * HEAD ** (-0.5)
        grad_values = jnp.einsum(
            "rhg,rhd->grhd", attn_probs.astype(NARROW), grad_slot, preferred_element_type=SINGLE
        )
        key_count = key_rows.shape[0]
        spread_grads = jnp.concatenate(
            [
                grad_keys.reshape(key_count, rows_here, C),
                grad_values.reshape(key_count, rows_here, C),
            ],
            -1,
        )
        own_grads = return_keys(spread_grads)[0]
        bias_grad = jnp.sum(grad_scores.astype(SINGLE), axis=0)
        return (jnp.concatenate([grad_queries.reshape(rows_here, C), own_grads], -1), bias_grad)

    grad_time_proj, bias_grads = lax.map(
        time_back, (time_proj, video_mask, video_number, time_lse, grad_time_mixed)
    )
    grad_table = jnp.dot(
        key_table.T, jnp.sum(bias_grads, axis=0).T, precision=PRECISE, preferred_element_type=SINGLE
    )
    grad_time_proj = grad_time_proj.astype(NARROW)
    grad_time_qkv = weight_grad(time_in, grad_time_proj)
    value_norm, pull_norm = jax.vjp(layer_norm, section_three, norm_gains[:, 4])
    norm_part, gain_four = pull_norm(back_project(grad_time_proj, time_weight))
    carried = carried + norm_part
    back_cross = carried.astype(NARROW)
    grad_cross_out = weight_grad(cross_mixed, back_cross)
    grad_cross_mixed = back_project(back_cross, cross_weight).astype(NARROW).reshape(heads_view)
    grad_cquery, grad_tkeys, grad_tvalues = jax.vmap(attend_backward)(
        cross_queries, text_keys, text_values, text_usable, cross_lse, grad_cross_mixed
    )
    grad_cquery = grad_cquery.reshape(FR_DEV, rows_here, C).astype(NARROW)
    grad_cross_q = weight_grad(cross_in, grad_cquery)
    value_norm, pull_norm = jax.vjp(layer_norm, section_two, norm_gains[:, 3])
    norm_part, gain_three = pull_norm(back_project(grad_cquery, query_weight))
    carried = carried + norm_part
    text_grads = jnp.concatenate(
        [grad_tkeys.reshape(FR_DEV, TEXT, C), grad_tvalues.reshape(FR_DEV, TEXT, C)], -1
    )
    middle_grads = settle(grad_cross_q, grad_cross_out, grad_time_qkv)
    back_self = carried.astype(NARROW)
    grad_self_out = weight_grad(self_mixed, back_self)
    grad_self_mixed = back_project(back_self, self_weight).astype(NARROW).reshape(heads_view)

    def self_back(inputs):
        proj_slot, text_slot, lse_slot, grad_slot, text_grad_slot = inputs
        frame_kv, text_again = gather_keys(proj_slot[:, C:], text_slot)
        grad_queries, grad_keys, grad_values = attend_backward(
            proj_slot[:, :C].reshape(rows_here, HEADS, HEAD),
            frame_kv[:, :C].reshape(-1, HEADS, HEAD),
            frame_kv[:, C:].reshape(-1, HEADS, HEAD),
            every_key,
            lse_slot,
            grad_slot,
        )
        frame_grads = jnp.concatenate([grad_keys.reshape(-1, C), grad_values.reshape(-1, C)], -1)
        own_frame, own_text = scatter_keys(frame_grads, text_grad_slot)
        return (jnp.concatenate([grad_queries.reshape(rows_here, C), own_frame], -1), own_text)

    grad_self_proj, grad_text_kv = lax.map(
        self_back, (self_proj, text_kv, self_lse, grad_self_mixed, text_grads)
    )
    grad_self_proj = grad_self_proj.astype(NARROW)
    grad_self_qkv = weight_grad(self_in, grad_self_proj)
    grad_keyval = weight_grad(
        text_embed.reshape(FR_DEV * text_here, CTX), grad_text_kv.astype(NARROW)
    )
    value_norm, pull_norm = jax.vjp(layer_norm, section_one, norm_gains[:, 2])
    norm_part, gain_two = pull_norm(back_project(grad_self_proj, qkv_weight))
    carried = carried + norm_part
    upper_grads = settle(grad_keyval, grad_self_qkv, grad_self_out)
    back_conv = carried.astype(NARROW)
    grad_conv_two = weight_grad(columns_of(pad_two), back_conv)
    grad_act_two = convolve_back(back_conv, conv_two)
    value_silu, pull_silu = jax.vjp(jax.nn.silu, pre_two)
    grad_pre_two = pull_silu(grad_act_two)[0]
    gain_one = jnp.sum(grad_pre_two * normed_two, axis=(0, 1))
    grad_hidden = group_backward(normed_two, spread_two, grad_pre_two * norm_gains[:, 1])
    grad_film = jnp.concatenate(
        [jnp.sum(grad_hidden * conv_out, axis=1), jnp.sum(grad_hidden, axis=1)], -1
    )
    grad_film_w = jnp.dot(
        temb_act.astype(SINGLE).T, grad_film, precision=PRECISE, preferred_element_type=SINGLE
    )
    back_first = (grad_hidden * film_scale).astype(NARROW)
    grad_conv_one = weight_grad(columns_of(pad_one), back_first)
    grad_act_one = convolve_back(back_first, conv_one)
    value_silu, pull_silu = jax.vjp(jax.nn.silu, pre_one)
    grad_pre_one = pull_silu(grad_act_one)[0]
    gain_zero = jnp.sum(grad_pre_one * normed_one, axis=(0, 1))
    carried = carried + group_backward(normed_one, spread_one, grad_pre_one * norm_gains[:, 0])
    input_grad = carried.astype(NARROW).reshape(video_in.shape)
    lower_grads = settle(grad_conv_one, grad_film_w, grad_conv_two)
    gain_stack = jnp.stack(
        [gain_zero, gain_one, gain_two, gain_three, gain_four, gain_five], axis=1
    )
    small_sums = lax.psum((gain_stack, grad_table), (FRAME, SPACE))
    return (
        block_out,
        input_grad,
        small_sums[0],
        small_sums[1],
        lower_grads[0],
        lower_grads[2],
        lower_grads[1],
        upper_grads[1],
        upper_grads[2],
        middle_grads[0],
        upper_grads[0],
        middle_grads[1],
        middle_grads[2],
        down_grads[0],
        down_grads[1],
        down_grads[2],
    )


PIX = IMG_H * IMG_W
CUBE = (QUAD, CORE, SPACE)
CHIPS = (QUAD, SPACE)
TRIO = (HALF, CORE, SPACE)
WORLD = (HALF, QUAD, CORE, SPACE)
SCALE = HEAD ** (-0.5)


def moves(turn):
    return [
        (4 * a + 2 * c + b, 4 * (b ^ turn) + 2 * c + (a ^ c))
        for a in range(2)
        for c in range(2)
        for b in range(2)
    ]


def back(pairs):
    return [(target, source) for source, target in pairs]


def pick(flag, pair):
    return jnp.where(flag == 0, pair[0], pair[1])


def to_slot(block, half, space):
    own = lax.ppermute(pick(space, block), TRIO, moves(0))
    other = lax.ppermute(pick(1 - space, block), TRIO, moves(1))
    return jnp.concatenate(
        [jnp.where(half == 0, own, other), jnp.where(half == 0, other, own)], axis=0
    )


def send_back(frame, half):
    pieces = frame.reshape((2, frame.shape[0] // 2) + frame.shape[1:])
    own = lax.ppermute(pick(half, pieces), TRIO, back(moves(0)))
    other = lax.ppermute(pick(1 - half, pieces), TRIO, back(moves(1)))
    return own, other


def both_slots(own, other, space):
    return jnp.stack([jnp.where(space == 0, own, other), jnp.where(space == 0, other, own)])


def meta_slot(block, space):
    return lax.ppermute(pick(space, block), TRIO, moves(0))


class Weights(NamedTuple):
    conv_first: Any
    conv_second: Any
    film_weight: Any
    self_project: Any
    self_output: Any
    cross_query: Any
    cross_keyval: Any
    cross_output: Any
    time_project: Any
    time_output: Any
    feed_up: Any
    feed_down: Any


def mm(a, b):
    return jnp.dot(a, b, preferred_element_type=SINGLE)


VMEM_BYTES = 58 * 1024 * 1024
STEP = 384
STEPS = PIX // STEP
NT = (((1,), (1,)), ((), ()))
TN = (((0,), (0,)), ((), ()))


def nt(a, b):
    return lax.dot_general(a, b, NT, preferred_element_type=SINGLE)


def tn(a, b):
    return lax.dot_general(a, b, TN, preferred_element_type=SINGLE)


def kernel_call(body, outs, scratch=(), flops=10**9):
    return pl.pallas_call(
        body,
        out_shape=[jax.ShapeDtypeStruct(s, d) for s, d in outs],
        scratch_shapes=[pltpu.VMEM(s, d) for s, d in scratch],
        compiler_params=pltpu.CompilerParams(vmem_limit_bytes=VMEM_BYTES),
        cost_estimate=pl.CostEstimate(flops=flops, bytes_accessed=min(flops, 10**7) // 100, transcendentals=0),
    )


def sweep(count, body):
    lax.fori_loop(0, count, lambda i, c: (body(i), c)[1], 0)


def rows_at(r):
    return pl.ds(pl.multiple_of(r * STEP, STEP), STEP)


def group_matrix():
    lanes = jnp.arange(C) // (C // GROUPS)
    return (lanes[:, None] == lanes[None, :]).astype(SINGLE)


def grouped(row, gmat):
    wide = jnp.broadcast_to(row, (8, C))
    return lax.dot_general(
        wide, gmat, (((1,), (0,)), ((), ())), precision=PRECISE, preferred_element_type=SINGLE
    )[:1]


def edge_masks(rows):
    col = lax.broadcasted_iota(jnp.int32, (rows, C), 0) % IMG_W
    return col != 0, col != IMG_W - 1


def spread_columns(cols_ref, start, act):
    not_first, not_last = edge_masks(STEP)
    left = jnp.where(not_first, pltpu.roll(act, 1, 0), 0.0)
    right = jnp.where(not_last, pltpu.roll(act, STEP - 1, 0), 0.0)
    cols_ref[pl.ds(start, STEP), :] = jnp.concatenate(
        [left.astype(NARROW), act.astype(NARROW), right.astype(NARROW)], axis=1
    )


def conv_rows(cols_ref, w_ref, start):
    total = None
    for i in range(3):
        part = mm(cols_ref[pl.ds(start + IMG_W * i, STEP), :], w_ref[3 * C * i : 3 * C * (i + 1), :])
        total = part if total is None else total + part
    return total


def gn_stats(total, square, gmat):
    members = PIX * (C // GROUPS)
    center = grouped(total, gmat) / members
    return center, lax.rsqrt(grouped(square, gmat) / members - center * center + EPSILON)


def unpack_tall(half, full_ref, out_ref, at, rows, cols):
    parts = BAND // cols
    tall = rows // parts
    for quad in range(4):
        pieces = []
        for frame in range(4 * quad, 4 * quad + 4):
            place = half if frame < 8 else 1 - half
            sides = [
                full_ref[2 * (frame % 8) + s, place, at : at + tall, :].astype(SINGLE) for s in range(2)
            ]
            pieces += [
                jnp.concatenate([side[:, cols * q : cols * (q + 1)] for side in sides], axis=1)
                for q in range(parts)
            ]
        out_ref[4 * rows * quad : 4 * rows * (quad + 1), :] = jnp.concatenate(pieces, axis=0).astype(NARROW)


def clear_border(cols_ref):
    border = jnp.zeros((IMG_W, 3 * C), NARROW)
    cols_ref[0:IMG_W, :] = border
    cols_ref[PIX + IMG_W :, :] = border


def conv_kernel(x_ref, w1_ref, w2_ref, temb_ref, wf_ref, gains_ref, gmat_ref,
                conv_out_ref, sec_ref, cols1_ref, cols2_ref, stats_ref, film_ref):
    film_ref[...] = mm(temb_ref[...], wf_ref[...])
    gmat = gmat_ref[...]
    clear_border(cols1_ref)
    clear_border(cols2_ref)
    total = jnp.zeros((1, C), SINGLE)
    square = jnp.zeros((1, C), SINGLE)
    for r in range(STEPS):
        x = x_ref[r * STEP : (r + 1) * STEP, :].astype(SINGLE)
        total += jnp.sum(x, axis=0, keepdims=True)
        square += jnp.sum(x * x, axis=0, keepdims=True)
    center, spread = gn_stats(total, square, gmat)
    stats_ref[0:1, :] = center
    stats_ref[1:2, :] = spread
    for r in range(STEPS):
        x = x_ref[r * STEP : (r + 1) * STEP, :].astype(SINGLE)
        pre = (x - center) * spread * gains_ref[0:1, :]
        spread_columns(cols1_ref, IMG_W + r * STEP, pre * (0.5 + 0.5 * jnp.tanh(0.5 * pre)))
    scale = 1.0 + film_ref[0:1, :C]
    shift = film_ref[0:1, C:]
    total = jnp.zeros((1, C), SINGLE)
    square = jnp.zeros((1, C), SINGLE)
    for r in range(STEPS):
        out = conv_rows(cols1_ref, w1_ref, r * STEP)
        conv_out_ref[r * STEP : (r + 1) * STEP, :] = out
        hidden = out * scale + shift
        total += jnp.sum(hidden, axis=0, keepdims=True)
        square += jnp.sum(hidden * hidden, axis=0, keepdims=True)
    center, spread = gn_stats(total, square, gmat)
    stats_ref[2:3, :] = center
    stats_ref[3:4, :] = spread
    for r in range(STEPS):
        hidden = conv_out_ref[r * STEP : (r + 1) * STEP, :] * scale + shift
        pre = (hidden - center) * spread * gains_ref[1:2, :]
        spread_columns(cols2_ref, IMG_W + r * STEP, pre * (0.5 + 0.5 * jnp.tanh(0.5 * pre)))
    for r in range(STEPS):
        out = conv_rows(cols2_ref, w2_ref, r * STEP)
        rows = slice(r * STEP, (r + 1) * STEP)
        sec_ref[rows, :] = x_ref[rows, :].astype(SINGLE) + out


def conv_block(x, w1, w2, temb, wf, gains, gmat):
    cols = (PIX + 2 * IMG_W, 3 * C)
    return kernel_call(
        conv_kernel,
        [((PIX, C), SINGLE), ((PIX, C), SINGLE), (cols, NARROW), (cols, NARROW), ((8, C), SINGLE), ((8, 2 * C), SINGLE)],
        flops=15 * 10**9,
    )(x, w1, w2, temb, wf, gains, gmat)


def ln_rows(layer, gain):
    centered = layer - jnp.mean(layer, axis=-1, keepdims=True)
    rstd = lax.rsqrt(jnp.mean(centered * centered, axis=-1, keepdims=True) + EPSILON)
    return centered * rstd, rstd


def with_ones(v):
    return jnp.concatenate([v, jnp.ones(v.shape, v.dtype)], axis=1)


def staged(count, front, rest):
    ahead = front(0)
    for i in range(count):
        now = ahead
        if i + 1 < count:
            ahead = front(i + 1)
        rest(i, now)


def head_lanes(h):
    return slice(h * HEAD, (h + 1) * HEAD)


def soft_values(scores, v_one):
    highest = jnp.max(scores, axis=-1, keepdims=True)
    both = mm(jnp.exp(scores - highest).astype(NARROW), v_one)
    total = both[:, HEAD : HEAD + 1]
    return both[:, :HEAD] / total, highest + jnp.log(total)


def self_kernel(sec1_ref, gains_ref, wqkv_ref, wso_ref, proj_ref, mix_ref, lse_ref, sec2_ref):
    hat, rstd = ln_rows(sec1_ref[...], None)
    proj_ref[...] = mm((hat * gains_ref[2:3, :]).astype(NARROW), wqkv_ref[...]).astype(NARROW)

    def front(i):
        h, r = divmod(i, STEPS)
        q = proj_ref[r * STEP : (r + 1) * STEP, head_lanes(h)] * jnp.bfloat16(SCALE)
        return nt(q, proj_ref[:, head_lanes(HEADS + h)])

    def rest(i, scores):
        h, r = divmod(i, STEPS)
        rows = slice(r * STEP, (r + 1) * STEP)
        mix, lse = soft_values(scores, with_ones(proj_ref[:, head_lanes(2 * HEADS + h)]))
        mix_ref[rows, head_lanes(h)] = mix
        lse_ref[rows, h : h + 1] = lse

    staged(HEADS * STEPS, front, rest)
    sec2_ref[...] = sec1_ref[...] + mm(mix_ref[...].astype(NARROW), wso_ref[...])


def cross_kernel(sec2_ref, gains_ref, text_ref, usable_ref, wkv_ref, wcq_ref, wco_ref, wtime_ref,
                 kv_ref, cq_ref, cmix_ref, clse_ref, sec3_ref, tproj_ref):
    kv_ref[...] = mm(text_ref[...], wkv_ref[...]).astype(NARROW)
    hat, rstd = ln_rows(sec2_ref[...], None)
    cq_ref[...] = mm((hat * gains_ref[3:4, :]).astype(NARROW), wcq_ref[...]).astype(NARROW)
    usable = jnp.broadcast_to(usable_ref[...], (PIX, TEXT)) == 1

    def front(h):
        return nt(cq_ref[:, head_lanes(h)] * jnp.bfloat16(SCALE), kv_ref[:, head_lanes(h)])

    def rest(h, scores):
        v = with_ones(kv_ref[:, head_lanes(HEADS + h)])
        mix, lse = soft_values(jnp.where(usable, scores, MASKED), v)
        cmix_ref[:, head_lanes(h)] = mix
        clse_ref[:, h : h + 1] = lse

    staged(HEADS, front, rest)
    sec3 = sec2_ref[...] + mm(cmix_ref[...].astype(NARROW), wco_ref[...])
    sec3_ref[...] = sec3
    hat, rstd = ln_rows(sec3, None)
    tproj_ref[...] = mm((hat * gains_ref[4:5, :]).astype(NARROW), wtime_ref[...]).astype(NARROW)


def attn_block(sec1, gains, wqkv, wso, text, usable, wkv, wcq, wco, wtime):
    full = ((PIX, C), SINGLE)
    column = ((PIX, 8), SINGLE)
    proj, mix, lse, sec2 = kernel_call(
        self_kernel, [((PIX, 3 * C), NARROW), full, column, full], flops=16 * 10**9
    )(sec1, gains, wqkv, wso)
    rest = kernel_call(
        cross_kernel,
        [((TEXT, 2 * C), NARROW), ((PIX, C), NARROW), full, column, full, ((PIX, 3 * C), NARROW)],
        flops=12 * 10**9,
    )(sec2, gains, text, usable, wkv, wcq, wco, wtime)
    return proj, mix, lse, sec2, *rest


def ln_back_rows(layer, gain, upstream):
    hat, rstd = ln_rows(layer, gain)
    dx = upstream * gain
    part = rstd * (
        dx - jnp.mean(dx, axis=-1, keepdims=True) - hat * jnp.mean(dx * hat, axis=-1, keepdims=True)
    )
    return part, jnp.sum(upstream * hat, axis=0, keepdims=True), hat


def split_three(column):
    one = column.astype(NARROW)
    rest = column - one.astype(SINGLE)
    two = rest.astype(NARROW)
    return [one, two, (rest - two.astype(SINGLE)).astype(NARROW)]


def extended(rows, column):
    return jnp.concatenate([rows] + split_three(-column), axis=1)


def with_units(rows):
    return jnp.concatenate([rows, jnp.ones((rows.shape[0], 3), rows.dtype)], axis=1)


def back_front(q, k, v, lse, grad, mix):
    inner = jnp.sum(grad.astype(SINGLE) * mix, axis=-1, keepdims=True)
    return nt(with_units(k), extended(q, lse)), nt(with_units(v), extended(grad, inner))


def cross_back_kernel(carried_ref, gtime_ref, sec3_ref, sec2_ref, cq_ref, cmix_ref, clse_ref,
                      kv_ref, usable_ref, text_ref, gains_ref, wtime_ref, wco_ref, wcq_ref,
                      carried_out_ref, pack_ref, gain_ref,
                      hat_s, back_s, dq_s, dkv_s, da_s, db_s, dw_s, gmix_s):
    gain_ref[...] = jnp.zeros((8, C), SINGLE)
    usable = jnp.broadcast_to(usable_ref[...], (TEXT, PIX)) == 1
    part, gain, hat = ln_back_rows(sec3_ref[...], gains_ref[4:5, :], nt(gtime_ref[...], wtime_ref[...]))
    gain_ref[1:2, :] = gain
    hat_s[...] = (hat * gains_ref[4:5, :]).astype(NARROW)
    carried = carried_ref[...] + part
    carried_out_ref[...] = carried
    back_s[...] = carried.astype(NARROW)
    gmix_s[...] = nt(back_s[...], wco_ref[...]).astype(NARROW)

    def front(h):
        lanes = head_lanes(h)
        return back_front(
            cq_ref[:, lanes] * jnp.bfloat16(SCALE), kv_ref[:, lanes],
            kv_ref[:, C + h * HEAD : C + (h + 1) * HEAD], clse_ref[:, h : h + 1], gmix_s[:, lanes], cmix_ref[:, lanes],
        )

    def rest(h, pair):
        lanes = head_lanes(h)
        scores, grad_probs = pair
        probs = jnp.exp(jnp.where(usable, scores, MASKED))
        grad_scores = (probs * grad_probs).astype(NARROW)
        dq_s[:, lanes] = (tn(grad_scores, kv_ref[:, lanes]) * SCALE).astype(NARROW)
        dkv_s[:, lanes] = mm(grad_scores, cq_ref[:, lanes] * jnp.bfloat16(SCALE))
        dkv_s[:, C + h * HEAD : C + (h + 1) * HEAD] = mm(probs.astype(NARROW), gmix_s[:, lanes])

    staged(HEADS, front, rest)
    da_s[...] = tn(hat_s[...], gtime_ref[...])
    db_s[...] = tn(cmix_ref[...].astype(NARROW), back_s[...])
    bands_out(pack_ref, 52, db_s, 20, 160)
    part, gain, hat = ln_back_rows(sec2_ref[...], gains_ref[3:4, :], nt(dq_s[...], wcq_ref[...]))
    gain_ref[0:1, :] = gain
    carried_out_ref[...] += part
    hat_s[...] = (hat * gains_ref[3:4, :]).astype(NARROW)
    db_s[...] = tn(hat_s[...], dq_s[...])
    pair_out(pack_ref, 32, da_s, db_s)
    dw_s[...] = tn(text_ref[...], dkv_s[...].astype(NARROW))
    bands_out(pack_ref, 0, dw_s, 64, 320)


def cross_back(*args):
    low = ((PIX, C), NARROW)
    return kernel_call(
        cross_back_kernel,
        [((PIX, C), SINGLE), (packed_shape(64), NARROW), ((8, C), SINGLE)],
        [low, low, low, ((TEXT, 2 * C), SINGLE), ((C, 3 * C), SINGLE), ((C, C), SINGLE), ((CTX, 2 * C), SINGLE), low],
        flops=26 * 10**9,
    )(*args)


def self_back_kernel(carried_ref, sec1_ref, proj_ref, mix_ref, lse_ref, gains_ref, wqkv_ref, wso_ref,
                     carried_out_ref, pack_ref, gain_ref,
                     back_s, gmix_s, dproj_s, hat_s, dk_s, dv_s, da_s, db_s):
    gain_ref[...] = jnp.zeros((8, C), SINGLE)
    back_s[...] = carried_ref[...].astype(NARROW)
    gmix_s[...] = nt(back_s[...], wso_ref[...]).astype(NARROW)
    db_s[...] = tn(mix_ref[...].astype(NARROW), back_s[...])

    def spots(i):
        h, r = divmod(i, STEPS)
        return slice(r * STEP, (r + 1) * STEP), head_lanes(h), head_lanes(HEADS + h), head_lanes(2 * HEADS + h), h, r

    def front(i):
        rows, lanes, lanes_k, lanes_v, h, r = spots(i)
        return back_front(
            proj_ref[rows, lanes] * jnp.bfloat16(SCALE), proj_ref[:, lanes_k], proj_ref[:, lanes_v],
            lse_ref[rows, h : h + 1], gmix_s[rows, lanes], mix_ref[rows, lanes],
        )

    def rest(i, pair):
        rows, lanes, lanes_k, lanes_v, h, r = spots(i)
        scores, grad_probs = pair
        probs = jnp.exp(scores)
        grad_scores = (probs * grad_probs).astype(NARROW)
        dproj_s[rows, lanes] = (tn(grad_scores, proj_ref[:, lanes_k]) * SCALE).astype(NARROW)
        dk = mm(grad_scores, proj_ref[rows, lanes] * jnp.bfloat16(SCALE))
        dv = mm(probs.astype(NARROW), gmix_s[rows, lanes])
        if r > 0:
            dk += dk_s[...]
            dv += dv_s[...]
        if r < STEPS - 1:
            dk_s[...] = dk
            dv_s[...] = dv
        else:
            dproj_s[:, lanes_k] = dk.astype(NARROW)
            dproj_s[:, lanes_v] = dv.astype(NARROW)

    staged(HEADS * STEPS, front, rest)
    part, gain, hat = ln_back_rows(sec1_ref[...], gains_ref[2:3, :], nt(dproj_s[...], wqkv_ref[...]))
    gain_ref[0:1, :] = gain
    hat_s[...] = (hat * gains_ref[2:3, :]).astype(NARROW)
    carried_out_ref[...] = carried_ref[...] + part
    da_s[...] = tn(hat_s[...], dproj_s[...])
    pair_out(pack_ref, 0, da_s, db_s)


def self_back_block(*args):
    low = ((PIX, C), NARROW)
    return kernel_call(
        self_back_kernel,
        [((PIX, C), SINGLE), (packed_shape(24), NARROW), ((8, C), SINGLE)],
        [low, low, ((PIX, 3 * C), NARROW), low, ((PIX, HEAD), SINGLE), ((PIX, HEAD), SINGLE),
         ((C, 3 * C), SINGLE), ((C, C), SINGLE)],
        flops=29 * 10**9,
    )(*args)


def feed_kernel(sec3_ref, mix_ref, cot_ref, gains_ref, wto_ref, wup_ref, wdown_ref,
                out_ref, carried_ref, gmix_ref, pack_ref, gain_ref,
                hat_s, act_s, lift_s, back_s, d_s, dw_s):
    gain_ref[...] = jnp.zeros((8, C), SINGLE)
    for r in range(1):
        rows = slice(0, PIX)
        sec4 = sec3_ref[rows, :] + mm(mix_ref[rows, :], wto_ref[...])
        hat, rstd = ln_rows(sec4, None)
        hat_s[rows, :] = (hat * gains_ref[5:6, :]).astype(NARROW)
        lifted = mm(hat_s[rows, :], wup_ref[...])
        cube = lifted * lifted
        inner = jnp.tanh(GELU_A * lifted * (1.0 + GELU_B * cube))
        gate = 0.5 + 0.5 * inner
        act_s[rows, :] = (lifted * gate).astype(NARROW)
        slope = gate + (0.5 * GELU_A) * lifted * (1.0 - inner * inner) * (1.0 + (3.0 * GELU_B) * cube)
        grad_act = nt(cot_ref[rows, :], wdown_ref[...])
        lift_s[rows, :] = (grad_act * slope).astype(NARROW)
        out_ref[rows, :] = (sec4 + mm(act_s[rows, :], wdown_ref[...])).astype(NARROW)
        part, gain, hat = ln_back_rows(sec4, gains_ref[5:6, :], nt(lift_s[rows, :], wup_ref[...]))
        gain_ref[0:1, :] += gain
        carried = cot_ref[rows, :].astype(SINGLE) + part
        carried_ref[rows, :] = carried
        back_s[rows, :] = carried.astype(NARROW)
        gmix_ref[rows, :] = nt(back_s[rows, :], wto_ref[...]).astype(NARROW)
    dw_s[...] = tn(hat_s[...], lift_s[...])
    bands_out(pack_ref, 0, dw_s, 20, 640)
    d_s[...] = tn(act_s[...], cot_ref[...])
    bands_out(pack_ref, 20, d_s, 80, 160)
    d_s[0:C, :] = tn(mix_ref[...], back_s[...])
    bands_out(pack_ref, 40, d_s, 20, 160)


def feed_block(*args):
    low = ((PIX, C), NARROW)
    wide = ((PIX, FF), NARROW)
    return kernel_call(
        feed_kernel,
        [low, ((PIX, C), SINGLE), low, (packed_shape(48), NARROW), ((8, C), SINGLE)],
        [low, wide, wide, low, ((FF, C), SINGLE), ((C, FF), SINGLE)],
        flops=20 * 10**9,
    )(*args)


def untile(tile):
    return tile.reshape(16, 8, tile.shape[-1])


def time_kernel(qkv_ref, bias_ref, low_ref, mix_ref, lse_ref, wide_s):
    wide_s[...] = qkv_ref[...].astype(SINGLE)

    def front(b):
        tile = wide_s[:, 8 * b : 8 * b + 8, :].reshape(128, 3 * C).astype(NARROW)
        scores = [
            nt(tile[:, head_lanes(h)] * jnp.bfloat16(SCALE), tile[:, head_lanes(HEADS + h)]) for h in range(HEADS)
        ]
        return jnp.concatenate(scores, axis=0) + bias_ref[...], tile

    def rest(b, pair):
        scores, tile = pair
        highest = jnp.max(scores, axis=-1, keepdims=True)
        probs = jnp.exp(scores - highest).astype(NARROW)
        both = jnp.concatenate(
            [mm(probs[128 * h : 128 * h + 128], with_ones(tile[:, head_lanes(2 * HEADS + h)])) for h in range(HEADS)],
            axis=0,
        )
        total = both[:, HEAD : HEAD + 1]
        mix = both[:, :HEAD] / total
        lse = highest + jnp.log(total)
        cut = [slice(128 * h, 128 * h + 128) for h in range(HEADS)]
        for h in range(HEADS):
            lse_ref[128 * b : 128 * b + 128, h : h + 1] = lse[cut[h]]
        mix_ref[:, 8 * b : 8 * b + 8, :] = untile(jnp.concatenate([mix[c] for c in cut], axis=1))

    staged(PIX // 16 // 8, front, rest)
    low_ref[...] = mix_ref[...].astype(NARROW)


def time_block(qkv, bias):
    rows = PIX // 16
    return kernel_call(
        time_kernel,
        [((16, rows, C), NARROW), ((16, rows, C), SINGLE), ((PIX, 8), SINGLE)],
        [((16, rows, 3 * C), SINGLE)],
        flops=15 * 10**9,
    )(qkv, bias)


def time_back_kernel(qkv_ref, bias_ref, mix_ref, lse_ref, grad_ref, fold_ref, dqkv_ref, small_ref,
                     wide_s, grad_s, out_s, dbias_s):
    dbias_s[...] = jnp.zeros((HEADS * 128, 128), SINGLE)
    wide_s[...] = qkv_ref[...].astype(SINGLE)
    grad_s[...] = grad_ref[...].astype(SINGLE)

    def front(b):
        part = slice(8 * b, 8 * b + 8)
        tile = wide_s[:, part, :].reshape(128, 3 * C).astype(NARROW)
        grads = grad_s[:, part, :].reshape(128, C)
        inners = grads * mix_ref[:, part, :].reshape(128, C)
        grads = grads.astype(NARROW)
        scores, grad_probs, qs, gs = [], [], [], []
        for h in range(HEADS):
            q = tile[:, head_lanes(h)] * jnp.bfloat16(SCALE)
            g = grads[:, head_lanes(h)]
            lse = lse_ref[128 * b : 128 * b + 128, h : h + 1]
            inner = jnp.sum(inners[:, head_lanes(h)], axis=-1, keepdims=True)
            scores.append(nt(with_units(tile[:, head_lanes(HEADS + h)]), extended(q, lse)))
            grad_probs.append(nt(with_units(tile[:, head_lanes(2 * HEADS + h)]), extended(g, inner)))
            qs.append(q)
            gs.append(g)
        return jnp.concatenate(scores, axis=0) + bias_ref[...], jnp.concatenate(grad_probs, axis=0), tile, qs, gs

    def rest(b, held):
        scores, grad_probs, tile, qs, gs = held
        probs = jnp.exp(scores)
        ds = (probs * grad_probs).astype(NARROW)
        dbias_s[...] += ds.astype(SINGLE)
        probs = probs.astype(NARROW)
        cut = [slice(128 * h, 128 * h + 128) for h in range(HEADS)]
        dqs = [tn(ds[cut[h]], tile[:, head_lanes(HEADS + h)]) * SCALE for h in range(HEADS)]
        dks = [mm(ds[cut[h]], qs[h]) for h in range(HEADS)]
        dvs = [mm(probs[cut[h]], gs[h]) for h in range(HEADS)]
        out_s[:, 8 * b : 8 * b + 8, :] = untile(jnp.concatenate(dqs + dks + dvs, axis=1))

    staged(PIX // 16 // 8, front, rest)
    dqkv_ref[...] = out_s[...].astype(NARROW)
    fold = fold_ref[...]
    for h in range(HEADS):
        rows = lax.dot_general(
            fold, dbias_s[128 * h : 128 * h + 128, :], TN, precision=PRECISE, preferred_element_type=SINGLE
        )
        small_ref[h] = jnp.dot(rows, fold, precision=PRECISE, preferred_element_type=SINGLE)


def time_back_block(qkv, bias_t, mix, lse, grad):
    fold = (jnp.arange(128)[:, None] // 8 == jnp.arange(16)[None, :]).astype(SINGLE)
    wide = ((16, PIX // 16, 3 * C), SINGLE)
    return kernel_call(
        time_back_kernel,
        [((16, PIX // 16, 3 * C), NARROW), ((HEADS, 16, 16), SINGLE)],
        [wide, ((16, PIX // 16, C), SINGLE), wide, ((HEADS * 128, 128), SINGLE)],
        flops=25 * 10**9,
    )(qkv, bias_t, mix, lse, grad, fold)


def conv_back_rows(y_s, r):
    not_first, not_last = edge_masks(STEP)
    base = r * STEP
    sides = []
    for j in range(3):
        total = None
        for i in range(3):
            lanes = slice((3 * i + j) * C, (3 * i + j + 1) * C)
            part = y_s[pl.ds(base + IMG_W * (2 - i), STEP), lanes]
            total = part if total is None else total + part
        sides.append(total)
    from_next = jnp.where(not_last, pltpu.roll(sides[0], STEP - 1, 0), 0.0)
    from_prev = jnp.where(not_first, pltpu.roll(sides[2], 1, 0), 0.0)
    return from_next + sides[1] + from_prev


def conv_weight_grad(cols_ref, back_s, d_s):
    for i in range(3):
        d_s[3 * C * i : 3 * C * (i + 1), :] = tn(cols_ref[pl.ds(IMG_W * i, PIX), :], back_s[...])


def conv_input_products(back_s, w_ref, y_s):
    border = jnp.zeros((IMG_W, 9 * C), SINGLE)
    y_s[0:IMG_W, :] = border
    y_s[PIX + IMG_W :, :] = border
    for r in range(STEPS):
        y_s[pl.ds(IMG_W + r * STEP, STEP), :] = nt(back_s[r * STEP : (r + 1) * STEP, :], w_ref[...])


def silu_slope(pre):
    gate = 0.5 + 0.5 * jnp.tanh(0.5 * pre)
    return gate * (1.0 + pre * (1.0 - gate))


def second_weight_kernel(carried_ref, cols2_ref, upper_ref, pack_ref, back_ref, d_s):
    pack_ref[:, :, :, 0:24, :] = upper_ref[...]
    for r in range(STEPS):
        rows = slice(r * STEP, (r + 1) * STEP)
        back_ref[rows, :] = carried_ref[rows, :].astype(NARROW)
    conv_weight_grad(cols2_ref, back_ref, d_s)
    bands_out(pack_ref, 24, d_s, 180, 160)


def second_weight(carried, cols2, upper):
    return kernel_call(
        second_weight_kernel, [(packed_shape(72), NARROW), ((PIX, C), NARROW)], [((9 * C, C), SINGLE)],
        flops=9 * 10**9,
    )(carried, cols2, upper)


def second_back_kernel(back_s, conv_out_ref, stats_ref, film_ref, gains_ref, gmat_ref,
                       w2_ref, hidden_ref, back_ref, sums_ref, y_s):
    conv_input_products(back_s, w2_ref, y_s)
    scale = 1.0 + film_ref[0:1, :C]
    shift = film_ref[0:1, C:]
    center, spread, gain = stats_ref[2:3, :], stats_ref[3:4, :], gains_ref[1:2, :]
    zero = jnp.zeros((1, C), SINGLE)
    gain_sum, total, crossed = zero, zero, zero
    for r in range(STEPS):
        rows = slice(r * STEP, (r + 1) * STEP)
        normed = (conv_out_ref[rows, :] * scale + shift - center) * spread
        grad_pre = conv_back_rows(y_s, r) * silu_slope(normed * gain)
        gain_sum += jnp.sum(grad_pre * normed, axis=0, keepdims=True)
        grad = grad_pre * gain
        hidden_ref[rows, :] = grad
        total += jnp.sum(grad, axis=0, keepdims=True)
        crossed += jnp.sum(grad * normed, axis=0, keepdims=True)
    members = PIX * (C // GROUPS)
    total = grouped(total, gmat_ref[...]) / members
    crossed = grouped(crossed, gmat_ref[...]) / members
    film_one, film_two = zero, zero
    for r in range(STEPS):
        rows = slice(r * STEP, (r + 1) * STEP)
        conv_out = conv_out_ref[rows, :]
        normed = (conv_out * scale + shift - center) * spread
        hidden = spread * (hidden_ref[rows, :] - total - normed * crossed)
        film_one += jnp.sum(hidden * conv_out, axis=0, keepdims=True)
        film_two += jnp.sum(hidden, axis=0, keepdims=True)
        back_ref[rows, :] = (hidden * scale).astype(NARROW)
    sums_ref[...] = jnp.zeros((8, C), SINGLE)
    sums_ref[0:1, :] = gain_sum
    sums_ref[1:2, :] = film_one
    sums_ref[2:3, :] = film_two


def second_back(*args):
    return kernel_call(
        second_back_kernel,
        [((PIX, C), SINGLE), ((PIX, C), NARROW), ((8, C), SINGLE)],
        [((PIX + 2 * IMG_W, 9 * C), SINGLE)],
        flops=9 * 10**9,
    )(*args)


def first_weight_kernel(cols1_ref, back_ref, pack_ref, d_s):
    conv_weight_grad(cols1_ref, back_ref, d_s)
    bands_out(pack_ref, 0, d_s, 180, 160)


def first_weight(cols1, back):
    return kernel_call(
        first_weight_kernel, [(packed_shape(48), NARROW)], [((9 * C, C), SINGLE)], flops=9 * 10**9
    )(cols1, back)[0]


def first_sum_kernel(core_ref, packed_ref, got_ref, sums_ref, out_ref):
    core = core_ref[0]
    row = jnp.concatenate([sums_ref[0:1, :], jnp.zeros((1, BAND - C), SINGLE)], axis=1).astype(NARROW)
    for j in range(8):
        for h in range(2):
            total = packed_ref[core, j, h].astype(SINGLE) + got_ref[j, h].astype(SINGLE)
            out_ref[j, h] = total.astype(NARROW)
            out_ref[j, h, 45:46, :] = row


def first_sum(core, packed, got, sums):
    core_vec = jnp.full((1,), core, jnp.int32)
    return smem_call(first_sum_kernel, 3, [(packed_shape(48)[1:], NARROW)], flops=10**6)(
        core_vec, packed, got, sums
    )[0]


def small_kernel(half_ref, got_ref, own_ref, other_ref, small_ref):
    half = half_ref[0]

    def film(place):
        both = got_ref[:, place, :]
        return lax.dot_general(
            both[:, C : C + 80], both[:, :C], TN, precision=PRECISE, preferred_element_type=SINGLE
        )

    own_ref[...] = film(half)
    other_ref[...] = film(1 - half).astype(NARROW)
    total = got_ref[0]
    for s in range(1, 16):
        total += got_ref[s]
    small_ref[...] = total


def small_pack_kernel(temb_ref, sums_d, gain_a, gain_b, gain_c, table_ref, out_ref):
    out_ref[...] = jnp.zeros((16, 8, BAND), SINGLE)
    temb = temb_ref[0:1, :].astype(SINGLE)
    same = jnp.concatenate(
        [sums_d[0:1, :], gain_c[0:1, :], gain_b[0:2, :], gain_a[0:1, :], table_ref[...]], axis=0
    )
    for j in range(16):
        for h in range(2):
            at = 80 * (8 * h + j // 2)
            out_ref[j, h : h + 1, 0 : C + 80] = jnp.concatenate(
                [sums_d[1 + j % 2 : 2 + j % 2, :], temb[:, at : at + 80]], axis=1
            )
        out_ref[j, 2:8, 0:C] = same


def small_swap(temb, sums_d, gain_a, gain_b, gain_c, grad_table):
    table_row = jnp.pad(grad_table.reshape(1, -1), ((0, 0), (0, C - NB * HEADS)))
    packed = kernel_call(small_pack_kernel, [((16, 8, BAND), SINGLE)], flops=10**6)(
        temb, sums_d, gain_a, gain_b, gain_c, table_row
    )[0]
    return lax.all_to_all(packed, CUBE, 0, 0, tiled=True)


def small_settle(got, half_vec):
    own, other, small = smem_call(
        small_kernel, 1, [((80, C), SINGLE), ((80, C), NARROW), ((8, BAND), SINGLE)], flops=10**6
    )(half_vec, got)
    swap = [(0, 1), (1, 0)]
    return own, lax.ppermute(other, HALF, swap), small + lax.ppermute(small, HALF, swap)


def finish_kernel(down, down_r, middle, middle_r, upper, upper_r, first, first_r,
                  film, film_r, *outs):
    w = Weights(*outs)
    total = down[...] + down_r[...].astype(SINGLE)
    bands_in(total, 0, w.feed_up, 20, 640)
    bands_in(total, 20, w.feed_down, 80, 160)
    bands_in(total, 40, w.time_output, 20, 160)
    total = middle[...] + middle_r[...].astype(SINGLE)
    bands_in(total, 0, w.cross_keyval, 64, 320)
    w.time_project[...] = total[32:52, 0:480]
    w.cross_query[...] = total[32:52, 480:640]
    bands_in(total, 52, w.cross_output, 20, 160)
    total = upper[...] + upper_r[...].astype(SINGLE)
    w.self_project[...] = total[0:20, 0:480]
    w.self_output[...] = total[0:20, 480:640]
    bands_turned(total, 24, w.conv_second, 180, 160)
    bands_turned(first[...] + first_r[...].astype(SINGLE), 0, w.conv_first, 180, 160)
    w.film_weight[...] = film[...] + film_r[...].astype(SINGLE)


def finish(*groups):
    shapes = Weights(
        conv_first=(160, 180), conv_second=(160, 180), film_weight=(80, C), self_project=(20, 480),
        self_output=(20, 160), cross_query=(20, 160), cross_keyval=(64, C), cross_output=(20, 160),
        time_project=(20, 480), time_output=(20, 160), feed_up=(20, BAND), feed_down=(80, 160),
    )
    out = Weights(*kernel_call(finish_kernel, [(s, SINGLE) for s in shapes], flops=10**6)(*groups))
    return out._replace(conv_first=out.conv_first.T, conv_second=out.conv_second.T)


def first_back_kernel(carried_ref, x_ref, stats_ref, gains_ref, gmat_ref, w1_ref, back_ref,
                      grad_ref, sums_ref, y_s, pre_s):
    conv_input_products(back_ref, w1_ref, y_s)
    center, spread, gain = stats_ref[0:1, :], stats_ref[1:2, :], gains_ref[0:1, :]
    zero = jnp.zeros((1, C), SINGLE)
    gain_sum, total, crossed = zero, zero, zero
    for r in range(STEPS):
        rows = slice(r * STEP, (r + 1) * STEP)
        normed = (x_ref[rows, :].astype(SINGLE) - center) * spread
        grad_pre = conv_back_rows(y_s, r) * silu_slope(normed * gain)
        gain_sum += jnp.sum(grad_pre * normed, axis=0, keepdims=True)
        grad = grad_pre * gain
        pre_s[rows, :] = grad
        total += jnp.sum(grad, axis=0, keepdims=True)
        crossed += jnp.sum(grad * normed, axis=0, keepdims=True)
    members = PIX * (C // GROUPS)
    total = grouped(total, gmat_ref[...]) / members
    crossed = grouped(crossed, gmat_ref[...]) / members
    for r in range(STEPS):
        rows = slice(r * STEP, (r + 1) * STEP)
        normed = (x_ref[rows, :].astype(SINGLE) - center) * spread
        grad = spread * (pre_s[rows, :] - total - normed * crossed)
        grad_ref[rows, :] = (carried_ref[rows, :] + grad).astype(NARROW)
    sums_ref[...] = jnp.zeros((8, C), SINGLE)
    sums_ref[0:1, :] = gain_sum


def first_back(*args):
    return kernel_call(
        first_back_kernel,
        [((PIX, C), NARROW), ((8, C), SINGLE)],
        [((PIX + 2 * IMG_W, 9 * C), SINGLE), ((PIX, C), SINGLE)],
        flops=11 * 10**9,
    )(*args)


BAND = 640
QUARTER = 160
PACK_ROWS = 256


def smem_call(body, n_in, outs, scratch=(), flops=10**9):
    specs = [pl.BlockSpec(memory_space=pltpu.SMEM)] + [pl.BlockSpec(memory_space=pltpu.VMEM)] * n_in
    return pl.pallas_call(
        body,
        in_specs=specs,
        out_shape=[jax.ShapeDtypeStruct(s, d) for s, d in outs],
        scratch_shapes=[pltpu.VMEM(s, d) for s, d in scratch],
        compiler_params=pltpu.CompilerParams(vmem_limit_bytes=VMEM_BYTES),
        cost_estimate=pl.CostEstimate(flops=flops, bytes_accessed=min(flops, 10**7) // 100, transcendentals=0),
    )


def side_by_side(out, at, ref, cols):
    parts = BAND // cols
    tall = ref.shape[0] // parts
    wide = ref[...].astype(SINGLE)
    out[at : at + tall, :] = jnp.concatenate(
        [wide[tall * q : tall * (q + 1), :] for q in range(parts)], axis=1
    ).astype(NARROW)


def pack_kernel(*refs):
    w = Weights(*refs[:12])
    out = refs[12]
    out[...] = jnp.zeros((PACK_ROWS, BAND), NARROW)
    side_by_side(out, 0, w.conv_first[...].astype(SINGLE).T, 160)
    side_by_side(out, 45, w.conv_second[...].astype(SINGLE).T, 160)
    side_by_side(out, 90, w.film_weight, 320)
    side_by_side(out, 130, w.cross_keyval, 320)
    out[162:182, 0:480] = w.self_project[...]
    out[162:182, 480:640] = w.self_output[...]
    out[182:202, 0:480] = w.time_project[...]
    out[182:202, 480:640] = w.time_output[...]
    out[202:222, :] = w.feed_up[...]
    side_by_side(out, 222, w.feed_down, 160)
    side_by_side(out, 242, w.cross_query, 160)
    side_by_side(out, 247, w.cross_output, 160)


def pack_weights(w):
    w = w._replace(conv_first=w.conv_first.T, conv_second=w.conv_second.T)
    return kernel_call(pack_kernel, [((PACK_ROWS, BAND), NARROW)])(*w)[0]


def unpack_pair(half, full_ref, wide, thin, at):
    for out, c0, cols in ((wide, 0, 480), (thin, 480, 160)):
        for quad in range(4):
            parts = []
            for f in range(4 * quad, 4 * quad + 4):
                place = half if f < 8 else 1 - half
                parts.append(jnp.concatenate(
                    [full_ref[2 * (f % 8) + s, place, at : at + 20, c0 : c0 + cols].astype(SINGLE) for s in range(2)],
                    axis=1,
                ))
            out[80 * quad : 80 * (quad + 1), :] = jnp.concatenate(parts, axis=0).astype(NARROW)


def unpack_kernel(half_ref, full_ref, first, second, film, wide, thin, query, keyval, mixed, time, time_out):
    half = half_ref[0]
    unpack_tall(half, full_ref, first, 0, 180, 160)
    unpack_tall(half, full_ref, second, 45, 180, 160)
    unpack_tall(half, full_ref, film, 90, 80, 320)
    unpack_tall(half, full_ref, keyval, 130, 64, 320)
    unpack_tall(half, full_ref, query, 242, 20, 160)
    unpack_tall(half, full_ref, mixed, 247, 20, 160)
    unpack_pair(half, full_ref, wide, thin, 162)
    unpack_pair(half, full_ref, time, time_out, 182)


def unpack_late_kernel(half_ref, full_ref, up, down):
    half = half_ref[0]
    unpack_tall(half, full_ref, up, 202, 20, 640)
    unpack_tall(half, full_ref, down, 222, 80, 160)


def unpacked(body, shapes, half_vec, full):
    return smem_call(body, 1, [(s, NARROW) for s in shapes], flops=3 * len(shapes) // 2 * 10**9)(half_vec, full)


def packed_shape(rows):
    return (2, 8, 2, rows, BAND)


def bands_out(out_ref, at, grad_ref, rows, cols):
    parts = BAND // cols
    tall = rows // parts
    for f in range(16):
        for s in range(2):
            lanes = slice(s * cols, (s + 1) * cols)
            pieces = [
                grad_ref[rows * f + tall * q : rows * f + tall * (q + 1), lanes] for q in range(parts)
            ]
            piece = pieces[0] if parts == 1 else jnp.concatenate(pieces, axis=1)
            out_ref[f % 2, 2 * (f % 8 // 2) + s, f // 8, at : at + tall, :] = piece.astype(NARROW)


def pair_out(out_ref, at, wide_ref, thin_ref):
    for f in range(16):
        for s in range(2):
            piece = jnp.concatenate(
                [wide_ref[20 * f : 20 * f + 20, 480 * s : 480 * s + 480],
                 thin_ref[20 * f : 20 * f + 20, 160 * s : 160 * s + 160]],
                axis=1,
            )
            out_ref[f % 2, 2 * (f % 8 // 2) + s, f // 8, at : at + 20, :] = piece.astype(NARROW)


def bands_turned(total, at, out_ref, rows, cols):
    parts = BAND // cols
    tall = rows // parts
    out_ref[...] = jnp.concatenate(
        [total[at : at + tall, cols * q : cols * (q + 1)] for q in range(parts)], axis=0
    ).T


def bands_in(total, at, out_ref, rows, cols):
    parts = BAND // cols
    tall = rows // parts
    for q in range(parts):
        out_ref[tall * q : tall * (q + 1), :] = total[at : at + tall, cols * q : cols * (q + 1)]


def reduce_kernel(half_ref, got_ref, own_ref, other_ref):
    half = half_ref[0]
    own = got_ref[0, half].astype(SINGLE)
    other = got_ref[0, 1 - half].astype(SINGLE)
    for s in range(1, 8):
        own += got_ref[s, half].astype(SINGLE)
        other += got_ref[s, 1 - half].astype(SINGLE)
    own_ref[...] = own
    other_ref[...] = other.astype(NARROW)


def chip_sum(packed, core):
    got = lax.ppermute(pick(1 - core, packed), CORE, [(0, 1), (1, 0)])
    return (pick(core, packed).astype(SINGLE) + got.astype(SINGLE)).astype(NARROW)


def chip_swap(chip):
    return lax.all_to_all(chip, CHIPS, 0, 0, tiled=True)


def reduce_half(got, half_vec):
    shape = got.shape[2:]
    own, other = smem_call(reduce_kernel, 1, [(shape, SINGLE), (shape, NARROW)], flops=10**6)(half_vec, got)
    return own, lax.ppermute(other, HALF, [(0, 1), (1, 0)])


def time_setup(video_mask, video_number, bucket_index, bias_table, half):
    order = jnp.array([8 * ((g % 2) ^ (g // 2 % 2)) + g // 2 for g in range(16)])
    live = pick(half, video_mask)
    number = pick(half, video_number)
    same = (live[:, None] == 1) & (live[None, :] == 1) & (number[:, None] == number[None, :])
    same = same | (jnp.arange(16)[:, None] == jnp.arange(16)[None, :])
    bucket = bucket_index[order][:, order]
    one_hot = (bucket.reshape(-1, 1) == jnp.arange(NB)[None, :]).astype(SINGLE)
    table = jnp.dot(one_hot, bias_table, precision=PRECISE).reshape(16, 16, HEADS).transpose(2, 0, 1)
    small = jnp.where(same[order][:, order][None], table, MASKED)
    pixel = jnp.arange(8)
    wide = jnp.where(
        (pixel[:, None] == pixel[None, :])[None, None, :, None, :], small[:, :, None, :, None], MASKED
    )
    return wide.reshape(HEADS * 128, 128), one_hot


def swap_frames(block, rows):
    return lax.all_to_all(block.reshape(16, rows, block.shape[-1]), CUBE, 0, 0, tiled=True)


def fast_shards(
    video_in, time_embed, text_embed, text_mask, video_mask, video_number, bucket_index,
    norm_gains, bias_table, conv_first, conv_second, film_weight, self_project, self_output,
    cross_query, cross_keyval, cross_output, time_project, time_output, feed_up, feed_down,
    cotangent,
):
    half = lax.axis_index(HALF)
    space = lax.axis_index(SPACE)
    core = lax.axis_index(CORE)
    gains = norm_gains.T
    half_vec = jnp.full((1,), half, jnp.int32)
    packed = pack_weights(Weights(
        conv_first=conv_first, conv_second=conv_second, film_weight=film_weight,
        self_project=self_project, self_output=self_output, cross_query=cross_query,
        cross_keyval=cross_keyval, cross_output=cross_output, time_project=time_project,
        time_output=time_output, feed_up=feed_up, feed_down=feed_down,
    ))
    other = lax.ppermute(packed, HALF, [(0, 1), (1, 0)])
    full = lax.all_gather(jnp.stack([packed, other]), CUBE, axis=0, tiled=False)
    video_in, text_embed, other = lax.optimization_barrier((video_in, text_embed, other))
    x = to_slot(video_in.reshape(FR_DEV, -1, C), half, space)
    text = to_slot(text_embed.reshape(FR_DEV, -1, CTX), half, space)
    x, text, full = lax.optimization_barrier((x, text, full))
    cotangent, full = lax.optimization_barrier((cotangent, full))
    now = unpacked(
        unpack_kernel,
        [(9 * C, C), (9 * C, C), (TEMB, 2 * C), (C, 3 * C), (C, C), (C, C), (CTX, 2 * C), (C, C),
         (C, 3 * C), (C, C)],
        half_vec, full,
    )
    cot = to_slot(cotangent.reshape(FR_DEV, -1, C), half, space)
    w = Weights(*now, None, None)
    temb = meta_slot(time_embed.reshape(FR_DEV, 1, TEMB), space)
    usable = meta_slot(text_mask.reshape(FR_DEV, 1, TEXT), space)[0] == 1
    temb_act = jax.nn.silu(temb.astype(SINGLE)).astype(NARROW)
    bias, one_hot = time_setup(video_mask, video_number, bucket_index, bias_table, half)
    gmat = group_matrix()

    temb_act = jnp.broadcast_to(temb_act, (8, TEMB))
    conv_out, sec1, cols1, cols2, stats, film = conv_block(
        x, w.conv_first, w.conv_second, temb_act, w.film_weight, gains, gmat
    )
    proj, mix, lse, sec2, text_kv, cq, cmix, clse, sec3, time_proj = attn_block(
        sec1, gains, w.self_project, w.self_output, text, usable[None, :], w.cross_keyval,
        w.cross_query, w.cross_output, w.time_project,
    )
    time_proj, cot, full = lax.optimization_barrier((time_proj, cot, full))
    time_qkv = swap_frames(time_proj, PIX // 16)
    w_up, w_down = unpacked(unpack_late_kernel, [(C, FF), (FF, C)], half_vec, full)
    time_low, time_mix_t, time_lse = time_block(time_qkv, bias)
    time_mix = swap_frames(time_low, PIX // 16).reshape(PIX, C)
    result, carried, grad_time_mix, packed, gain_a = feed_block(
        sec3, time_mix, cot, gains, w.time_output, w_up, w_down
    )
    grad_mix_t = swap_frames(grad_time_mix, PIX // 16)
    chip_down = chip_sum(packed, core)
    chip_down, grad_mix_t = lax.optimization_barrier((chip_down, grad_mix_t))
    down = chip_swap(chip_down)
    grad_qkv_t, bias_grad = time_back_block(time_qkv, bias.reshape(HEADS, 128, 128).transpose(0, 2, 1).reshape(HEADS * 128, 128), time_mix_t, time_lse, grad_mix_t)
    grad_qkv_t, down = lax.optimization_barrier((grad_qkv_t, down))
    grad_time_proj = swap_frames(grad_qkv_t, PIX // 16).reshape(PIX, 3 * C)
    grad_time_proj, result, down = lax.optimization_barrier((grad_time_proj, result, down))
    block_out = both_slots(*send_back(result, half), space).reshape(video_in.shape)
    small = bias_grad.transpose(2, 1, 0)
    grad_table = jnp.dot(one_hot.T, small.reshape(-1, HEADS), precision=PRECISE)
    carried, packed, gain_b = cross_back(
        carried, grad_time_proj, sec3, sec2, cq, cmix, clse, text_kv, usable[:, None], text, gains,
        w.time_project, w.cross_output, w.cross_query,
    )
    carried, packed, block_out, down, grad_table = lax.optimization_barrier(
        (carried, packed, block_out, down, grad_table)
    )
    down = reduce_half(down, half_vec)
    chip_middle = chip_sum(packed, core)
    carried, chip_middle = lax.optimization_barrier((carried, chip_middle))
    middle = chip_swap(chip_middle)
    carried, packed, gain_c = self_back_block(
        carried, sec1, proj, mix, lse, gains, w.self_project, w.self_output
    )
    packed, back_second = second_weight(carried, cols2, packed)
    chip_upper = chip_sum(packed, core)
    back_second, middle, chip_upper = lax.optimization_barrier((back_second, middle, chip_upper))
    middle = reduce_half(middle, half_vec)
    upper = chip_swap(chip_upper)
    _, back_first, sums_d = second_back(
        back_second, conv_out, stats, film, gains, gmat, w.conv_second
    )
    packed = first_weight(cols1, back_first)
    got = lax.ppermute(pick(1 - core, packed), CORE, [(0, 1), (1, 0)])
    back_first, packed, upper, sums_d = lax.optimization_barrier((back_first, packed, upper, sums_d))
    small_got = small_swap(temb_act, sums_d, gain_a, gain_b, gain_c, grad_table)
    grad_x, sums_e = first_back(carried, x, stats, gains, gmat, w.conv_first, back_first)
    got, small_got, sums_e = lax.optimization_barrier((got, small_got, sums_e))
    first = chip_swap(first_sum(core, packed, got, sums_e))
    own, other = send_back(grad_x, half)
    upper = reduce_half(upper, half_vec)
    film_own, film_got, small = small_settle(small_got, half_vec)
    first = reduce_half(first, half_vec)
    film_got, first, own, other = lax.optimization_barrier((film_got, first, own, other))
    input_grad = both_slots(own, other, space).reshape(video_in.shape)
    zero = first[0][45:46, :C] + first[1][45:46, :C].astype(SINGLE)
    zero = zero + lax.ppermute(zero, CORE, [(0, 1), (1, 0)])
    gain_sum = jnp.concatenate([zero, small[2:7, :C]]).T
    out = finish(*down, *middle, *upper, *first, film_own, film_got)
    return (
        block_out, input_grad, gain_sum, small[7, : NB * HEADS].reshape(NB, HEADS),
        out.conv_first, out.conv_second, out.film_weight, out.self_project, out.self_output,
        out.cross_query, out.cross_keyval, out.cross_output, out.time_project, out.time_output,
        out.feed_up, out.feed_down,
    )


def fast_solution(mesh):
    split = Mesh(mesh.devices.reshape(2, 4, 2, 2), WORLD)
    frames = (HALF, QUAD, CORE)
    image = P(None, frames, SPACE, None, None)
    weight = P(frames, SPACE)
    placed = (
        image, P(None, frames, None), P(None, frames, SPACE, None), P(None, frames, None),
        P(), P(), P(), P(), P(),
    ) + (weight,) * 12 + (image,)
    return jax.shard_map(
        fast_shards, mesh=split, in_specs=placed,
        out_specs=(image, image, P(), P()) + (weight,) * 12, check_vma=False,
    )


def solution(mesh):
    if mesh.shape[FRAME] == GROUP_LEN and mesh.shape[SPACE] == FR_DEV:
        return fast_solution(mesh)
    placed = (
        P(None, FRAME, SPACE, None, None),
        P(None, FRAME, None),
        P(None, FRAME, SPACE, None),
        P(None, FRAME, None),
        P(),
        P(),
        P(),
        P(),
        P(),
        P(FRAME, SPACE),
        P(FRAME, SPACE),
        P(FRAME, SPACE),
        P(FRAME, SPACE),
        P(FRAME, SPACE),
        P(FRAME, SPACE),
        P(FRAME, SPACE),
        P(FRAME, SPACE),
        P(FRAME, SPACE),
        P(FRAME, SPACE),
        P(FRAME, SPACE),
        P(FRAME, SPACE),
        P(None, FRAME, SPACE, None, None),
    )
    return jax.shard_map(
        shards,
        mesh=mesh,
        in_specs=placed,
        out_specs=(
            P(None, FRAME, SPACE, None, None),
            P(None, FRAME, SPACE, None, None),
            P(),
            P(),
            P(FRAME, SPACE),
            P(FRAME, SPACE),
            P(FRAME, SPACE),
            P(FRAME, SPACE),
            P(FRAME, SPACE),
            P(FRAME, SPACE),
            P(FRAME, SPACE),
            P(FRAME, SPACE),
            P(FRAME, SPACE),
            P(FRAME, SPACE),
            P(FRAME, SPACE),
            P(FRAME, SPACE),
        ),
        check_vma=False,
    )
```

```python
from typing import Any, NamedTuple

import jax
import jax.numpy as jnp
from jax import lax
from jax.experimental import pallas as pl
from jax.experimental.pallas import tpu as pltpu
from jax.sharding import Mesh
from jax.sharding import PartitionSpec as P

C = 320
HEADS = 5
HEAD = 64
GROUPS = 32
CTX = 1024
TEMB = 1280
TEXT = 128
IMG_H = 24
IMG_W = 48
FR_DEV = 2
GROUP_LEN = 16
NB = 32
FF = 1280
GELU_A = 0.7978845608028654
GELU_B = 0.044715


FRAME = "frame"
SPACE = "space"
HALF = "half"
QUAD = "quad"
CORE = "core"
EPSILON = 1e-05
MASKED = -1e30
SINGLE = jnp.float32
NARROW = jnp.bfloat16
PRECISE = lax.Precision.HIGHEST


def with_halo(block, sides, width):
    for axis, dim in sides:
        count = lax.axis_size(axis)
        forward = [(i, i + 1) for i in range(count - 1)]
        backward = [(target, source) for source, target in forward]
        low = lax.ppermute(
            lax.slice_in_dim(block, block.shape[dim] - width, None, axis=dim), axis, forward
        )
        high = lax.ppermute(lax.slice_in_dim(block, 0, width, axis=dim), axis, backward)
        block = jnp.concatenate([low, block, high], axis=dim)
    return block


def collect(item_one, item_two, item_three):
    row_full = (
        lax.all_gather(item_one, FRAME, axis=0, tiled=True),
        lax.all_gather(item_two, FRAME, axis=0, tiled=True),
        lax.all_gather(item_three, FRAME, axis=0, tiled=True),
    )
    return (
        lax.all_gather(row_full[0], SPACE, axis=1, tiled=True),
        lax.all_gather(row_full[1], SPACE, axis=1, tiled=True),
        lax.all_gather(row_full[2], SPACE, axis=1, tiled=True),
    )


def settle(item_one, item_two, item_three):
    column_sums = (
        lax.psum_scatter(
            item_one.astype(jnp.bfloat16), SPACE, scatter_dimension=1, tiled=True
        ).astype(jnp.float32),
        lax.psum_scatter(
            item_two.astype(jnp.bfloat16), SPACE, scatter_dimension=1, tiled=True
        ).astype(jnp.float32),
        lax.psum_scatter(
            item_three.astype(jnp.bfloat16), SPACE, scatter_dimension=1, tiled=True
        ).astype(jnp.float32),
    )
    return (
        lax.psum_scatter(
            column_sums[0].astype(jnp.bfloat16), FRAME, scatter_dimension=0, tiled=True
        ).astype(jnp.float32),
        lax.psum_scatter(
            column_sums[1].astype(jnp.bfloat16), FRAME, scatter_dimension=0, tiled=True
        ).astype(jnp.float32),
        lax.psum_scatter(
            column_sums[2].astype(jnp.bfloat16), FRAME, scatter_dimension=0, tiled=True
        ).astype(jnp.float32),
    )


def space_sums(item_one, item_two):
    return lax.psum((item_one, item_two), SPACE)


def columns_of(padded):
    height_here = padded.shape[1] - 2
    pieces = [
        padded[:, row_off : row_off + height_here, col_off : col_off + IMG_W, :]
        for row_off in range(3)
        for col_off in range(3)
    ]
    return jnp.concatenate(pieces, axis=-1).reshape(-1, 9 * C)


def convolve(activation, weight):
    slot_count, rows_here = (activation.shape[0], activation.shape[1])
    image = activation.reshape(slot_count, rows_here // IMG_W, IMG_W, C)
    rimmed = with_halo(image, ((SPACE, 1),), 1)
    padded = jnp.pad(rimmed, ((0, 0), (0, 0), (1, 1), (0, 0)))
    summed = jnp.dot(columns_of(padded), weight, preferred_element_type=SINGLE)
    return (summed.reshape(slot_count, rows_here, C), padded)


def convolve_back(grad_low, weight):
    flipped = weight.reshape(3, 3, C, C)[::-1, ::-1].transpose(0, 1, 3, 2).reshape(9 * C, C)
    summed, padded = convolve(grad_low, flipped)
    return summed


def weight_grad(left, right):
    return lax.dot_general(
        left.reshape(-1, left.shape[-1]),
        right.reshape(-1, right.shape[-1]),
        (((0,), (0,)), ((), ())),
        preferred_element_type=SINGLE,
    )


def back_project(grad_low, weight):
    return jnp.einsum("...o,io->...i", grad_low, weight, preferred_element_type=SINGLE)


def layer_norm(layer, gain):
    centered = layer - jnp.mean(layer, axis=-1, keepdims=True)
    return (
        centered * lax.rsqrt(jnp.mean(centered * centered, axis=-1, keepdims=True) + EPSILON) * gain
    )


def group_forward(layer):
    slot_count, rows_here = (layer.shape[0], layer.shape[1])
    grouped = layer.reshape(slot_count, rows_here, GROUPS, C // GROUPS)
    summed, squares = space_sums(
        jnp.sum(grouped, axis=(1, 3)), jnp.sum(grouped * grouped, axis=(1, 3))
    )
    members = IMG_H * IMG_W * (C // GROUPS)
    center = summed / members
    spread = lax.rsqrt(squares / members - center * center + EPSILON)
    normed = (grouped - center[:, None, :, None]) * spread[:, None, :, None]
    return (normed.reshape(slot_count, rows_here, C), spread)


def group_backward(normed, spread, upstream):
    slot_count, rows_here = (normed.shape[0], normed.shape[1])
    grad_groups = upstream.reshape(slot_count, rows_here, GROUPS, C // GROUPS)
    norm_groups = normed.reshape(slot_count, rows_here, GROUPS, C // GROUPS)
    summed, crossed = space_sums(
        jnp.sum(grad_groups, axis=(1, 3)), jnp.sum(grad_groups * norm_groups, axis=(1, 3))
    )
    members = IMG_H * IMG_W * (C // GROUPS)
    result = spread[:, None, :, None] * (
        grad_groups
        - summed[:, None, :, None] / members
        - norm_groups * crossed[:, None, :, None] / members
    )
    return result.reshape(slot_count, rows_here, C)


def masked_scores(queries, key_rows, usable):
    scores = jnp.einsum(
        "qhd,khd->hqk", queries, key_rows, preferred_element_type=SINGLE
    ) * HEAD ** (-0.5)
    return jnp.where(usable[None, None, :], scores, MASKED)


def attend_forward(queries, key_rows, value_rows, usable):
    scores = masked_scores(queries, key_rows, usable)
    highest = jnp.max(scores, axis=-1, keepdims=True)
    log_total = highest + jnp.log(jnp.sum(jnp.exp(scores - highest), axis=-1, keepdims=True))
    attn_probs = jnp.exp(scores - log_total).astype(NARROW)
    mixture = jnp.einsum(
        "hqk,khd->qhd", attn_probs, value_rows, preferred_element_type=SINGLE
    ).astype(NARROW)
    return (mixture, log_total[..., 0])


def attend_backward(queries, key_rows, value_rows, usable, log_total, grad_mixture):
    scores = masked_scores(queries, key_rows, usable)
    attn_probs = jnp.exp(scores - log_total[..., None])
    grad_probs = jnp.einsum("qhd,khd->hqk", grad_mixture, value_rows, preferred_element_type=SINGLE)
    row_inner = jnp.sum(grad_probs * attn_probs, axis=-1, keepdims=True)
    grad_scores = (attn_probs * (grad_probs - row_inner)).astype(NARROW)
    grad_queries = jnp.einsum(
        "hqk,khd->qhd", grad_scores, key_rows, preferred_element_type=SINGLE
    ) * HEAD ** (-0.5)
    grad_keys = jnp.einsum(
        "hqk,qhd->khd", grad_scores, queries, preferred_element_type=SINGLE
    ) * HEAD ** (-0.5)
    grad_values = jnp.einsum(
        "hqk,qhd->khd", attn_probs.astype(NARROW), grad_mixture, preferred_element_type=SINGLE
    )
    return (grad_queries, grad_keys, grad_values)


def time_scores(queries, gathered, time_bias, allowed):
    key_rows = gathered[..., :C].reshape(gathered.shape[0], gathered.shape[1], HEADS, HEAD)
    scores = (
        jnp.einsum("rhd,grhd->rhg", queries, key_rows, preferred_element_type=SINGLE)
        * HEAD ** (-0.5)
        + time_bias[None]
    )
    return (jnp.where(allowed[None, None, :], scores, MASKED), key_rows)


def shards(
    video_in,
    time_embed,
    text_embed,
    text_mask,
    video_mask,
    video_number,
    bucket_index,
    norm_gains,
    bias_table,
    conv_first,
    conv_second,
    film_weight,
    self_project,
    self_output,
    cross_query,
    cross_keyval,
    cross_output,
    time_project,
    time_output,
    feed_up,
    feed_down,
    cotangent,
):
    height_here = video_in.shape[2]
    rows_here = height_here * IMG_W
    text_here = text_embed.shape[2]
    frame_count = video_mask.shape[1]
    frame_index = lax.axis_index(FRAME)
    group_place = frame_index % GROUP_LEN
    heads_view = (FR_DEV, rows_here, HEADS, HEAD)
    every_key = jnp.ones((IMG_H * IMG_W,), jnp.bool_)
    frame_ids = jnp.arange(frame_count)
    place_ids = jnp.arange(GROUP_LEN)
    bucket_row = jnp.sum(jnp.where((place_ids == group_place)[:, None], bucket_index, 0), axis=0)
    key_buckets = jnp.sum(
        jnp.where((frame_ids % GROUP_LEN)[:, None] == place_ids[None, :], bucket_row[None, :], 0),
        axis=1,
    )
    key_table = (key_buckets[:, None] == jnp.arange(NB)[None, :]).astype(SINGLE)
    time_bias = jnp.dot(key_table, bias_table, precision=PRECISE, preferred_element_type=SINGLE).T

    def allowed_for(live_slot, number_slot):
        chooser = frame_ids[:, None] == frame_ids[None, :]
        live_keys = jnp.sum(jnp.where(chooser, live_slot[None, :], 0), axis=1)
        number_keys = jnp.sum(jnp.where(chooser, number_slot[None, :], 0), axis=1)
        own_frame = frame_ids == frame_index
        live_own = jnp.sum(jnp.where(own_frame, live_slot, 0))
        number_own = jnp.sum(jnp.where(own_frame, number_slot, 0))
        same_group = frame_ids // GROUP_LEN == frame_index // GROUP_LEN
        together = (live_keys == 1) & (live_own == 1) & (number_keys == number_own)
        return same_group & (together | (frame_ids == frame_index))

    def spread_keys(own_pair):
        return lax.all_gather(own_pair, FRAME, axis=0, tiled=True)

    def return_keys(spread_grads):
        return lax.psum_scatter(
            spread_grads.astype(jnp.bfloat16), FRAME, scatter_dimension=0, tiled=True
        ).astype(jnp.float32)

    def gather_keys(frame_pair, text_pair):
        return (
            lax.all_gather(frame_pair, SPACE, axis=0, tiled=True),
            lax.all_gather(text_pair, SPACE, axis=0, tiled=True),
        )

    def scatter_keys(frame_grads, text_grads):
        return (
            lax.psum_scatter(
                frame_grads.astype(jnp.bfloat16), SPACE, scatter_dimension=0, tiled=True
            ).astype(jnp.float32),
            lax.psum_scatter(
                text_grads.astype(jnp.bfloat16), SPACE, scatter_dimension=0, tiled=True
            ).astype(jnp.float32),
        )

    resid = video_in.reshape(FR_DEV, rows_here, C).astype(SINGLE)
    conv_one, film_full, conv_two = collect(conv_first, film_weight, conv_second)
    temb_act = jax.nn.silu(time_embed.reshape(FR_DEV, TEMB).astype(SINGLE)).astype(NARROW)
    film_all = jnp.dot(temb_act, film_full, preferred_element_type=SINGLE)
    film_scale = 1.0 + film_all[:, None, :C]
    film_shift = film_all[:, None, C:]
    normed_one, spread_one = group_forward(resid)
    pre_one = normed_one * norm_gains[:, 0]
    conv_out, pad_one = convolve(jax.nn.silu(pre_one).astype(NARROW), conv_one)
    hidden = conv_out * film_scale + film_shift
    normed_two, spread_two = group_forward(hidden)
    pre_two = normed_two * norm_gains[:, 1]
    branch_two, pad_two = convolve(jax.nn.silu(pre_two).astype(NARROW), conv_two)
    section_one = resid + branch_two
    kv_weight, qkv_weight, self_weight = collect(cross_keyval, self_project, self_output)
    text_kv = (
        jnp.dot(
            text_embed.reshape(FR_DEV * text_here, CTX), kv_weight, preferred_element_type=SINGLE
        )
        .astype(NARROW)
        .reshape(FR_DEV, text_here, 2 * C)
    )
    self_in = layer_norm(section_one, norm_gains[:, 2]).astype(NARROW)
    self_proj = jnp.dot(self_in, qkv_weight, preferred_element_type=SINGLE).astype(NARROW)

    def self_slot(inputs):
        proj_slot, text_slot = inputs
        frame_kv, text_full = gather_keys(proj_slot[:, C:], text_slot)
        mixture, log_total = attend_forward(
            proj_slot[:, :C].reshape(rows_here, HEADS, HEAD),
            frame_kv[:, :C].reshape(-1, HEADS, HEAD),
            frame_kv[:, C:].reshape(-1, HEADS, HEAD),
            every_key,
        )
        return (mixture, log_total, text_full)

    self_mixed, self_lse, text_all = lax.map(self_slot, (self_proj, text_kv))
    self_mixed = self_mixed.reshape(FR_DEV, rows_here, C)
    section_two = section_one + jnp.dot(self_mixed, self_weight, preferred_element_type=SINGLE)
    query_weight, cross_weight, time_weight = collect(cross_query, cross_output, time_project)
    cross_in = layer_norm(section_two, norm_gains[:, 3]).astype(NARROW)
    cross_queries = (
        jnp.dot(cross_in, query_weight, preferred_element_type=SINGLE)
        .astype(NARROW)
        .reshape(heads_view)
    )
    text_usable = text_mask.reshape(FR_DEV, TEXT) == 1
    text_keys = text_all[..., :C].reshape(FR_DEV, TEXT, HEADS, HEAD)
    text_values = text_all[..., C:].reshape(FR_DEV, TEXT, HEADS, HEAD)
    cross_mixed, cross_lse = jax.vmap(attend_forward)(
        cross_queries, text_keys, text_values, text_usable
    )
    cross_mixed = cross_mixed.reshape(FR_DEV, rows_here, C)
    section_three = section_two + jnp.dot(cross_mixed, cross_weight, preferred_element_type=SINGLE)
    time_in = layer_norm(section_three, norm_gains[:, 4]).astype(NARROW)
    time_proj = jnp.dot(time_in, time_weight, preferred_element_type=SINGLE).astype(NARROW)

    def time_slot(inputs):
        proj_slot, live_slot, number_slot = inputs
        gathered = spread_keys(proj_slot[None, :, C:])
        queries = proj_slot[:, :C].reshape(rows_here, HEADS, HEAD)
        scores, key_rows = time_scores(
            queries, gathered, time_bias, allowed_for(live_slot, number_slot)
        )
        value_rows = gathered[..., C:].reshape(key_rows.shape)
        highest = jnp.max(scores, axis=-1, keepdims=True)
        log_total = highest + jnp.log(jnp.sum(jnp.exp(scores - highest), axis=-1, keepdims=True))
        attn_probs = jnp.exp(scores - log_total).astype(NARROW)
        mixture = jnp.einsum(
            "rhg,grhd->rhd", attn_probs, value_rows, preferred_element_type=SINGLE
        ).astype(NARROW)
        return (mixture, log_total[..., 0])

    time_mixed, time_lse = lax.map(time_slot, (time_proj, video_mask, video_number))
    time_mixed = time_mixed.reshape(FR_DEV, rows_here, C)
    out_weight, inner_weight, outer_weight = collect(time_output, feed_up, feed_down)
    section_four = section_three + jnp.dot(time_mixed, out_weight, preferred_element_type=SINGLE)
    feed_in = layer_norm(section_four, norm_gains[:, 5]).astype(NARROW)
    lifted = jnp.dot(feed_in, inner_weight, preferred_element_type=SINGLE)
    activated = jax.nn.gelu(lifted, approximate=True).astype(NARROW)
    result = section_four + jnp.dot(activated, outer_weight, preferred_element_type=SINGLE)
    block_out = result.astype(NARROW).reshape(video_in.shape)
    carried = cotangent.reshape(FR_DEV, rows_here, C).astype(SINGLE)
    back_feed = carried.astype(NARROW)
    grad_down = weight_grad(activated, back_feed)
    grad_act = back_project(back_feed, outer_weight)
    value_gelu, pull_gelu = jax.vjp(lambda layer: jax.nn.gelu(layer, approximate=True), lifted)
    grad_lifted = pull_gelu(grad_act)[0].astype(NARROW)
    grad_up = weight_grad(feed_in, grad_lifted)
    value_norm, pull_norm = jax.vjp(layer_norm, section_four, norm_gains[:, 5])
    norm_part, gain_five = pull_norm(back_project(grad_lifted, inner_weight))
    carried = carried + norm_part
    back_time = carried.astype(NARROW)
    grad_time_out = weight_grad(time_mixed, back_time)
    grad_time_mixed = back_project(back_time, out_weight).astype(NARROW).reshape(heads_view)
    down_grads = settle(grad_time_out, grad_up, grad_down)

    def time_back(inputs):
        proj_slot, live_slot, number_slot, lse_slot, grad_slot = inputs
        gathered = spread_keys(proj_slot[None, :, C:])
        queries = proj_slot[:, :C].reshape(rows_here, HEADS, HEAD)
        scores, key_rows = time_scores(
            queries, gathered, time_bias, allowed_for(live_slot, number_slot)
        )
        value_rows = gathered[..., C:].reshape(key_rows.shape)
        attn_probs = jnp.exp(scores - lse_slot[..., None])
        grad_probs = jnp.einsum(
            "rhd,grhd->rhg", grad_slot, value_rows, preferred_element_type=SINGLE
        )
        row_inner = jnp.sum(grad_probs * attn_probs, axis=-1, keepdims=True)
        grad_scores = (attn_probs * (grad_probs - row_inner)).astype(NARROW)
        grad_queries = jnp.einsum(
            "rhg,grhd->rhd", grad_scores, key_rows, preferred_element_type=SINGLE
        ) * HEAD ** (-0.5)
        grad_keys = jnp.einsum(
            "rhg,rhd->grhd", grad_scores, queries, preferred_element_type=SINGLE
        ) * HEAD ** (-0.5)
        grad_values = jnp.einsum(
            "rhg,rhd->grhd", attn_probs.astype(NARROW), grad_slot, preferred_element_type=SINGLE
        )
        key_count = key_rows.shape[0]
        spread_grads = jnp.concatenate(
            [
                grad_keys.reshape(key_count, rows_here, C),
                grad_values.reshape(key_count, rows_here, C),
            ],
            -1,
        )
        own_grads = return_keys(spread_grads)[0]
        bias_grad = jnp.sum(grad_scores.astype(SINGLE), axis=0)
        return (jnp.concatenate([grad_queries.reshape(rows_here, C), own_grads], -1), bias_grad)

    grad_time_proj, bias_grads = lax.map(
        time_back, (time_proj, video_mask, video_number, time_lse, grad_time_mixed)
    )
    grad_table = jnp.dot(
        key_table.T, jnp.sum(bias_grads, axis=0).T, precision=PRECISE, preferred_element_type=SINGLE
    )
    grad_time_proj = grad_time_proj.astype(NARROW)
    grad_time_qkv = weight_grad(time_in, grad_time_proj)
    value_norm, pull_norm = jax.vjp(layer_norm, section_three, norm_gains[:, 4])
    norm_part, gain_four = pull_norm(back_project(grad_time_proj, time_weight))
    carried = carried + norm_part
    back_cross = carried.astype(NARROW)
    grad_cross_out = weight_grad(cross_mixed, back_cross)
    grad_cross_mixed = back_project(back_cross, cross_weight).astype(NARROW).reshape(heads_view)
    grad_cquery, grad_tkeys, grad_tvalues = jax.vmap(attend_backward)(
        cross_queries, text_keys, text_values, text_usable, cross_lse, grad_cross_mixed
    )
    grad_cquery = grad_cquery.reshape(FR_DEV, rows_here, C).astype(NARROW)
    grad_cross_q = weight_grad(cross_in, grad_cquery)
    value_norm, pull_norm = jax.vjp(layer_norm, section_two, norm_gains[:, 3])
    norm_part, gain_three = pull_norm(back_project(grad_cquery, query_weight))
    carried = carried + norm_part
    text_grads = jnp.concatenate(
        [grad_tkeys.reshape(FR_DEV, TEXT, C), grad_tvalues.reshape(FR_DEV, TEXT, C)], -1
    )
    middle_grads = settle(grad_cross_q, grad_cross_out, grad_time_qkv)
    back_self = carried.astype(NARROW)
    grad_self_out = weight_grad(self_mixed, back_self)
    grad_self_mixed = back_project(back_self, self_weight).astype(NARROW).reshape(heads_view)

    def self_back(inputs):
        proj_slot, text_slot, lse_slot, grad_slot, text_grad_slot = inputs
        frame_kv, text_again = gather_keys(proj_slot[:, C:], text_slot)
        grad_queries, grad_keys, grad_values = attend_backward(
            proj_slot[:, :C].reshape(rows_here, HEADS, HEAD),
            frame_kv[:, :C].reshape(-1, HEADS, HEAD),
            frame_kv[:, C:].reshape(-1, HEADS, HEAD),
            every_key,
            lse_slot,
            grad_slot,
        )
        frame_grads = jnp.concatenate([grad_keys.reshape(-1, C), grad_values.reshape(-1, C)], -1)
        own_frame, own_text = scatter_keys(frame_grads, text_grad_slot)
        return (jnp.concatenate([grad_queries.reshape(rows_here, C), own_frame], -1), own_text)

    grad_self_proj, grad_text_kv = lax.map(
        self_back, (self_proj, text_kv, self_lse, grad_self_mixed, text_grads)
    )
    grad_self_proj = grad_self_proj.astype(NARROW)
    grad_self_qkv = weight_grad(self_in, grad_self_proj)
    grad_keyval = weight_grad(
        text_embed.reshape(FR_DEV * text_here, CTX), grad_text_kv.astype(NARROW)
    )
    value_norm, pull_norm = jax.vjp(layer_norm, section_one, norm_gains[:, 2])
    norm_part, gain_two = pull_norm(back_project(grad_self_proj, qkv_weight))
    carried = carried + norm_part
    upper_grads = settle(grad_keyval, grad_self_qkv, grad_self_out)
    back_conv = carried.astype(NARROW)
    grad_conv_two = weight_grad(columns_of(pad_two), back_conv)
    grad_act_two = convolve_back(back_conv, conv_two)
    value_silu, pull_silu = jax.vjp(jax.nn.silu, pre_two)
    grad_pre_two = pull_silu(grad_act_two)[0]
    gain_one = jnp.sum(grad_pre_two * normed_two, axis=(0, 1))
    grad_hidden = group_backward(normed_two, spread_two, grad_pre_two * norm_gains[:, 1])
    grad_film = jnp.concatenate(
        [jnp.sum(grad_hidden * conv_out, axis=1), jnp.sum(grad_hidden, axis=1)], -1
    )
    grad_film_w = jnp.dot(
        temb_act.astype(SINGLE).T, grad_film, precision=PRECISE, preferred_element_type=SINGLE
    )
    back_first = (grad_hidden * film_scale).astype(NARROW)
    grad_conv_one = weight_grad(columns_of(pad_one), back_first)
    grad_act_one = convolve_back(back_first, conv_one)
    value_silu, pull_silu = jax.vjp(jax.nn.silu, pre_one)
    grad_pre_one = pull_silu(grad_act_one)[0]
    gain_zero = jnp.sum(grad_pre_one * normed_one, axis=(0, 1))
    carried = carried + group_backward(normed_one, spread_one, grad_pre_one * norm_gains[:, 0])
    input_grad = carried.astype(NARROW).reshape(video_in.shape)
    lower_grads = settle(grad_conv_one, grad_film_w, grad_conv_two)
    gain_stack = jnp.stack(
        [gain_zero, gain_one, gain_two, gain_three, gain_four, gain_five], axis=1
    )
    small_sums = lax.psum((gain_stack, grad_table), (FRAME, SPACE))
    return (
        block_out,
        input_grad,
        small_sums[0],
        small_sums[1],
        lower_grads[0],
        lower_grads[2],
        lower_grads[1],
        upper_grads[1],
        upper_grads[2],
        middle_grads[0],
        upper_grads[0],
        middle_grads[1],
        middle_grads[2],
        down_grads[0],
        down_grads[1],
        down_grads[2],
    )


PIX = IMG_H * IMG_W
CUBE = (QUAD, CORE, SPACE)
CHIPS = (QUAD, SPACE)
TRIO = (HALF, CORE, SPACE)
WORLD = (HALF, QUAD, CORE, SPACE)
SCALE = HEAD ** (-0.5)


def moves(turn):
    return [
        (4 * a + 2 * c + b, 4 * (b ^ turn) + 2 * c + (a ^ c))
        for a in range(2)
        for c in range(2)
        for b in range(2)
    ]


def back(pairs):
    return [(target, source) for source, target in pairs]


def pick(flag, pair):
    return jnp.where(flag == 0, pair[0], pair[1])


def to_slot(block, half, space):
    own = lax.ppermute(pick(space, block), TRIO, moves(0))
    other = lax.ppermute(pick(1 - space, block), TRIO, moves(1))
    return jnp.concatenate(
        [jnp.where(half == 0, own, other), jnp.where(half == 0, other, own)], axis=0
    )


def send_back(frame, half):
    pieces = frame.reshape((2, frame.shape[0] // 2) + frame.shape[1:])
    own = lax.ppermute(pick(half, pieces), TRIO, back(moves(0)))
    other = lax.ppermute(pick(1 - half, pieces), TRIO, back(moves(1)))
    return own, other


def both_slots(own, other, space):
    return jnp.stack([jnp.where(space == 0, own, other), jnp.where(space == 0, other, own)])


def meta_slot(block, space):
    return lax.ppermute(pick(space, block), TRIO, moves(0))


class Weights(NamedTuple):
    conv_first: Any
    conv_second: Any
    film_weight: Any
    self_project: Any
    self_output: Any
    cross_query: Any
    cross_keyval: Any
    cross_output: Any
    time_project: Any
    time_output: Any
    feed_up: Any
    feed_down: Any


def mm(a, b):
    return jnp.dot(a, b, preferred_element_type=SINGLE)


VMEM_BYTES = 58 * 1024 * 1024
STEP = 384
STEPS = PIX // STEP
NT = (((1,), (1,)), ((), ()))
TN = (((0,), (0,)), ((), ()))


def nt(a, b):
    return lax.dot_general(a, b, NT, preferred_element_type=SINGLE)


def tn(a, b):
    return lax.dot_general(a, b, TN, preferred_element_type=SINGLE)


def kernel_call(body, outs, scratch=(), flops=10**9):
    return pl.pallas_call(
        body,
        out_shape=[jax.ShapeDtypeStruct(s, d) for s, d in outs],
        scratch_shapes=[pltpu.VMEM(s, d) for s, d in scratch],
        compiler_params=pltpu.CompilerParams(vmem_limit_bytes=VMEM_BYTES),
        cost_estimate=pl.CostEstimate(flops=flops, bytes_accessed=min(flops, 10**7) // 100, transcendentals=0),
    )


def sweep(count, body):
    lax.fori_loop(0, count, lambda i, c: (body(i), c)[1], 0)


def rows_at(r):
    return pl.ds(pl.multiple_of(r * STEP, STEP), STEP)


def group_matrix():
    lanes = jnp.arange(C) // (C // GROUPS)
    return (lanes[:, None] == lanes[None, :]).astype(SINGLE)


def grouped(row, gmat):
    wide = jnp.broadcast_to(row, (8, C))
    return lax.dot_general(
        wide, gmat, (((1,), (0,)), ((), ())), precision=PRECISE, preferred_element_type=SINGLE
    )[:1]


def edge_masks(rows):
    col = lax.broadcasted_iota(jnp.int32, (rows, C), 0) % IMG_W
    return col != 0, col != IMG_W - 1


def spread_columns(cols_ref, start, act):
    not_first, not_last = edge_masks(STEP)
    left = jnp.where(not_first, pltpu.roll(act, 1, 0), 0.0)
    right = jnp.where(not_last, pltpu.roll(act, STEP - 1, 0), 0.0)
    cols_ref[pl.ds(start, STEP), :] = jnp.concatenate(
        [left.astype(NARROW), act.astype(NARROW), right.astype(NARROW)], axis=1
    )


def conv_rows(cols_ref, w_ref, start):
    total = None
    for i in range(3):
        part = mm(cols_ref[pl.ds(start + IMG_W * i, STEP), :], w_ref[3 * C * i : 3 * C * (i + 1), :])
        total = part if total is None else total + part
    return total


def gn_stats(total, square, gmat):
    members = PIX * (C // GROUPS)
    center = grouped(total, gmat) / members
    return center, lax.rsqrt(grouped(square, gmat) / members - center * center + EPSILON)


def unpack_tall(half, full_ref, out_ref, at, rows, cols):
    parts = BAND // cols
    tall = rows // parts
    for quad in range(4):
        pieces = []
        for frame in range(4 * quad, 4 * quad + 4):
            place = half if frame < 8 else 1 - half
            sides = [
                full_ref[2 * (frame % 8) + s, place, at : at + tall, :].astype(SINGLE) for s in range(2)
            ]
            pieces += [
                jnp.concatenate([side[:, cols * q : cols * (q + 1)] for side in sides], axis=1)
                for q in range(parts)
            ]
        out_ref[4 * rows * quad : 4 * rows * (quad + 1), :] = jnp.concatenate(pieces, axis=0).astype(NARROW)


def clear_border(cols_ref):
    border = jnp.zeros((IMG_W, 3 * C), NARROW)
    cols_ref[0:IMG_W, :] = border
    cols_ref[PIX + IMG_W :, :] = border


def conv_kernel(x_ref, w1_ref, w2_ref, temb_ref, wf_ref, gains_ref, gmat_ref,
                conv_out_ref, sec_ref, cols1_ref, cols2_ref, stats_ref, film_ref):
    film_ref[...] = mm(temb_ref[...], wf_ref[...])
    gmat = gmat_ref[...]
    clear_border(cols1_ref)
    clear_border(cols2_ref)
    total = jnp.zeros((1, C), SINGLE)
    square = jnp.zeros((1, C), SINGLE)
    for r in range(STEPS):
        x = x_ref[r * STEP : (r + 1) * STEP, :].astype(SINGLE)
        total += jnp.sum(x, axis=0, keepdims=True)
        square += jnp.sum(x * x, axis=0, keepdims=True)
    center, spread = gn_stats(total, square, gmat)
    stats_ref[0:1, :] = center
    stats_ref[1:2, :] = spread
    for r in range(STEPS):
        x = x_ref[r * STEP : (r + 1) * STEP, :].astype(SINGLE)
        pre = (x - center) * spread * gains_ref[0:1, :]
        spread_columns(cols1_ref, IMG_W + r * STEP, pre * (0.5 + 0.5 * jnp.tanh(0.5 * pre)))
    scale = 1.0 + film_ref[0:1, :C]
    shift = film_ref[0:1, C:]
    total = jnp.zeros((1, C), SINGLE)
    square = jnp.zeros((1, C), SINGLE)
    for r in range(STEPS):
        out = conv_rows(cols1_ref, w1_ref, r * STEP)
        conv_out_ref[r * STEP : (r + 1) * STEP, :] = out
        hidden = out * scale + shift
        total += jnp.sum(hidden, axis=0, keepdims=True)
        square += jnp.sum(hidden * hidden, axis=0, keepdims=True)
    center, spread = gn_stats(total, square, gmat)
    stats_ref[2:3, :] = center
    stats_ref[3:4, :] = spread
    for r in range(STEPS):
        hidden = conv_out_ref[r * STEP : (r + 1) * STEP, :] * scale + shift
        pre = (hidden - center) * spread * gains_ref[1:2, :]
        spread_columns(cols2_ref, IMG_W + r * STEP, pre * (0.5 + 0.5 * jnp.tanh(0.5 * pre)))
    for r in range(STEPS):
        out = conv_rows(cols2_ref, w2_ref, r * STEP)
        rows = slice(r * STEP, (r + 1) * STEP)
        sec_ref[rows, :] = x_ref[rows, :].astype(SINGLE) + out


def conv_block(x, w1, w2, temb, wf, gains, gmat):
    cols = (PIX + 2 * IMG_W, 3 * C)
    return kernel_call(
        conv_kernel,
        [((PIX, C), SINGLE), ((PIX, C), SINGLE), (cols, NARROW), (cols, NARROW), ((8, C), SINGLE), ((8, 2 * C), SINGLE)],
        flops=15 * 10**9,
    )(x, w1, w2, temb, wf, gains, gmat)


def ln_rows(layer, gain):
    centered = layer - jnp.mean(layer, axis=-1, keepdims=True)
    rstd = lax.rsqrt(jnp.mean(centered * centered, axis=-1, keepdims=True) + EPSILON)
    return centered * rstd, rstd


def with_ones(v):
    return jnp.concatenate([v, jnp.ones(v.shape, v.dtype)], axis=1)


def staged(count, front, rest):
    ahead = front(0)
    for i in range(count):
        now = ahead
        if i + 1 < count:
            ahead = front(i + 1)
        rest(i, now)


def head_lanes(h):
    return slice(h * HEAD, (h + 1) * HEAD)


def soft_values(scores, v_one):
    highest = jnp.max(scores, axis=-1, keepdims=True)
    both = mm(jnp.exp(scores - highest).astype(NARROW), v_one)
    total = both[:, HEAD : HEAD + 1]
    return both[:, :HEAD] / total, highest + jnp.log(total)


def soft_columns(scores, v_one):
    highest = jnp.max(scores, axis=0, keepdims=True)
    both = tn(jnp.exp(scores - highest).astype(NARROW), v_one)
    total = both[:, HEAD : HEAD + 1]
    column = jnp.broadcast_to(highest, (8, highest.shape[1])).T[:, 0:1]
    return both[:, :HEAD] / total, column + jnp.log(total)


def self_kernel(sec1_ref, gains_ref, wqkv_ref, wso_ref, proj_ref, mix_ref, lse_ref, sec2_ref):
    hat, rstd = ln_rows(sec1_ref[...], None)
    proj_ref[...] = mm((hat * gains_ref[2:3, :]).astype(NARROW), wqkv_ref[...]).astype(NARROW)

    def front(i):
        h, r = divmod(i, STEPS)
        q = proj_ref[r * STEP : (r + 1) * STEP, head_lanes(h)] * jnp.bfloat16(SCALE)
        return nt(q, proj_ref[:, head_lanes(HEADS + h)])

    def rest(i, scores):
        h, r = divmod(i, STEPS)
        rows = slice(r * STEP, (r + 1) * STEP)
        mix, lse = soft_values(scores, with_ones(proj_ref[:, head_lanes(2 * HEADS + h)]))
        mix_ref[rows, head_lanes(h)] = mix
        lse_ref[rows, h : h + 1] = lse

    staged(HEADS * STEPS, front, rest)
    sec2_ref[...] = sec1_ref[...] + mm(mix_ref[...].astype(NARROW), wso_ref[...])


def cross_kernel(sec2_ref, gains_ref, text_ref, usable_ref, wkv_ref, wcq_ref, wco_ref, wtime_ref,
                 kv_ref, cq_ref, cmix_ref, clse_ref, sec3_ref, tproj_ref):
    kv_ref[...] = mm(text_ref[...], wkv_ref[...]).astype(NARROW)
    hat, rstd = ln_rows(sec2_ref[...], None)
    cq_ref[...] = mm((hat * gains_ref[3:4, :]).astype(NARROW), wcq_ref[...]).astype(NARROW)
    usable = jnp.broadcast_to(usable_ref[...], (TEXT, PIX)) == 1

    def front(h):
        return nt(kv_ref[:, head_lanes(h)], cq_ref[:, head_lanes(h)] * jnp.bfloat16(SCALE))

    def rest(h, scores):
        v = with_ones(kv_ref[:, head_lanes(HEADS + h)])
        mix, lse = soft_columns(jnp.where(usable, scores, MASKED), v)
        cmix_ref[:, head_lanes(h)] = mix
        clse_ref[:, h : h + 1] = lse

    staged(HEADS, front, rest)
    sec3 = sec2_ref[...] + mm(cmix_ref[...].astype(NARROW), wco_ref[...])
    sec3_ref[...] = sec3
    hat, rstd = ln_rows(sec3, None)
    tproj_ref[...] = mm((hat * gains_ref[4:5, :]).astype(NARROW), wtime_ref[...]).astype(NARROW)


def attn_block(sec1, gains, wqkv, wso, text, usable, wkv, wcq, wco, wtime):
    full = ((PIX, C), SINGLE)
    column = ((PIX, 8), SINGLE)
    proj, mix, lse, sec2 = kernel_call(
        self_kernel, [((PIX, 3 * C), NARROW), full, column, full], flops=16 * 10**9
    )(sec1, gains, wqkv, wso)
    rest = kernel_call(
        cross_kernel,
        [((TEXT, 2 * C), NARROW), ((PIX, C), NARROW), full, column, full, ((PIX, 3 * C), NARROW)],
        flops=12 * 10**9,
    )(sec2, gains, text, usable, wkv, wcq, wco, wtime)
    return proj, mix, lse, sec2, *rest


def ln_back_rows(layer, gain, upstream):
    hat, rstd = ln_rows(layer, gain)
    dx = upstream * gain
    part = rstd * (
        dx - jnp.mean(dx, axis=-1, keepdims=True) - hat * jnp.mean(dx * hat, axis=-1, keepdims=True)
    )
    return part, jnp.sum(upstream * hat, axis=0, keepdims=True), hat


def split_three(column):
    one = column.astype(NARROW)
    rest = column - one.astype(SINGLE)
    two = rest.astype(NARROW)
    return [one, two, (rest - two.astype(SINGLE)).astype(NARROW)]


def extended(rows, column):
    return jnp.concatenate([rows] + split_three(-column), axis=1)


def with_units(rows):
    return jnp.concatenate([rows, jnp.ones((rows.shape[0], 3), rows.dtype)], axis=1)


def back_front(q, k, v, lse, grad, mix):
    inner = jnp.sum(grad.astype(SINGLE) * mix, axis=-1, keepdims=True)
    return nt(with_units(k), extended(q, lse)), nt(with_units(v), extended(grad, inner))


def cross_back_kernel(carried_ref, gtime_ref, sec3_ref, sec2_ref, cq_ref, cmix_ref, clse_ref,
                      kv_ref, usable_ref, text_ref, gains_ref, wtime_ref, wco_ref, wcq_ref,
                      carried_out_ref, pack_ref, gain_ref,
                      hat_s, back_s, dq_s, dkv_s, da_s, db_s, dw_s, gmix_s):
    gain_ref[...] = jnp.zeros((8, C), SINGLE)
    usable = jnp.broadcast_to(usable_ref[...], (TEXT, PIX)) == 1
    part, gain, hat = ln_back_rows(sec3_ref[...], gains_ref[4:5, :], nt(gtime_ref[...], wtime_ref[...]))
    gain_ref[1:2, :] = gain
    hat_s[...] = (hat * gains_ref[4:5, :]).astype(NARROW)
    carried = carried_ref[...] + part
    carried_out_ref[...] = carried
    back_s[...] = carried.astype(NARROW)
    gmix_s[...] = nt(back_s[...], wco_ref[...]).astype(NARROW)

    def front(h):
        lanes = head_lanes(h)
        return back_front(
            cq_ref[:, lanes] * jnp.bfloat16(SCALE), kv_ref[:, lanes],
            kv_ref[:, C + h * HEAD : C + (h + 1) * HEAD], clse_ref[:, h : h + 1], gmix_s[:, lanes], cmix_ref[:, lanes],
        )

    def rest(h, pair):
        lanes = head_lanes(h)
        scores, grad_probs = pair
        probs = jnp.exp(jnp.where(usable, scores, MASKED))
        grad_scores = (probs * grad_probs).astype(NARROW)
        dq_s[:, lanes] = (tn(grad_scores, kv_ref[:, lanes]) * SCALE).astype(NARROW)
        dkv_s[:, lanes] = mm(grad_scores, cq_ref[:, lanes] * jnp.bfloat16(SCALE))
        dkv_s[:, C + h * HEAD : C + (h + 1) * HEAD] = mm(probs.astype(NARROW), gmix_s[:, lanes])

    staged(HEADS, front, rest)
    da_s[...] = tn(hat_s[...], gtime_ref[...])
    db_s[...] = tn(cmix_ref[...].astype(NARROW), back_s[...])
    bands_out(pack_ref, 52, db_s, 20, 160)
    part, gain, hat = ln_back_rows(sec2_ref[...], gains_ref[3:4, :], nt(dq_s[...], wcq_ref[...]))
    gain_ref[0:1, :] = gain
    carried_out_ref[...] += part
    hat_s[...] = (hat * gains_ref[3:4, :]).astype(NARROW)
    db_s[...] = tn(hat_s[...], dq_s[...])
    pair_out(pack_ref, 32, da_s, db_s)
    dw_s[...] = tn(text_ref[...], dkv_s[...].astype(NARROW))
    bands_out(pack_ref, 0, dw_s, 64, 320)


def cross_back(*args):
    low = ((PIX, C), NARROW)
    return kernel_call(
        cross_back_kernel,
        [((PIX, C), SINGLE), (packed_shape(64), NARROW), ((8, C), SINGLE)],
        [low, low, low, ((TEXT, 2 * C), SINGLE), ((C, 3 * C), SINGLE), ((C, C), SINGLE), ((CTX, 2 * C), SINGLE), low],
        flops=26 * 10**9,
    )(*args)


def self_back_kernel(carried_ref, sec1_ref, proj_ref, mix_ref, lse_ref, gains_ref, wqkv_ref, wso_ref,
                     carried_out_ref, pack_ref, gain_ref,
                     back_s, gmix_s, dproj_s, hat_s, dk_s, dv_s, da_s, db_s):
    gain_ref[...] = jnp.zeros((8, C), SINGLE)
    back_s[...] = carried_ref[...].astype(NARROW)
    gmix_s[...] = nt(back_s[...], wso_ref[...]).astype(NARROW)
    db_s[...] = tn(mix_ref[...].astype(NARROW), back_s[...])

    def spots(i):
        h, r = divmod(i, STEPS)
        return slice(r * STEP, (r + 1) * STEP), head_lanes(h), head_lanes(HEADS + h), head_lanes(2 * HEADS + h), h, r

    def front(i):
        rows, lanes, lanes_k, lanes_v, h, r = spots(i)
        return back_front(
            proj_ref[rows, lanes] * jnp.bfloat16(SCALE), proj_ref[:, lanes_k], proj_ref[:, lanes_v],
            lse_ref[rows, h : h + 1], gmix_s[rows, lanes], mix_ref[rows, lanes],
        )

    def rest(i, pair):
        rows, lanes, lanes_k, lanes_v, h, r = spots(i)
        scores, grad_probs = pair
        probs = jnp.exp(scores)
        grad_scores = (probs * grad_probs).astype(NARROW)
        dproj_s[rows, lanes] = (tn(grad_scores, proj_ref[:, lanes_k]) * SCALE).astype(NARROW)
        dk = mm(grad_scores, proj_ref[rows, lanes] * jnp.bfloat16(SCALE))
        dv = mm(probs.astype(NARROW), gmix_s[rows, lanes])
        if r > 0:
            dk += dk_s[...]
            dv += dv_s[...]
        if r < STEPS - 1:
            dk_s[...] = dk
            dv_s[...] = dv
        else:
            dproj_s[:, lanes_k] = dk.astype(NARROW)
            dproj_s[:, lanes_v] = dv.astype(NARROW)

    staged(HEADS * STEPS, front, rest)
    part, gain, hat = ln_back_rows(sec1_ref[...], gains_ref[2:3, :], nt(dproj_s[...], wqkv_ref[...]))
    gain_ref[0:1, :] = gain
    hat_s[...] = (hat * gains_ref[2:3, :]).astype(NARROW)
    carried_out_ref[...] = carried_ref[...] + part
    da_s[...] = tn(hat_s[...], dproj_s[...])
    pair_out(pack_ref, 0, da_s, db_s)


def self_back_block(*args):
    low = ((PIX, C), NARROW)
    return kernel_call(
        self_back_kernel,
        [((PIX, C), SINGLE), (packed_shape(24), NARROW), ((8, C), SINGLE)],
        [low, low, ((PIX, 3 * C), NARROW), low, ((PIX, HEAD), SINGLE), ((PIX, HEAD), SINGLE),
         ((C, 3 * C), SINGLE), ((C, C), SINGLE)],
        flops=29 * 10**9,
    )(*args)


def feed_kernel(sec3_ref, mix_ref, cot_ref, gains_ref, wto_ref, wup_ref, wdown_ref,
                out_ref, carried_ref, gmix_ref, gain_ref, hat_s, act_s, lift_s, back_s):
    gain_ref[...] = jnp.zeros((8, C), SINGLE)
    for r in range(1):
        rows = slice(0, PIX)
        sec4 = sec3_ref[rows, :] + mm(mix_ref[rows, :], wto_ref[...])
        hat, rstd = ln_rows(sec4, None)
        hat_s[rows, :] = (hat * gains_ref[5:6, :]).astype(NARROW)
        lifted = mm(hat_s[rows, :], wup_ref[...])
        cube = lifted * lifted
        inner = jnp.tanh(GELU_A * lifted * (1.0 + GELU_B * cube))
        gate = 0.5 + 0.5 * inner
        act_s[rows, :] = (lifted * gate).astype(NARROW)
        slope = gate + (0.5 * GELU_A) * lifted * (1.0 - inner * inner) * (1.0 + (3.0 * GELU_B) * cube)
        grad_act = nt(cot_ref[rows, :], wdown_ref[...])
        lift_s[rows, :] = (grad_act * slope).astype(NARROW)
        out_ref[rows, :] = (sec4 + mm(act_s[rows, :], wdown_ref[...])).astype(NARROW)
        part, gain, hat = ln_back_rows(sec4, gains_ref[5:6, :], nt(lift_s[rows, :], wup_ref[...]))
        gain_ref[0:1, :] += gain
        carried = cot_ref[rows, :].astype(SINGLE) + part
        carried_ref[rows, :] = carried
        back_s[rows, :] = carried.astype(NARROW)
        gmix_ref[rows, :] = nt(back_s[rows, :], wto_ref[...]).astype(NARROW)


def feed_weight_kernel(hat_s, act_s, lift_s, back_s, mix_ref, cot_ref, pack_ref, d_s, dw_s):
    dw_s[...] = tn(hat_s[...], lift_s[...])
    bands_out(pack_ref, 0, dw_s, 20, 640)
    d_s[...] = tn(act_s[...], cot_ref[...])
    bands_out(pack_ref, 20, d_s, 80, 160)
    d_s[0:C, :] = tn(mix_ref[...], back_s[...])
    bands_out(pack_ref, 40, d_s, 20, 160)


def feed_weight(*args):
    return kernel_call(
        feed_weight_kernel, [(packed_shape(48), NARROW)], [((FF, C), SINGLE), ((C, FF), SINGLE)], flops=8 * 10**9
    )(*args)[0]


def feed_block(*args):
    low = ((PIX, C), NARROW)
    wide = ((PIX, FF), NARROW)
    return kernel_call(
        feed_kernel,
        [low, ((PIX, C), SINGLE), low, ((8, C), SINGLE), low, wide, wide, low],
        flops=12 * 10**9,
    )(*args)


def untile(tile):
    return tile.reshape(16, 8, tile.shape[-1])


def time_kernel(qkv_ref, bias_ref, low_ref, mix_ref, lse_ref, wide_s):
    wide_s[...] = qkv_ref[...].astype(SINGLE)

    def front(b):
        tile = wide_s[:, 8 * b : 8 * b + 8, :].reshape(128, 3 * C).astype(NARROW)
        scores = [
            nt(tile[:, head_lanes(h)] * jnp.bfloat16(SCALE), tile[:, head_lanes(HEADS + h)]) for h in range(HEADS)
        ]
        return jnp.concatenate(scores, axis=0) + bias_ref[...], tile

    def rest(b, pair):
        scores, tile = pair
        highest = jnp.max(scores, axis=-1, keepdims=True)
        probs = jnp.exp(scores - highest).astype(NARROW)
        both = jnp.concatenate(
            [mm(probs[128 * h : 128 * h + 128], with_ones(tile[:, head_lanes(2 * HEADS + h)])) for h in range(HEADS)],
            axis=0,
        )
        total = both[:, HEAD : HEAD + 1]
        mix = both[:, :HEAD] / total
        lse = highest + jnp.log(total)
        cut = [slice(128 * h, 128 * h + 128) for h in range(HEADS)]
        for h in range(HEADS):
            lse_ref[128 * b : 128 * b + 128, h : h + 1] = lse[cut[h]]
        mix_ref[:, 8 * b : 8 * b + 8, :] = untile(jnp.concatenate([mix[c] for c in cut], axis=1))

    staged(PIX // 16 // 8, front, rest)
    low_ref[...] = mix_ref[...].astype(NARROW)


def time_block(qkv, bias):
    rows = PIX // 16
    return kernel_call(
        time_kernel,
        [((16, rows, C), NARROW), ((16, rows, C), SINGLE), ((PIX, 8), SINGLE)],
        [((16, rows, 3 * C), SINGLE)],
        flops=15 * 10**9,
    )(qkv, bias)


def time_back_kernel(qkv_ref, bias_ref, mix_ref, lse_ref, grad_ref, fold_ref, dqkv_ref, small_ref,
                     wide_s, grad_s, out_s, dbias_s):
    dbias_s[...] = jnp.zeros((HEADS * 128, 128), SINGLE)
    wide_s[...] = qkv_ref[...].astype(SINGLE)
    grad_s[...] = grad_ref[...].astype(SINGLE)

    def front(b):
        part = slice(8 * b, 8 * b + 8)
        tile = wide_s[:, part, :].reshape(128, 3 * C).astype(NARROW)
        grads = grad_s[:, part, :].reshape(128, C)
        inners = grads * mix_ref[:, part, :].reshape(128, C)
        grads = grads.astype(NARROW)
        scores, grad_probs, qs, gs = [], [], [], []
        for h in range(HEADS):
            q = tile[:, head_lanes(h)] * jnp.bfloat16(SCALE)
            g = grads[:, head_lanes(h)]
            lse = lse_ref[128 * b : 128 * b + 128, h : h + 1]
            inner = jnp.sum(inners[:, head_lanes(h)], axis=-1, keepdims=True)
            scores.append(nt(with_units(tile[:, head_lanes(HEADS + h)]), extended(q, lse)))
            grad_probs.append(nt(with_units(tile[:, head_lanes(2 * HEADS + h)]), extended(g, inner)))
            qs.append(q)
            gs.append(g)
        return jnp.concatenate(scores, axis=0) + bias_ref[...], jnp.concatenate(grad_probs, axis=0), tile, qs, gs

    def rest(b, held):
        scores, grad_probs, tile, qs, gs = held
        probs = jnp.exp(scores)
        ds = (probs * grad_probs).astype(NARROW)
        dbias_s[...] += ds.astype(SINGLE)
        probs = probs.astype(NARROW)
        cut = [slice(128 * h, 128 * h + 128) for h in range(HEADS)]
        dqs = [tn(ds[cut[h]], tile[:, head_lanes(HEADS + h)]) * SCALE for h in range(HEADS)]
        dks = [mm(ds[cut[h]], qs[h]) for h in range(HEADS)]
        dvs = [mm(probs[cut[h]], gs[h]) for h in range(HEADS)]
        out_s[:, 8 * b : 8 * b + 8, :] = untile(jnp.concatenate(dqs + dks + dvs, axis=1))

    staged(PIX // 16 // 8, front, rest)
    dqkv_ref[...] = out_s[...].astype(NARROW)
    fold = fold_ref[...]
    for h in range(HEADS):
        rows = lax.dot_general(
            fold, dbias_s[128 * h : 128 * h + 128, :], TN, precision=PRECISE, preferred_element_type=SINGLE
        )
        small_ref[h] = jnp.dot(rows, fold, precision=PRECISE, preferred_element_type=SINGLE)


def time_back_block(qkv, bias_t, mix, lse, grad):
    fold = (jnp.arange(128)[:, None] // 8 == jnp.arange(16)[None, :]).astype(SINGLE)
    wide = ((16, PIX // 16, 3 * C), SINGLE)
    return kernel_call(
        time_back_kernel,
        [((16, PIX // 16, 3 * C), NARROW), ((HEADS, 16, 16), SINGLE)],
        [wide, ((16, PIX // 16, C), SINGLE), wide, ((HEADS * 128, 128), SINGLE)],
        flops=25 * 10**9,
    )(qkv, bias_t, mix, lse, grad, fold)


def conv_back_rows(y_s, r):
    not_first, not_last = edge_masks(STEP)
    base = r * STEP
    sides = []
    for j in range(3):
        total = None
        for i in range(3):
            lanes = slice((3 * i + j) * C, (3 * i + j + 1) * C)
            part = y_s[pl.ds(base + IMG_W * (2 - i), STEP), lanes]
            total = part if total is None else total + part
        sides.append(total)
    from_next = jnp.where(not_last, pltpu.roll(sides[0], STEP - 1, 0), 0.0)
    from_prev = jnp.where(not_first, pltpu.roll(sides[2], 1, 0), 0.0)
    return from_next + sides[1] + from_prev


def conv_weight_grad(cols_ref, back_s, d_s):
    for i in range(3):
        d_s[3 * C * i : 3 * C * (i + 1), :] = tn(cols_ref[pl.ds(IMG_W * i, PIX), :], back_s[...])


def conv_input_products(back_s, w_ref, y_s):
    border = jnp.zeros((IMG_W, 9 * C), SINGLE)
    y_s[0:IMG_W, :] = border
    y_s[PIX + IMG_W :, :] = border
    for r in range(STEPS):
        y_s[pl.ds(IMG_W + r * STEP, STEP), :] = nt(back_s[r * STEP : (r + 1) * STEP, :], w_ref[...])


def silu_slope(pre):
    gate = 0.5 + 0.5 * jnp.tanh(0.5 * pre)
    return gate * (1.0 + pre * (1.0 - gate))


def second_weight_kernel(carried_ref, cols2_ref, upper_ref, pack_ref, back_ref, d_s):
    pack_ref[:, :, :, 0:24, :] = upper_ref[...]
    for r in range(STEPS):
        rows = slice(r * STEP, (r + 1) * STEP)
        back_ref[rows, :] = carried_ref[rows, :].astype(NARROW)
    conv_weight_grad(cols2_ref, back_ref, d_s)
    bands_out(pack_ref, 24, d_s, 180, 160)


def second_weight(carried, cols2, upper):
    return kernel_call(
        second_weight_kernel, [(packed_shape(72), NARROW), ((PIX, C), NARROW)], [((9 * C, C), SINGLE)],
        flops=9 * 10**9,
    )(carried, cols2, upper)


def second_back_kernel(back_s, conv_out_ref, stats_ref, film_ref, gains_ref, gmat_ref,
                       w2_ref, hidden_ref, back_ref, sums_ref, y_s):
    conv_input_products(back_s, w2_ref, y_s)
    scale = 1.0 + film_ref[0:1, :C]
    shift = film_ref[0:1, C:]
    center, spread, gain = stats_ref[2:3, :], stats_ref[3:4, :], gains_ref[1:2, :]
    zero = jnp.zeros((1, C), SINGLE)
    gain_sum, total, crossed = zero, zero, zero
    for r in range(STEPS):
        rows = slice(r * STEP, (r + 1) * STEP)
        normed = (conv_out_ref[rows, :] * scale + shift - center) * spread
        grad_pre = conv_back_rows(y_s, r) * silu_slope(normed * gain)
        gain_sum += jnp.sum(grad_pre * normed, axis=0, keepdims=True)
        grad = grad_pre * gain
        hidden_ref[rows, :] = grad
        total += jnp.sum(grad, axis=0, keepdims=True)
        crossed += jnp.sum(grad * normed, axis=0, keepdims=True)
    members = PIX * (C // GROUPS)
    total = grouped(total, gmat_ref[...]) / members
    crossed = grouped(crossed, gmat_ref[...]) / members
    film_one, film_two = zero, zero
    for r in range(STEPS):
        rows = slice(r * STEP, (r + 1) * STEP)
        conv_out = conv_out_ref[rows, :]
        normed = (conv_out * scale + shift - center) * spread
        hidden = spread * (hidden_ref[rows, :] - total - normed * crossed)
        film_one += jnp.sum(hidden * conv_out, axis=0, keepdims=True)
        film_two += jnp.sum(hidden, axis=0, keepdims=True)
        back_ref[rows, :] = (hidden * scale).astype(NARROW)
    sums_ref[...] = jnp.zeros((8, C), SINGLE)
    sums_ref[0:1, :] = gain_sum
    sums_ref[1:2, :] = film_one
    sums_ref[2:3, :] = film_two


def second_back(*args):
    return kernel_call(
        second_back_kernel,
        [((PIX, C), SINGLE), ((PIX, C), NARROW), ((8, C), SINGLE)],
        [((PIX + 2 * IMG_W, 9 * C), SINGLE)],
        flops=9 * 10**9,
    )(*args)


def first_weight_kernel(cols1_ref, back_ref, pack_ref, d_s):
    conv_weight_grad(cols1_ref, back_ref, d_s)
    bands_out(pack_ref, 0, d_s, 180, 160)


def first_weight(cols1, back):
    return kernel_call(
        first_weight_kernel, [(packed_shape(48), NARROW)], [((9 * C, C), SINGLE)], flops=9 * 10**9
    )(cols1, back)[0]


def first_sum_kernel(core_ref, packed_ref, got_ref, sums_ref, out_ref):
    core = core_ref[0]
    row = jnp.concatenate([sums_ref[0:1, :], jnp.zeros((1, BAND - C), SINGLE)], axis=1).astype(NARROW)
    for j in range(8):
        for h in range(2):
            total = packed_ref[core, j, h].astype(SINGLE) + got_ref[j, h].astype(SINGLE)
            out_ref[j, h] = total.astype(NARROW)
            out_ref[j, h, 45:46, :] = row


def first_sum(core, packed, got, sums):
    core_vec = jnp.full((1,), core, jnp.int32)
    return smem_call(first_sum_kernel, 3, [(packed_shape(48)[1:], NARROW)], flops=10**6)(
        core_vec, packed, got, sums
    )[0]


def small_kernel(half_ref, got_ref, own_ref, other_ref, small_ref):
    half = half_ref[0]

    def film(place):
        both = got_ref[:, place, :]
        return lax.dot_general(
            both[:, C : C + 80], both[:, :C], TN, precision=PRECISE, preferred_element_type=SINGLE
        )

    own_ref[...] = film(half)
    other_ref[...] = film(1 - half).astype(NARROW)
    total = got_ref[0]
    for s in range(1, 16):
        total += got_ref[s]
    small_ref[...] = total


def small_pack_kernel(temb_ref, sums_d, gain_a, gain_b, gain_c, table_ref, out_ref):
    out_ref[...] = jnp.zeros((16, 8, BAND), SINGLE)
    temb = temb_ref[0:1, :].astype(SINGLE)
    same = jnp.concatenate(
        [sums_d[0:1, :], gain_c[0:1, :], gain_b[0:2, :], gain_a[0:1, :], table_ref[...]], axis=0
    )
    for j in range(16):
        for h in range(2):
            at = 80 * (8 * h + j // 2)
            out_ref[j, h : h + 1, 0 : C + 80] = jnp.concatenate(
                [sums_d[1 + j % 2 : 2 + j % 2, :], temb[:, at : at + 80]], axis=1
            )
        out_ref[j, 2:8, 0:C] = same


def small_swap(temb, sums_d, gain_a, gain_b, gain_c, grad_table):
    table_row = jnp.pad(grad_table.reshape(1, -1), ((0, 0), (0, C - NB * HEADS)))
    packed = kernel_call(small_pack_kernel, [((16, 8, BAND), SINGLE)], flops=10**6)(
        temb, sums_d, gain_a, gain_b, gain_c, table_row
    )[0]
    return lax.all_to_all(packed, CUBE, 0, 0, tiled=True)


def small_settle(got, half_vec):
    own, other, small = smem_call(
        small_kernel, 1, [((80, C), SINGLE), ((80, C), NARROW), ((8, BAND), SINGLE)], flops=10**6
    )(half_vec, got)
    swap = [(0, 1), (1, 0)]
    return own, lax.ppermute(other, HALF, swap), small + lax.ppermute(small, HALF, swap)


def finish_kernel(down, down_r, middle, middle_r, upper, upper_r, first, first_r,
                  film, film_r, *outs):
    w = Weights(*outs)
    total = down[...] + down_r[...].astype(SINGLE)
    bands_in(total, 0, w.feed_up, 20, 640)
    bands_in(total, 20, w.feed_down, 80, 160)
    bands_in(total, 40, w.time_output, 20, 160)
    total = middle[...] + middle_r[...].astype(SINGLE)
    bands_in(total, 0, w.cross_keyval, 64, 320)
    w.time_project[...] = total[32:52, 0:480]
    w.cross_query[...] = total[32:52, 480:640]
    bands_in(total, 52, w.cross_output, 20, 160)
    total = upper[...] + upper_r[...].astype(SINGLE)
    w.self_project[...] = total[0:20, 0:480]
    w.self_output[...] = total[0:20, 480:640]
    bands_turned(total, 24, w.conv_second, 180, 160)
    bands_turned(first[...] + first_r[...].astype(SINGLE), 0, w.conv_first, 180, 160)
    w.film_weight[...] = film[...] + film_r[...].astype(SINGLE)


def finish(*groups):
    shapes = Weights(
        conv_first=(160, 180), conv_second=(160, 180), film_weight=(80, C), self_project=(20, 480),
        self_output=(20, 160), cross_query=(20, 160), cross_keyval=(64, C), cross_output=(20, 160),
        time_project=(20, 480), time_output=(20, 160), feed_up=(20, BAND), feed_down=(80, 160),
    )
    out = Weights(*kernel_call(finish_kernel, [(s, SINGLE) for s in shapes], flops=10**6)(*groups))
    return out._replace(conv_first=out.conv_first.T, conv_second=out.conv_second.T)


def first_back_kernel(carried_ref, x_ref, stats_ref, gains_ref, gmat_ref, w1_ref, back_ref,
                      grad_ref, sums_ref, y_s, pre_s):
    conv_input_products(back_ref, w1_ref, y_s)
    center, spread, gain = stats_ref[0:1, :], stats_ref[1:2, :], gains_ref[0:1, :]
    zero = jnp.zeros((1, C), SINGLE)
    gain_sum, total, crossed = zero, zero, zero
    for r in range(STEPS):
        rows = slice(r * STEP, (r + 1) * STEP)
        normed = (x_ref[rows, :].astype(SINGLE) - center) * spread
        grad_pre = conv_back_rows(y_s, r) * silu_slope(normed * gain)
        gain_sum += jnp.sum(grad_pre * normed, axis=0, keepdims=True)
        grad = grad_pre * gain
        pre_s[rows, :] = grad
        total += jnp.sum(grad, axis=0, keepdims=True)
        crossed += jnp.sum(grad * normed, axis=0, keepdims=True)
    members = PIX * (C // GROUPS)
    total = grouped(total, gmat_ref[...]) / members
    crossed = grouped(crossed, gmat_ref[...]) / members
    for r in range(STEPS):
        rows = slice(r * STEP, (r + 1) * STEP)
        normed = (x_ref[rows, :].astype(SINGLE) - center) * spread
        grad = spread * (pre_s[rows, :] - total - normed * crossed)
        grad_ref[rows, :] = (carried_ref[rows, :] + grad).astype(NARROW)
    sums_ref[...] = jnp.zeros((8, C), SINGLE)
    sums_ref[0:1, :] = gain_sum


def first_back(*args):
    return kernel_call(
        first_back_kernel,
        [((PIX, C), NARROW), ((8, C), SINGLE)],
        [((PIX + 2 * IMG_W, 9 * C), SINGLE), ((PIX, C), SINGLE)],
        flops=11 * 10**9,
    )(*args)


BAND = 640
QUARTER = 160
PACK_ROWS = 256


def smem_call(body, n_in, outs, scratch=(), flops=10**9):
    specs = [pl.BlockSpec(memory_space=pltpu.SMEM)] + [pl.BlockSpec(memory_space=pltpu.VMEM)] * n_in
    return pl.pallas_call(
        body,
        in_specs=specs,
        out_shape=[jax.ShapeDtypeStruct(s, d) for s, d in outs],
        scratch_shapes=[pltpu.VMEM(s, d) for s, d in scratch],
        compiler_params=pltpu.CompilerParams(vmem_limit_bytes=VMEM_BYTES),
        cost_estimate=pl.CostEstimate(flops=flops, bytes_accessed=min(flops, 10**7) // 100, transcendentals=0),
    )


def side_by_side(out, at, ref, cols):
    parts = BAND // cols
    tall = ref.shape[0] // parts
    wide = ref[...].astype(SINGLE)
    out[at : at + tall, :] = jnp.concatenate(
        [wide[tall * q : tall * (q + 1), :] for q in range(parts)], axis=1
    ).astype(NARROW)


def pack_kernel(*refs):
    w = Weights(*refs[:12])
    out = refs[12]
    out[...] = jnp.zeros((PACK_ROWS, BAND), NARROW)
    side_by_side(out, 0, w.conv_first[...].astype(SINGLE).T, 160)
    side_by_side(out, 45, w.conv_second[...].astype(SINGLE).T, 160)
    side_by_side(out, 90, w.film_weight, 320)
    side_by_side(out, 130, w.cross_keyval, 320)
    out[162:182, 0:480] = w.self_project[...]
    out[162:182, 480:640] = w.self_output[...]
    out[182:202, 0:480] = w.time_project[...]
    out[182:202, 480:640] = w.time_output[...]
    out[202:222, :] = w.feed_up[...]
    side_by_side(out, 222, w.feed_down, 160)
    side_by_side(out, 242, w.cross_query, 160)
    side_by_side(out, 247, w.cross_output, 160)


def pack_weights(w):
    w = w._replace(conv_first=w.conv_first.T, conv_second=w.conv_second.T)
    return kernel_call(pack_kernel, [((PACK_ROWS, BAND), NARROW)])(*w)[0]


def unpack_pair(half, full_ref, wide, thin, at):
    for out, c0, cols in ((wide, 0, 480), (thin, 480, 160)):
        for quad in range(4):
            parts = []
            for f in range(4 * quad, 4 * quad + 4):
                place = half if f < 8 else 1 - half
                parts.append(jnp.concatenate(
                    [full_ref[2 * (f % 8) + s, place, at : at + 20, c0 : c0 + cols].astype(SINGLE) for s in range(2)],
                    axis=1,
                ))
            out[80 * quad : 80 * (quad + 1), :] = jnp.concatenate(parts, axis=0).astype(NARROW)


def unpack_kernel(half_ref, full_ref, first, second, film, wide, thin, query, keyval, mixed, time, time_out):
    half = half_ref[0]
    unpack_tall(half, full_ref, first, 0, 180, 160)
    unpack_tall(half, full_ref, second, 45, 180, 160)
    unpack_tall(half, full_ref, film, 90, 80, 320)
    unpack_tall(half, full_ref, keyval, 130, 64, 320)
    unpack_tall(half, full_ref, query, 242, 20, 160)
    unpack_tall(half, full_ref, mixed, 247, 20, 160)
    unpack_pair(half, full_ref, wide, thin, 162)
    unpack_pair(half, full_ref, time, time_out, 182)


def unpack_late_kernel(half_ref, full_ref, up, down):
    half = half_ref[0]
    unpack_tall(half, full_ref, up, 202, 20, 640)
    unpack_tall(half, full_ref, down, 222, 80, 160)


def unpacked(body, shapes, half_vec, full):
    return smem_call(body, 1, [(s, NARROW) for s in shapes], flops=3 * len(shapes) // 2 * 10**9)(half_vec, full)


def packed_shape(rows):
    return (2, 8, 2, rows, BAND)


def bands_out(out_ref, at, grad_ref, rows, cols):
    parts = BAND // cols
    tall = rows // parts
    for f in range(16):
        for s in range(2):
            lanes = slice(s * cols, (s + 1) * cols)
            pieces = [
                grad_ref[rows * f + tall * q : rows * f + tall * (q + 1), lanes] for q in range(parts)
            ]
            piece = pieces[0] if parts == 1 else jnp.concatenate(pieces, axis=1)
            out_ref[f % 2, 2 * (f % 8 // 2) + s, f // 8, at : at + tall, :] = piece.astype(NARROW)


def pair_out(out_ref, at, wide_ref, thin_ref):
    for f in range(16):
        for s in range(2):
            piece = jnp.concatenate(
                [wide_ref[20 * f : 20 * f + 20, 480 * s : 480 * s + 480],
                 thin_ref[20 * f : 20 * f + 20, 160 * s : 160 * s + 160]],
                axis=1,
            )
            out_ref[f % 2, 2 * (f % 8 // 2) + s, f // 8, at : at + 20, :] = piece.astype(NARROW)


def bands_turned(total, at, out_ref, rows, cols):
    parts = BAND // cols
    tall = rows // parts
    out_ref[...] = jnp.concatenate(
        [total[at : at + tall, cols * q : cols * (q + 1)] for q in range(parts)], axis=0
    ).T


def bands_in(total, at, out_ref, rows, cols):
    parts = BAND // cols
    tall = rows // parts
    for q in range(parts):
        out_ref[tall * q : tall * (q + 1), :] = total[at : at + tall, cols * q : cols * (q + 1)]


def reduce_kernel(half_ref, got_ref, own_ref, other_ref):
    half = half_ref[0]
    own = got_ref[0, half].astype(SINGLE)
    other = got_ref[0, 1 - half].astype(SINGLE)
    for s in range(1, 8):
        own += got_ref[s, half].astype(SINGLE)
        other += got_ref[s, 1 - half].astype(SINGLE)
    own_ref[...] = own
    other_ref[...] = other.astype(NARROW)


def chip_sum(packed, core):
    got = lax.ppermute(pick(1 - core, packed), CORE, [(0, 1), (1, 0)])
    return (pick(core, packed).astype(SINGLE) + got.astype(SINGLE)).astype(NARROW)


def chip_swap(chip):
    return lax.all_to_all(chip, CHIPS, 0, 0, tiled=True)


def reduce_half(got, half_vec):
    shape = got.shape[2:]
    own, other = smem_call(reduce_kernel, 1, [(shape, SINGLE), (shape, NARROW)], flops=10**6)(half_vec, got)
    return own, lax.ppermute(other, HALF, [(0, 1), (1, 0)])


def time_setup(video_mask, video_number, bucket_index, bias_table, half):
    order = jnp.array([8 * ((g % 2) ^ (g // 2 % 2)) + g // 2 for g in range(16)])
    live = pick(half, video_mask)
    number = pick(half, video_number)
    same = (live[:, None] == 1) & (live[None, :] == 1) & (number[:, None] == number[None, :])
    same = same | (jnp.arange(16)[:, None] == jnp.arange(16)[None, :])
    bucket = bucket_index[order][:, order]
    one_hot = (bucket.reshape(-1, 1) == jnp.arange(NB)[None, :]).astype(SINGLE)
    table = jnp.dot(one_hot, bias_table, precision=PRECISE).reshape(16, 16, HEADS).transpose(2, 0, 1)
    small = jnp.where(same[order][:, order][None], table, MASKED)
    pixel = jnp.arange(8)
    wide = jnp.where(
        (pixel[:, None] == pixel[None, :])[None, None, :, None, :], small[:, :, None, :, None], MASKED
    )
    return wide.reshape(HEADS * 128, 128), one_hot


def swap_frames(block, rows):
    return lax.all_to_all(block.reshape(16, rows, block.shape[-1]), CUBE, 0, 0, tiled=True)


def fast_shards(
    video_in, time_embed, text_embed, text_mask, video_mask, video_number, bucket_index,
    norm_gains, bias_table, conv_first, conv_second, film_weight, self_project, self_output,
    cross_query, cross_keyval, cross_output, time_project, time_output, feed_up, feed_down,
    cotangent,
):
    half = lax.axis_index(HALF)
    space = lax.axis_index(SPACE)
    core = lax.axis_index(CORE)
    gains = norm_gains.T
    half_vec = jnp.full((1,), half, jnp.int32)
    packed = pack_weights(Weights(
        conv_first=conv_first, conv_second=conv_second, film_weight=film_weight,
        self_project=self_project, self_output=self_output, cross_query=cross_query,
        cross_keyval=cross_keyval, cross_output=cross_output, time_project=time_project,
        time_output=time_output, feed_up=feed_up, feed_down=feed_down,
    ))
    other = lax.ppermute(packed, HALF, [(0, 1), (1, 0)])
    full = lax.all_gather(jnp.stack([packed, other]), CUBE, axis=0, tiled=False)
    video_in, text_embed, other = lax.optimization_barrier((video_in, text_embed, other))
    x = to_slot(video_in.reshape(FR_DEV, -1, C), half, space)
    text = to_slot(text_embed.reshape(FR_DEV, -1, CTX), half, space)
    x, text, full = lax.optimization_barrier((x, text, full))
    cotangent, full = lax.optimization_barrier((cotangent, full))
    now = unpacked(
        unpack_kernel,
        [(9 * C, C), (9 * C, C), (TEMB, 2 * C), (C, 3 * C), (C, C), (C, C), (CTX, 2 * C), (C, C),
         (C, 3 * C), (C, C)],
        half_vec, full,
    )
    cot = to_slot(cotangent.reshape(FR_DEV, -1, C), half, space)
    w = Weights(*now, None, None)
    temb = meta_slot(time_embed.reshape(FR_DEV, 1, TEMB), space)
    usable = meta_slot(text_mask.reshape(FR_DEV, 1, TEXT), space)[0] == 1
    temb_act = jax.nn.silu(temb.astype(SINGLE)).astype(NARROW)
    bias, one_hot = time_setup(video_mask, video_number, bucket_index, bias_table, half)
    gmat = group_matrix()

    temb_act = jnp.broadcast_to(temb_act, (8, TEMB))
    conv_out, sec1, cols1, cols2, stats, film = conv_block(
        x, w.conv_first, w.conv_second, temb_act, w.film_weight, gains, gmat
    )
    proj, mix, lse, sec2, text_kv, cq, cmix, clse, sec3, time_proj = attn_block(
        sec1, gains, w.self_project, w.self_output, text, usable[:, None], w.cross_keyval,
        w.cross_query, w.cross_output, w.time_project,
    )
    time_proj, cot, full = lax.optimization_barrier((time_proj, cot, full))
    time_qkv = swap_frames(time_proj, PIX // 16)
    w_up, w_down = unpacked(unpack_late_kernel, [(C, FF), (FF, C)], half_vec, full)
    bias_t = bias.reshape(HEADS, 128, 128).transpose(0, 2, 1).reshape(HEADS * 128, 128)
    bias, bias_t = lax.optimization_barrier((bias, bias_t))
    time_low, time_mix_t, time_lse = time_block(time_qkv, bias)
    time_mix = swap_frames(time_low, PIX // 16).reshape(PIX, C)
    result, carried, grad_time_mix, gain_a, *held = feed_block(
        sec3, time_mix, cot, gains, w.time_output, w_up, w_down
    )
    grad_mix_t = swap_frames(grad_time_mix, PIX // 16)
    packed = feed_weight(*held, time_mix, cot)
    chip_down = chip_sum(packed, core)
    chip_down, grad_mix_t = lax.optimization_barrier((chip_down, grad_mix_t))
    down = chip_swap(chip_down)
    grad_qkv_t, bias_grad = time_back_block(time_qkv, bias_t, time_mix_t, time_lse, grad_mix_t)
    grad_qkv_t, down = lax.optimization_barrier((grad_qkv_t, down))
    grad_time_proj = swap_frames(grad_qkv_t, PIX // 16).reshape(PIX, 3 * C)
    grad_time_proj, result, down = lax.optimization_barrier((grad_time_proj, result, down))
    block_out = both_slots(*send_back(result, half), space).reshape(video_in.shape)
    small = bias_grad.transpose(2, 1, 0)
    grad_table = jnp.dot(one_hot.T, small.reshape(-1, HEADS), precision=PRECISE)
    carried, packed, gain_b = cross_back(
        carried, grad_time_proj, sec3, sec2, cq, cmix, clse, text_kv, usable[:, None], text, gains,
        w.time_project, w.cross_output, w.cross_query,
    )
    carried, packed, block_out, down, grad_table = lax.optimization_barrier(
        (carried, packed, block_out, down, grad_table)
    )
    down = reduce_half(down, half_vec)
    chip_middle = chip_sum(packed, core)
    carried, chip_middle = lax.optimization_barrier((carried, chip_middle))
    middle = chip_swap(chip_middle)
    carried, packed, gain_c = self_back_block(
        carried, sec1, proj, mix, lse, gains, w.self_project, w.self_output
    )
    packed, back_second = second_weight(carried, cols2, packed)
    chip_upper = chip_sum(packed, core)
    back_second, middle, chip_upper = lax.optimization_barrier((back_second, middle, chip_upper))
    middle = reduce_half(middle, half_vec)
    upper = chip_swap(chip_upper)
    _, back_first, sums_d = second_back(
        back_second, conv_out, stats, film, gains, gmat, w.conv_second
    )
    packed = first_weight(cols1, back_first)
    got = lax.ppermute(pick(1 - core, packed), CORE, [(0, 1), (1, 0)])
    back_first, packed, upper, sums_d = lax.optimization_barrier((back_first, packed, upper, sums_d))
    small_got = small_swap(temb_act, sums_d, gain_a, gain_b, gain_c, grad_table)
    grad_x, sums_e = first_back(carried, x, stats, gains, gmat, w.conv_first, back_first)
    got, small_got, sums_e = lax.optimization_barrier((got, small_got, sums_e))
    first = chip_swap(first_sum(core, packed, got, sums_e))
    own, other = send_back(grad_x, half)
    upper = reduce_half(upper, half_vec)
    film_own, film_got, small = small_settle(small_got, half_vec)
    first = reduce_half(first, half_vec)
    film_got, first, own, other = lax.optimization_barrier((film_got, first, own, other))
    input_grad = both_slots(own, other, space).reshape(video_in.shape)
    zero = first[0][45:46, :C] + first[1][45:46, :C].astype(SINGLE)
    zero = zero + lax.ppermute(zero, CORE, [(0, 1), (1, 0)])
    gain_sum = jnp.concatenate([zero, small[2:7, :C]]).T
    out = finish(*down, *middle, *upper, *first, film_own, film_got)
    return (
        block_out, input_grad, gain_sum, small[7, : NB * HEADS].reshape(NB, HEADS),
        out.conv_first, out.conv_second, out.film_weight, out.self_project, out.self_output,
        out.cross_query, out.cross_keyval, out.cross_output, out.time_project, out.time_output,
        out.feed_up, out.feed_down,
    )


def fast_solution(mesh):
    split = Mesh(mesh.devices.reshape(2, 4, 2, 2), WORLD)
    frames = (HALF, QUAD, CORE)
    image = P(None, frames, SPACE, None, None)
    weight = P(frames, SPACE)
    placed = (
        image, P(None, frames, None), P(None, frames, SPACE, None), P(None, frames, None),
        P(), P(), P(), P(), P(),
    ) + (weight,) * 12 + (image,)
    return jax.shard_map(
        fast_shards, mesh=split, in_specs=placed,
        out_specs=(image, image, P(), P()) + (weight,) * 12, check_vma=False,
    )


def solution(mesh):
    if mesh.shape[FRAME] == GROUP_LEN and mesh.shape[SPACE] == FR_DEV:
        return fast_solution(mesh)
    placed = (
        P(None, FRAME, SPACE, None, None),
        P(None, FRAME, None),
        P(None, FRAME, SPACE, None),
        P(None, FRAME, None),
        P(),
        P(),
        P(),
        P(),
        P(),
        P(FRAME, SPACE),
        P(FRAME, SPACE),
        P(FRAME, SPACE),
        P(FRAME, SPACE),
        P(FRAME, SPACE),
        P(FRAME, SPACE),
        P(FRAME, SPACE),
        P(FRAME, SPACE),
        P(FRAME, SPACE),
        P(FRAME, SPACE),
        P(FRAME, SPACE),
        P(FRAME, SPACE),
        P(None, FRAME, SPACE, None, None),
    )
    return jax.shard_map(
        shards,
        mesh=mesh,
        in_specs=placed,
        out_specs=(
            P(None, FRAME, SPACE, None, None),
            P(None, FRAME, SPACE, None, None),
            P(),
            P(),
            P(FRAME, SPACE),
            P(FRAME, SPACE),
            P(FRAME, SPACE),
            P(FRAME, SPACE),
            P(FRAME, SPACE),
            P(FRAME, SPACE),
            P(FRAME, SPACE),
            P(FRAME, SPACE),
            P(FRAME, SPACE),
            P(FRAME, SPACE),
            P(FRAME, SPACE),
            P(FRAME, SPACE),
        ),
        check_vma=False,
    )
```
